128 devices in a mesh: prow: 16 (over z, y), pcol: 8 (over x, core).
Axes of the slice: x: 4, y: 4, z: 4, core: 2. Of those that a mesh axis runs over, the one named last changes fastest.
Arguments:
- rhs: float32 [8, 16, 64, 128], P(None, 'prow'), may hold values from -6 to 6
- lower: float32 [8, 16, 16, 8, 128, 128], P(None, 'prow', None, 'pcol'), may hold values from -0.25 to 0.25
- upper: float32 [8, 16, 16, 8, 128, 128], P(None, 'prow', None, 'pcol'), may hold values from -0.25 to 0.25
- lower_inverse: float32 [8, 16, 128, 128], P(None, 'prow'), as said below
- upper_inverse: float32 [8, 16, 128, 128], P(None, 'prow'), as said below
- pattern: int32 [128, 128], replicated, may hold values from 0 to 1, as said below
- levels: int32 [128], replicated, may hold values from 0 to 5, as said below
- widths: int32 [128], replicated, may hold values from 64 to 128
Outputs:
- forward: float32 [8, 16, 64, 128], P(None, 'prow')
- solution: float32 [8, 16, 64, 128], P(None, 'prow')
The draws below stay inside these ranges and needn't reach their ends.
Inputs may be any that keep to these rules, and one draw needn't show every extreme that they name: `lower_inverse`: each inverse has diagonal entries between 0.5 and 2 plus a dense random part of standard deviation 0.4 / sqrt(128). `upper_inverse`: each inverse has diagonal entries between 0.5 and 2 plus a dense random part of standard deviation 0.4 / sqrt(128). The supernodes form one binary elimination tree; pattern[i, j] is 1 exactly where i is a proper ancestor of j or j of i, and 0 elsewhere and on the diagonal. `levels`: A supernode's level is its height in the tree (leaves 0), capped at 5, which the root reaches; a parent's level is above its child's unless both are capped. Levels 1 to 4 each hold half as many supernodes as the one below.
All inputs are finite; a program needn't handle non-finite values.
Results may differ from the reference program's by a relative error of at most 0.00017.
Values sent between devices are 32-bit elements; how exact they have to be, the bound alone decides.
No kernel may reach another device: no remote copies, remote signals or barrier semaphores. Data moves between devices by JAX's collectives and lax.ppermute only.
A program may use at most 128 MiB of HBM per device.

```python
import jax
import jax.numpy as jnp
from jax import lax

W = 128
NRHS = 64
LEVELS = 6
RB = 8
NB = 128
CB = 16
N_PROW = 16
N_PCOL = 8


def dominant_inverse(key):
    first, second = jax.random.split(key)
    diagonal = jnp.exp(jax.random.uniform(first, (RB, N_PROW, W), jnp.float32, -0.7, 0.7))
    spread = jax.random.normal(second, (RB, N_PROW, W, W), jnp.float32) * (0.4 / W ** 0.5)
    return spread + diagonal[..., None] * jnp.eye(W, dtype=jnp.float32)


def tree_shape(key):
    count = RB * N_PROW
    placed = jax.random.permutation(key, count).astype(jnp.int32)
    heap = jnp.arange(count, dtype=jnp.int32) + 1
    height = jnp.zeros((count,), jnp.int32)
    related = jnp.zeros((count, count), jnp.int32)
    for step in range(1, 13):
        height = height + (heap * 2 ** step <= count).astype(jnp.int32)
        shifted = jnp.right_shift(heap, step)
        related = related + (shifted[None, :] == heap[:, None]).astype(jnp.int32)
    height = jnp.minimum(height, LEVELS - 1)
    related = jnp.minimum(related + related.T, 1)
    inverse_order = jnp.argsort(placed, stable=True).astype(jnp.int32)
    levels = height[inverse_order]
    pattern = related[inverse_order][:, inverse_order]
    return (pattern.astype(jnp.int32), levels.astype(jnp.int32))


def draw_pattern(key, part):
    pattern, levels = tree_shape(key)
    return pattern


def draw_levels(key, part):
    pattern, levels = tree_shape(key)
    return levels


def draw_lower_inverse(key, part):
    key = jax.random.fold_in(key, 11)
    return dominant_inverse(key)


def draw_upper_inverse(key, part):
    key = jax.random.fold_in(key, 23)
    return dominant_inverse(key)


def with_ends(array, own_key, least, largest):
    longest = array.shape.index(max(array.shape))
    spots = []
    for shift in (0, 1):
        where = [jax.random.randint(jax.random.fold_in(own_key, axis), (), 0, length) for axis, length in enumerate(array.shape)]
        where[longest] = (where[longest] + shift) % array.shape[longest]
        spots.append(tuple(where))
    return array.at[spots[0]].set(least).at[spots[1]].set(largest)


def steps_of(rng, dims, cuts, least, largest):
    gain, own = 1.0, jax.random.fold_in(rng, 6)
    for dim, parts in cuts:
        steps = jnp.exp(jax.random.uniform(jax.random.fold_in(own, dim), (parts,), jnp.float32, least / len(cuts), largest / len(cuts)))
        gain = gain * jnp.repeat(steps, dims[dim] // parts).reshape([-1 if axis == dim else 1 for axis in range(len(dims))])
    return gain


def normal_values(key, dims, width, limit, cuts=(), kind=jnp.bfloat16):
    values = jax.random.normal(key, dims, jnp.float32) * width
    if len(cuts) > 0:
        values = steps_of(key, dims, cuts, -0.22, 0.18) * values
    return jnp.clip(values, min=-limit, max=limit).astype(kind)


def setup_inputs(seed: int = 0) -> dict:
    splits = jax.random.split(jax.random.key(seed), 9)
    return {
        "rhs": normal_values(splits[0], (RB, N_PROW, NRHS, W), 1.0, 6.0, ((1, 16),), jnp.float32),
        "lower": normal_values(splits[1], (RB, N_PROW, CB, N_PCOL, W, W), (W * 4) ** -0.5, 0.25, ((1, 16), (3, 8)), jnp.float32),
        "upper": normal_values(splits[2], (RB, N_PROW, CB, N_PCOL, W, W), (W * 4) ** -0.5, 0.25, ((1, 16), (3, 8)), jnp.float32),
        "lower_inverse": draw_lower_inverse(jax.random.fold_in(splits[8], 71), 0),
        "upper_inverse": draw_upper_inverse(jax.random.fold_in(splits[8], 71), 0),
        "pattern": draw_pattern(jax.random.fold_in(splits[8], 71), 0),
        "levels": draw_levels(jax.random.fold_in(splits[8], 71), 0),
        "widths": with_ends(jax.random.randint(splits[7], (NB,), W // 2, W + 1), jax.random.fold_in(splits[7], 1), W // 2, W).astype(jnp.int32),
    }


def sweep(blocks, mask, inverse, right, valid, order):
    def advance(state, index):
        row = blocks[index] * mask[index][:, None, None]
        sums = jnp.einsum("jkl,jhl->hk", row, state, precision=lax.Precision.HIGHEST)
        value = jnp.einsum("kl,hl->hk", inverse[index], right[index] - sums, precision=lax.Precision.HIGHEST)
        return state.at[index].set(value * valid[index]), None

    start = jnp.zeros(right.shape, jnp.float32)
    final, _ = lax.scan(advance, start, order)
    return final


def reference(rhs, lower, upper, lower_inverse, upper_inverse, pattern, levels, widths):
    count = RB * N_PROW
    lower_blocks = lower.reshape(count, count, W, W)
    upper_blocks = upper.reshape(count, count, W, W)
    right = rhs.reshape(count, NRHS, W)
    valid = (jnp.arange(W)[None, :] < widths[:, None]).astype(jnp.float32)[:, None, :]
    below = (levels[None, :] < levels[:, None]).astype(jnp.float32) * pattern.astype(jnp.float32)
    above = (levels[None, :] > levels[:, None]).astype(jnp.float32) * pattern.astype(jnp.float32)
    rising = jnp.argsort(levels, stable=True).astype(jnp.int32)
    falling = jnp.argsort(-levels, stable=True).astype(jnp.int32)
    forward = sweep(lower_blocks, below, lower_inverse.reshape(count, W, W), right, valid, rising)
    solution = sweep(upper_blocks, above, upper_inverse.reshape(count, W, W), forward, valid, falling)
    shape = (RB, N_PROW, NRHS, W)
    return forward.reshape(shape), solution.reshape(shape)
```

```python
import jax
import jax.numpy as jnp
from jax import lax
from jax.experimental import pallas as pl
from jax.experimental.pallas import tpu as pltpu
from jax.sharding import PartitionSpec as P

LEVELS = 6
W = 128
NRHS = 64
NB = 128
RB = 8
CB = 16
PR = 16
PC = 8
HS = NRHS // PC
CAP_L = 12
CAP_U = 28
LIST = 64
ANY = pl.BlockSpec(memory_space=pl.ANY)
SMEM = pl.BlockSpec(memory_space=pltpu.SMEM)
VMEM = pl.BlockSpec(memory_space=pltpu.VMEM)


def spread(value, axis, source):
    kept = jnp.where(lax.axis_index(axis) == source, value, 0).astype(value.dtype)
    return lax.psum(kept, axis)


def apply_inverse(inverse, right):
    return jnp.einsum("akl,ahl->ahk", inverse, right, precision=lax.Precision.HIGHEST)


def solve_levels(blocks, inverse, right, valid, row_levels, mask, rising):
    prow_count = lax.axis_size("prow")
    pcol_count = lax.axis_size("pcol")
    column = lax.axis_index("pcol")
    ratio = prow_count // pcol_count
    masked = blocks * mask[:, :, None, None]
    row_state = jnp.zeros(right.shape, jnp.float32)
    col_state = jnp.zeros((masked.shape[1],) + right.shape[1:], jnp.float32)
    order = list(range(LEVELS)) if rising else list(range(LEVELS - 1, -1, -1))
    for place, level in enumerate(order):
        partial_sum = jnp.einsum(
            "ackl,chl->ahk", masked, col_state, precision=lax.Precision.HIGHEST
        )
        total = lax.psum(partial_sum, "pcol")
        fresh = apply_inverse(inverse, right - total) * valid
        current = (row_levels == level)[:, None, None]
        row_state = jnp.where(current, fresh, row_state)
        if place + 1 < LEVELS:
            pieces = []
            for offset in range(ratio):
                pieces.append(spread(row_state, "prow", column + offset * pcol_count))
            stacked = jnp.stack(pieces, axis=1)
            col_state = stacked.reshape((-1,) + right.shape[1:])
    return row_state


def general(rhs, lower, upper, lower_inverse, upper_inverse, pattern, levels, widths):
    prow_count = lax.axis_size("prow")
    pcol_count = lax.axis_size("pcol")
    row_index = lax.axis_index("prow")
    col_index = lax.axis_index("pcol")
    row_blocks = rhs.shape[0]
    col_blocks = lower.shape[2]
    width = rhs.shape[3]
    right = rhs.reshape(row_blocks, rhs.shape[2], width)
    lower_local = lower.reshape(row_blocks, col_blocks, width, width)
    upper_local = upper.reshape(row_blocks, col_blocks, width, width)
    lower_inv = lower_inverse.reshape(row_blocks, width, width)
    upper_inv = upper_inverse.reshape(row_blocks, width, width)
    row_levels = lax.dynamic_index_in_dim(
        levels.reshape(row_blocks, prow_count), row_index, 1, keepdims=False
    )
    col_levels = lax.dynamic_index_in_dim(
        levels.reshape(col_blocks, pcol_count), col_index, 1, keepdims=False
    )
    row_widths = lax.dynamic_index_in_dim(
        widths.reshape(row_blocks, prow_count), row_index, 1, keepdims=False
    )
    grid = pattern.reshape(row_blocks, prow_count, col_blocks, pcol_count)
    grid = lax.dynamic_index_in_dim(grid, row_index, 1, keepdims=False)
    grid = lax.dynamic_index_in_dim(grid, col_index, 2, keepdims=False).astype(jnp.float32)
    valid = (jnp.arange(width)[None, :] < row_widths[:, None]).astype(jnp.float32)[:, None, :]
    below = grid * (col_levels[None, :] < row_levels[:, None]).astype(jnp.float32)
    above = grid * (col_levels[None, :] > row_levels[:, None]).astype(jnp.float32)
    forward = solve_levels(lower_local, lower_inv, right, valid, row_levels, below, True)
    solution = solve_levels(upper_local, upper_inv, forward, valid, row_levels, above, False)
    shape = rhs.shape
    return (forward.reshape(shape), solution.reshape(shape))


def dot3(x, w):
    m = x.shape[0]
    xh = x.astype(jnp.bfloat16).astype(jnp.float32)
    xs = jnp.concatenate([xh, x - xh], axis=0).astype(jnp.bfloat16)
    wh = w.astype(jnp.bfloat16)
    wl = (w - wh.astype(jnp.float32)).astype(jnp.bfloat16)
    dims = (((1,), (1,)), ((), ()))
    a = lax.dot_general(xs, wl, dims, preferred_element_type=jnp.float32)
    b = lax.dot_general(xs, wh, dims, preferred_element_type=jnp.float32)
    return (a[m:] + a[:m]) + (b[m:] + b[:m])


def pack_kernel(meta, lower, upper, out_l, out_u, sems):
    nl = meta[0]
    nu = meta[1]

    def copy_l(t):
        n = meta[2 + t]
        return pltpu.make_async_copy(lower.at[n >> 4, n & (CB - 1)], out_l.at[t], sems.at[t])

    def copy_u(t):
        n = meta[2 + CAP_L + t]
        return pltpu.make_async_copy(upper.at[n >> 4, n & (CB - 1)], out_u.at[t], sems.at[CAP_L + t])

    pl.loop(0, nl)(lambda t: copy_l(t).start())
    pl.loop(0, nu)(lambda t: copy_u(t).start())
    pl.loop(0, nl)(lambda t: copy_l(t).wait())
    pl.loop(0, nu)(lambda t: copy_u(t).wait())


def pack(meta, lower, upper):
    return pl.pallas_call(
        pack_kernel,
        out_shape=(
            jax.ShapeDtypeStruct((CAP_L, W, W), jnp.float32),
            jax.ShapeDtypeStruct((CAP_U, W, W), jnp.float32),
        ),
        in_specs=[SMEM, ANY, ANY],
        out_specs=(ANY, ANY),
        scratch_shapes=[pltpu.SemaphoreType.DMA((CAP_L + CAP_U,))],
        cost_estimate=pl.CostEstimate(flops=0, bytes_accessed=2 * (CAP_L + CAP_U) * W * W * 4, transcendentals=0),
    )(meta, lower, upper)


def level_kernel(level, rows, meta, known, right, state, inverse, panel, out, blocks, inv, sems, isems):
    def copy(t):
        slot = meta[t] >> 7
        return pltpu.make_async_copy(panel.at[slot], blocks.at[t], sems.at[t])

    def icopy(a):
        return pltpu.make_async_copy(inverse.at[a], inv.at[a], isems.at[a])

    for a in range(RB):
        @pl.when(rows[a] == level)
        def _():
            icopy(a).start()
            pl.loop(rows[2 * RB + a], rows[2 * RB + a + 1])(lambda t: copy(t).start())

    for a in range(RB):
        out[a] = state[a]

        @pl.when(rows[a] == level)
        def _():
            def step(t, acc):
                copy(t).wait()
                node = meta[t] & (NB - 1)
                return acc - dot3(known[node & (PR - 1), node >> 4], blocks[t])

            acc = lax.fori_loop(rows[2 * RB + a], rows[2 * RB + a + 1], step, right[a])
            icopy(a).wait()
            fresh = dot3(acc, inv[a])
            lane = lax.broadcasted_iota(jnp.int32, (HS, W), 1)
            out[a] = jnp.where(lane < rows[RB + a], fresh, 0.0)


def level_step(level, rows, meta, known, right, state, inverse, panel):
    return pl.pallas_call(
        lambda *refs: level_kernel(level, *refs),
        out_shape=jax.ShapeDtypeStruct((RB, HS, W), jnp.float32),
        in_specs=[SMEM, SMEM, VMEM, VMEM, VMEM, ANY, ANY],
        out_specs=VMEM,
        scratch_shapes=[
            pltpu.VMEM((LIST, W, W), jnp.float32),
            pltpu.VMEM((RB, W, W), jnp.float32),
            pltpu.SemaphoreType.DMA((LIST,)),
            pltpu.SemaphoreType.DMA((RB,)),
        ],
        compiler_params=pltpu.CompilerParams(vmem_limit_bytes=24 * 1024 * 1024),
    )(rows, meta, known, right, state, inverse, panel)


def across_kernel(meta, known, lower, out, blocks, sems):
    count = meta[0]

    def copy(t):
        n = meta[1 + t]
        return pltpu.make_async_copy(lower.at[n >> 4, n & (CB - 1)], blocks.at[t], sems.at[t])

    pl.loop(0, count)(lambda t: copy(t).start())
    out[...] = jnp.zeros_like(out)

    def step(t, carry):
        copy(t).wait()
        n = meta[1 + t]
        a = n >> 4
        c = n & (CB - 1)
        x = known[:, c & 1, c >> 1].reshape(NRHS, W)
        out[:, a] += dot3(x, blocks[t]).reshape(PC, HS, W)
        return carry

    lax.fori_loop(0, count, step, 0)


def across(meta, known, lower):
    return pl.pallas_call(
        across_kernel,
        out_shape=jax.ShapeDtypeStruct((PC, RB, HS, W), jnp.float32),
        in_specs=[SMEM, VMEM, ANY],
        out_specs=VMEM,
        scratch_shapes=[pltpu.VMEM((NB, W, W), jnp.float32), pltpu.SemaphoreType.DMA((NB,))],
        compiler_params=pltpu.CompilerParams(vmem_limit_bytes=24 * 1024 * 1024),
    )(meta, known, lower)


def gather_rows(state):
    copies = jnp.broadcast_to(state[None], (PR,) + state.shape)
    return lax.all_to_all(copies, "prow", 0, 0)


def before(flags, count):
    n = flags.shape[0]
    tri = (jnp.arange(n)[:, None] > jnp.arange(n)[None, :]).astype(jnp.bfloat16)
    out = jnp.dot(tri, flags.astype(jnp.bfloat16), preferred_element_type=jnp.float32)
    return out.astype(jnp.int32)


def listed(flags, place, value, size):
    hit = flags[:, None] & (place[:, None] == jnp.arange(size)[None, :])
    return jnp.sum(jnp.where(hit, value[:, None], 0), axis=0)


def own_list(sel, size):
    flat = sel.reshape(NB)
    place = before(flat[:, None], NB)[:, 0]
    return listed(flat, place, jnp.arange(NB, dtype=jnp.int32), size), jnp.sum(flat.astype(jnp.int32))


def row_list(sel, cap):
    by_col = sel.reshape(RB * CB, PC)
    rank = before(by_col, NB).reshape(RB, NB)
    node = jnp.arange(NB, dtype=jnp.int32)
    slot = (node % PC)[None, :] * cap + rank
    within = before(sel.T, NB).T
    sums = jnp.sum(sel.astype(jnp.int32), axis=1)
    ends = jnp.sum(jnp.where(jnp.arange(RB)[None, :] <= jnp.arange(RB)[:, None], sums[None, :], 0), axis=1)
    place = within + (ends - sums)[:, None]
    value = slot * NB + node[None, :]
    meta = listed(sel.reshape(-1), place.reshape(-1), value.reshape(-1), LIST)
    return meta, jnp.concatenate([jnp.zeros((1,), jnp.int32), ends])


def selections(pattern, levels):
    linked = pattern > 0
    low = linked & (levels[None, :] < levels[:, None])
    high = linked & (levels[None, :] > levels[:, None])
    near = (levels[:, None] <= 2) | (levels[None, :] >= 3)
    return low & near, low & ~near, high


def fast(rhs, lower, upper, lower_inverse, upper_inverse, near, far, high, levels, widths):
    p = lax.axis_index("prow")
    q = lax.axis_index("pcol")
    right = rhs.reshape(RB, NRHS, W)
    lower = lower.reshape(RB, CB, W, W)
    upper = upper.reshape(RB, CB, W, W)
    lower_inv = lower_inverse.reshape(RB, W, W)
    upper_inv = upper_inverse.reshape(RB, W, W)
    row_levels = lax.dynamic_index_in_dim(levels.reshape(RB, PR), p, 1, keepdims=False)
    row_widths = lax.dynamic_index_in_dim(widths.reshape(RB, PR), p, 1, keepdims=False)
    rows_of = lambda sel: lax.dynamic_index_in_dim(sel.reshape(RB, PR, NB), p, 1, keepdims=False)
    cols_of = lambda sel: lax.dynamic_index_in_dim(sel.reshape(RB, CB, PC), q, 2, keepdims=False)
    near_p, far_p, high_p = rows_of(near), rows_of(far), rows_of(high)
    list_l, count_l = own_list(cols_of(near_p), CAP_L)
    list_u, count_u = own_list(cols_of(high_p), CAP_U)
    list_t, count_t = own_list(cols_of(far_p), NB)
    pack_meta = jnp.concatenate([count_l[None], count_u[None], list_l, list_u])
    meta_t = jnp.concatenate([count_t[None], list_t])
    packed_l, packed_u = pack(pack_meta, lower, upper)
    panel_l = lax.all_gather(packed_l, "pcol", tiled=True)
    panel_u = lax.all_gather(packed_u, "pcol", tiled=True)
    meta_l, ptr_l = row_list(near_p, CAP_L)
    meta_u, ptr_u = row_list(high_p, CAP_U)
    rows_l = jnp.concatenate([row_levels, row_widths, ptr_l])
    rows_u = jnp.concatenate([row_levels, row_widths, ptr_u])

    b = lax.dynamic_slice_in_dim(right, q * HS, HS, 1)
    state = jnp.zeros((RB, HS, W), jnp.float32)
    known = jnp.zeros((PR, RB, HS, W), jnp.float32)
    for level in range(LEVELS):
        if level == 3:
            split = known.reshape(2, PC, RB, HS, W).transpose(1, 0, 2, 3, 4)
            columns = lax.all_to_all(split, "pcol", 0, 0)
            sums = lax.all_to_all(across(meta_t, columns, lower), "pcol", 0, 0)
            b = b - jnp.sum(sums, axis=0)
        state = level_step(level, rows_l, meta_l, known, b, state, lower_inv, panel_l)
        if level + 1 < LEVELS:
            known = gather_rows(state)
    forward = state
    full_f = lax.all_gather(forward, "pcol")
    state = jnp.zeros((RB, HS, W), jnp.float32)
    for level in range(LEVELS - 1, -1, -1):
        state = level_step(level, rows_u, meta_u, known, forward, state, upper_inv, panel_u)
        if level > 0:
            known = gather_rows(state)
    copies = jnp.broadcast_to(state[None], (PC,) + state.shape)
    full_s = lax.all_to_all(copies, "pcol", 0, 0)
    shape = rhs.shape
    whole = lambda x: x.transpose(1, 0, 2, 3).reshape(shape)
    return whole(full_f), whole(full_s)


def local(rhs, lower, upper, lower_inverse, upper_inverse, pattern, levels, widths):
    near, far, high = selections(pattern, levels)
    held = lambda sel: jnp.sum(sel.reshape(RB, PR, CB, PC).astype(jnp.int32), axis=(0, 2))
    held_l, held_u = held(near), held(high)
    fits = (
        (jnp.max(held_l) <= CAP_L)
        & (jnp.max(held_u) <= CAP_U)
        & (jnp.max(jnp.sum(held_l, axis=1)) <= LIST)
        & (jnp.max(jnp.sum(held_u, axis=1)) <= LIST)
    )
    return lax.cond(
        fits,
        lambda: fast(rhs, lower, upper, lower_inverse, upper_inverse, near, far, high, levels, widths),
        lambda: general(rhs, lower, upper, lower_inverse, upper_inverse, pattern, levels, widths),
    )


def solution(mesh):
    in_specs = (
        P(None, "prow", None, None),
        P(None, "prow", None, "pcol", None, None),
        P(None, "prow", None, "pcol", None, None),
        P(None, "prow", None, None),
        P(None, "prow", None, None),
        P(),
        P(),
        P(),
    )
    out_specs = (P(None, "prow", None, None), P(None, "prow", None, None))
    return jax.shard_map(local, mesh=mesh, in_specs=in_specs, out_specs=out_specs, check_vma=False)
```

```python
import jax
import jax.numpy as jnp
from jax import lax
from jax.experimental import pallas as pl
from jax.experimental.pallas import tpu as pltpu
from jax.sharding import PartitionSpec as P

LEVELS = 6
W = 128
NRHS = 64
NB = 128
RB = 8
CB = 16
PR = 16
PC = 8
HS = NRHS // PC
CAP_L = 12
CAP_U = 28
LIST = 64
HBM = pl.BlockSpec(memory_space=pltpu.HBM)
SMEM = pl.BlockSpec(memory_space=pltpu.SMEM)
VMEM = pl.BlockSpec(memory_space=pltpu.VMEM)
LEVEL, WIDTH, START_L, END_L, START_U, END_U = range(6)
LIST_L, LIST_U, LIST_T, PACK_L, PACK_U, COUNTS = range(8, 14)
SAME_CORE = [[2 * x + c for x in range(PC // 2)] for c in range(2)]


def spread(value, axis, source):
    kept = jnp.where(lax.axis_index(axis) == source, value, 0).astype(value.dtype)
    return lax.psum(kept, axis)


def apply_inverse(inverse, right):
    return jnp.einsum("akl,ahl->ahk", inverse, right, precision=lax.Precision.HIGHEST)


def solve_levels(blocks, inverse, right, valid, row_levels, mask, rising):
    prow_count = lax.axis_size("prow")
    pcol_count = lax.axis_size("pcol")
    column = lax.axis_index("pcol")
    ratio = prow_count // pcol_count
    masked = blocks * mask[:, :, None, None]
    row_state = jnp.zeros(right.shape, jnp.float32)
    col_state = jnp.zeros((masked.shape[1],) + right.shape[1:], jnp.float32)
    order = list(range(LEVELS)) if rising else list(range(LEVELS - 1, -1, -1))
    for place, level in enumerate(order):
        partial_sum = jnp.einsum(
            "ackl,chl->ahk", masked, col_state, precision=lax.Precision.HIGHEST
        )
        total = lax.psum(partial_sum, "pcol")
        fresh = apply_inverse(inverse, right - total) * valid
        current = (row_levels == level)[:, None, None]
        row_state = jnp.where(current, fresh, row_state)
        if place + 1 < LEVELS:
            pieces = []
            for offset in range(ratio):
                pieces.append(spread(row_state, "prow", column + offset * pcol_count))
            stacked = jnp.stack(pieces, axis=1)
            col_state = stacked.reshape((-1,) + right.shape[1:])
    return row_state


def general(rhs, lower, upper, lower_inverse, upper_inverse, pattern, levels, widths):
    prow_count = lax.axis_size("prow")
    pcol_count = lax.axis_size("pcol")
    row_index = lax.axis_index("prow")
    col_index = lax.axis_index("pcol")
    row_blocks = rhs.shape[0]
    col_blocks = lower.shape[2]
    width = rhs.shape[3]
    right = rhs.reshape(row_blocks, rhs.shape[2], width)
    lower_local = lower.reshape(row_blocks, col_blocks, width, width)
    upper_local = upper.reshape(row_blocks, col_blocks, width, width)
    lower_inv = lower_inverse.reshape(row_blocks, width, width)
    upper_inv = upper_inverse.reshape(row_blocks, width, width)
    row_levels = lax.dynamic_index_in_dim(
        levels.reshape(row_blocks, prow_count), row_index, 1, keepdims=False
    )
    col_levels = lax.dynamic_index_in_dim(
        levels.reshape(col_blocks, pcol_count), col_index, 1, keepdims=False
    )
    row_widths = lax.dynamic_index_in_dim(
        widths.reshape(row_blocks, prow_count), row_index, 1, keepdims=False
    )
    grid = pattern.reshape(row_blocks, prow_count, col_blocks, pcol_count)
    grid = lax.dynamic_index_in_dim(grid, row_index, 1, keepdims=False)
    grid = lax.dynamic_index_in_dim(grid, col_index, 2, keepdims=False).astype(jnp.float32)
    valid = (jnp.arange(width)[None, :] < row_widths[:, None]).astype(jnp.float32)[:, None, :]
    below = grid * (col_levels[None, :] < row_levels[:, None]).astype(jnp.float32)
    above = grid * (col_levels[None, :] > row_levels[:, None]).astype(jnp.float32)
    forward = solve_levels(lower_local, lower_inv, right, valid, row_levels, below, True)
    solution = solve_levels(upper_local, upper_inv, forward, valid, row_levels, above, False)
    shape = rhs.shape
    return (forward.reshape(shape), solution.reshape(shape))


def dot3(x, w):
    m = x.shape[0]
    xh = x.astype(jnp.bfloat16).astype(jnp.float32)
    xs = jnp.concatenate([xh, x - xh], axis=0).astype(jnp.bfloat16)
    wh = w.astype(jnp.bfloat16)
    wl = (w - wh.astype(jnp.float32)).astype(jnp.bfloat16)
    dims = (((1,), (1,)), ((), ()))
    a = lax.dot_general(xs, wl, dims, preferred_element_type=jnp.float32)
    b = lax.dot_general(xs, wh, dims, preferred_element_type=jnp.float32)
    return (a[m:] + a[:m]) + (b[m:] + b[:m])


def iota(shape, dim):
    return lax.broadcasted_iota(jnp.int32, shape, dim)


def flag(cond):
    return jnp.where(cond, 1.0, 0.0)


def table_kernel(pattern, levels, widths, out):
    p = lax.axis_index("prow")
    q = lax.axis_index("pcol")
    lev = levels[...].astype(jnp.float32)
    wid = widths[...].astype(jnp.float32)
    i = iota((NB, NB), 0)
    j = iota((NB, NB), 1)
    lev_col = jnp.sum(jnp.where(i == j, lev, 0.0), axis=1, keepdims=True)
    linked = flag(pattern[...] > 0)
    low = linked * flag(lev < lev_col)
    high = linked * flag(lev > lev_col)
    near = low * flag((lev_col < 2.5) | (lev > 2.5))
    far = low - near
    same = flag((i & (PC - 1)) == (j & (PC - 1)))
    ahead = flag(i < j)
    same_ahead = same * ahead

    def dot(x, y):
        return jnp.dot(x, y, preferred_element_type=jnp.float32)

    by_row = flag((iota((PR, NB), 1) & (PR - 1)) == iota((PR, NB), 0))

    def over(full, cap):
        rows = dot(by_row, full)
        most = jnp.max(jnp.max(dot(rows, same), axis=1, keepdims=True), axis=0, keepdims=True)
        listed = jnp.max(jnp.sum(rows, axis=1, keepdims=True), axis=0, keepdims=True)
        return flag((most > cap) | (listed > LIST))

    full = jnp.maximum(over(near, CAP_L), over(high, CAP_U))

    lane = iota((RB, NB), 1)
    sub = iota((RB, NB), 0)
    mine = flag(lane == sub * PR + p)
    row_lev = jnp.sum(mine * lev, axis=1, keepdims=True)
    row_wid = jnp.sum(mine * wid, axis=1, keepdims=True)
    col = lane & (PC - 1)
    own = flag(col == q)
    node = lane.astype(jnp.float32)
    spot = (sub * CB + (lane >> 3)).astype(jnp.float32)

    def ranks(sel):
        total = jnp.zeros((1, NB), jnp.float32)
        rows = []
        for a in range(RB):
            rows.append(total)
            total = total + sel[a : a + 1]
        prior = jnp.concatenate(rows, axis=0)
        start = jnp.sum(prior, axis=1, keepdims=True)
        end = start + jnp.sum(sel, axis=1, keepdims=True)
        return start, end, start + dot(sel, ahead), dot(prior, same) + dot(sel, same_ahead)

    def listing(sel, place, value, size):
        t = iota((size, NB), 0).astype(jnp.float32)
        held = jnp.zeros((size, NB), jnp.float32)
        for a in range(RB):
            hit = flag(t == place[a : a + 1]) * sel[a : a + 1]
            held = held + hit * value[a : a + 1]
        ones = jnp.ones((RB, NB), jnp.float32)
        row = lax.dot_general(ones, held, (((1,), (1,)), ((), ())), preferred_element_type=jnp.float32)[:1]
        if size < NB:
            row = jnp.concatenate([row, jnp.zeros((1, NB - size), jnp.float32)], axis=1)
        return row

    def count(sel):
        return jnp.sum(jnp.sum(sel, axis=1, keepdims=True), axis=0, keepdims=True)

    def panel(sel, cap):
        start, end, place, rank = ranks(sel)
        slot = ((col & 1) * (4 * cap) + (col >> 1) * cap).astype(jnp.float32) + jnp.minimum(rank, cap - 1.0)
        listed = listing(sel, place, slot, LIST) * NB + listing(sel, place, node, LIST)
        packed = listing(sel * own, rank, spot, 32)
        return jnp.minimum(start, LIST), jnp.minimum(end, LIST), listed, packed, jnp.minimum(count(sel * own), cap)

    near_p = dot(mine, near)
    high_p = dot(mine, high)
    far_p = dot(mine, far)
    start_l, end_l, list_l, pack_l, count_l = panel(near_p, CAP_L)
    start_u, end_u, list_u, pack_u, count_u = panel(high_p, CAP_U)
    _, _, _, rank_t = ranks(far_p)
    list_t = listing(far_p * own, rank_t, spot, NB)
    count_t = count(far_p * own)
    rows = jnp.zeros((RB, NB), jnp.float32)
    for k, value in enumerate([row_lev, row_wid, start_l, end_l, start_u, end_u]):
        rows = rows + flag(lane == k) * value
    counts = jnp.zeros((1, NB), jnp.float32)
    for k, value in enumerate([count_l, count_u, count_t, full]):
        counts = counts + flag(lane[:1] == k) * value
    none = jnp.zeros((1, NB), jnp.float32)
    lists = jnp.concatenate([list_l, list_u, list_t, pack_l, pack_u, counts, none, none], axis=0)
    out[0:8, :] = rows.astype(jnp.int32)
    out[8:16, :] = lists.astype(jnp.int32)


def tables(pattern, levels, widths):
    return pl.pallas_call(
        table_kernel,
        out_shape=jax.ShapeDtypeStruct((16, NB), jnp.int32),
        in_specs=[VMEM, VMEM, VMEM],
        out_specs=VMEM,
    )(pattern, levels.reshape(1, NB), widths.reshape(1, NB))


def pack_kernel(where, cap, table, blocks, out, held, sems_in, sems_out):
    count = table[COUNTS, where]
    row = PACK_L + where

    def load(t):
        n = table[row, t]
        return pltpu.make_async_copy(blocks.at[n >> 4, n & (CB - 1)], held.at[t], sems_in.at[t])

    def store(t):
        return pltpu.make_async_copy(held.at[t], out.at[t], sems_out.at[t])

    pl.loop(0, count)(lambda t: load(t).start())

    @pl.loop(0, count)
    def _(t):
        load(t).wait()
        store(t).start()

    pl.loop(0, count)(lambda t: store(t).wait())


def pack(where, cap, table, blocks):
    return pl.pallas_call(
        lambda *refs: pack_kernel(where, cap, *refs),
        out_shape=jax.ShapeDtypeStruct((cap, W, W), jnp.float32),
        in_specs=[SMEM, HBM],
        out_specs=HBM,
        scratch_shapes=[
            pltpu.VMEM((cap, W, W), jnp.float32),
            pltpu.SemaphoreType.DMA((cap,)),
            pltpu.SemaphoreType.DMA((cap,)),
        ],
    )(table, blocks)


def level_kernel(level, copies, kind, cap, turn, table, known, right, inverse, panel_0, panel_1, *rest):
    if turn:
        inverse_2, out, out_2, blocks, inv, inv_2, sems, isems = rest
    else:
        out, blocks, inv, sems, isems = rest
    p = lax.axis_index("prow")
    row = LIST_U if kind else LIST_L
    first, last = (START_U, END_U) if kind else (START_L, END_L)

    def copy(t, panel=panel_0):
        slot = table[row, t] >> 7
        slot = jnp.where(slot >= 4 * cap, slot - 4 * cap, slot)
        return pltpu.make_async_copy(panel.at[slot], blocks.at[t], sems.at[t])

    core = lax.axis_index("pcol") & 1

    def begin(t):
        other = jnp.where((table[row, t] >> 7) >= 4 * cap, 1 - core, core)

        @pl.when(other == 1)
        def _():
            copy(t, panel_1).start()

        @pl.when(other == 0)
        def _():
            copy(t, panel_0).start()

    def icopy(a):
        return pltpu.make_async_copy(inverse.at[a], inv.at[a], isems.at[a])

    def icopy_2(a):
        return pltpu.make_async_copy(inverse_2.at[a], inv_2.at[a], isems.at[RB + a])

    for a in range(RB):
        @pl.when(table[a, LEVEL] == level)
        def _():
            if panel_0 is not None:
                pl.loop(table[a, first], table[a, last])(begin)
            icopy(a).start()
            if turn:
                icopy_2(a).start()

    lane = iota((HS, W), 1)
    for a in range(RB):
        old = known[p, a] if known is not None else jnp.zeros((HS, W), jnp.float32)
        for r in range(copies):
            out[r, a] = old if not turn else jnp.zeros((HS, W), jnp.float32)
        if turn:
            out_2[a] = old

        @pl.when(table[a, LEVEL] == level)
        def _():
            acc = right[a]
            if panel_0 is not None:
                def step(t, acc):
                    copy(t).wait()
                    node = table[row, t] & (NB - 1)
                    return acc - dot3(known[node & (PR - 1), node >> 4], blocks[t])

                acc = lax.fori_loop(table[a, first], table[a, last], step, acc)
            icopy(a).wait()
            keep = lane < table[a, WIDTH]
            fresh = jnp.where(keep, dot3(acc, inv[a]), 0.0)
            if turn:
                out_2[a] = fresh
                icopy_2(a).wait()
                fresh = jnp.where(keep, dot3(fresh, inv_2[a]), 0.0)
            for r in range(copies):
                out[r, a] = fresh


def level_step(level, copies, kind, table, known, right, inverse, panel, turn=None):
    cap = CAP_U if kind else CAP_L
    ins, specs = [table], [SMEM]
    for x, spec in ((known, VMEM), (right, VMEM), (inverse, HBM)):
        if x is not None:
            ins.append(x)
            specs.append(spec)
    if panel is not None:
        ins += list(panel)
        specs += [HBM, HBM]
    if turn is not None:
        ins.append(turn)
        specs.append(HBM)

    def kernel(*refs):
        refs = list(refs)
        given = [refs.pop(0)]
        given.append(refs.pop(0) if known is not None else None)
        given += [refs.pop(0), refs.pop(0)]
        given += [refs.pop(0), refs.pop(0)] if panel is not None else [None, None]
        level_kernel(level, copies, kind, cap, turn is not None, *given, *refs)

    out_shape = [jax.ShapeDtypeStruct((copies, RB, HS, W), jnp.float32)]
    scratch = [pltpu.VMEM((LIST, W, W), jnp.float32), pltpu.VMEM((RB, W, W), jnp.float32)]
    if turn is not None:
        out_shape.append(jax.ShapeDtypeStruct((RB, HS, W), jnp.float32))
        scratch.append(pltpu.VMEM((RB, W, W), jnp.float32))
    scratch += [pltpu.SemaphoreType.DMA((LIST,)), pltpu.SemaphoreType.DMA((2 * RB,))]
    out = pl.pallas_call(
        kernel,
        out_shape=out_shape,
        in_specs=specs,
        out_specs=[VMEM] * len(out_shape),
        scratch_shapes=scratch,
        compiler_params=pltpu.CompilerParams(vmem_limit_bytes=24 * 1024 * 1024),
    )(*ins)
    return out if turn is not None else out[0]


def across_kernel(table, known, lower, out, blocks, sems):
    count = table[COUNTS, 2]

    def copy(t):
        n = table[LIST_T, t]
        return pltpu.make_async_copy(lower.at[n >> 4, n & (CB - 1)], blocks.at[t], sems.at[t])

    pl.loop(0, count)(lambda t: copy(t).start())
    out[...] = jnp.zeros_like(out)

    def step(t, carry):
        copy(t).wait()
        n = table[LIST_T, t]
        a = n >> 4
        c = n & (CB - 1)
        x = known[:, c & 1, c >> 1].reshape(NRHS, W)
        out[:, a] += dot3(x, blocks[t]).reshape(PC, HS, W)
        return carry

    lax.fori_loop(0, count, step, 0)


def across(table, known, lower):
    return pl.pallas_call(
        across_kernel,
        out_shape=jax.ShapeDtypeStruct((PC, RB, HS, W), jnp.float32),
        in_specs=[SMEM, VMEM, HBM],
        out_specs=VMEM,
        scratch_shapes=[pltpu.VMEM((NB, W, W), jnp.float32), pltpu.SemaphoreType.DMA((NB,))],
        compiler_params=pltpu.CompilerParams(vmem_limit_bytes=24 * 1024 * 1024),
    )(table, known, lower)


def gather_panel(packed):
    here = lax.all_gather(packed, "pcol", axis_index_groups=SAME_CORE, tiled=True)
    there = lax.ppermute(here, "pcol", [(k, k ^ 1) for k in range(PC)])
    return here, there


def local(rhs, lower, upper, lower_inverse, upper_inverse, pattern, levels, widths):
    q = lax.axis_index("pcol")
    right = rhs.reshape(RB, NRHS, W)
    lower_blocks = lower.reshape(RB, CB, W, W)
    upper_blocks = upper.reshape(RB, CB, W, W)
    lower_inv = lower_inverse.reshape(RB, W, W)
    upper_inv = upper_inverse.reshape(RB, W, W)
    table = tables(pattern, levels, widths)
    panel_l = gather_panel(pack(0, CAP_L, table, lower_blocks))
    panel_u = gather_panel(pack(1, CAP_U, table, upper_blocks))
    swap = lambda x: lax.all_to_all(x, "prow", 0, 0)

    b = lax.dynamic_slice_in_dim(right, q * HS, HS, 1)
    known = swap(level_step(0, PR, 0, table, None, b, lower_inv, None))
    for level in range(1, LEVELS - 1):
        if level == 3:
            split = known.reshape(2, PC, RB, HS, W).transpose(1, 0, 2, 3, 4)
            columns = lax.all_to_all(split, "pcol", 0, 0)
            sums = lax.all_to_all(across(table, columns, lower_blocks), "pcol", 0, 0)
            b = b - jnp.sum(sums, axis=0)
        known = swap(level_step(level, PR, 0, table, known, b, lower_inv, panel_l))
    state, forward = level_step(LEVELS - 1, PR, 0, table, known, b, lower_inv, panel_l, upper_inv)
    full_f = lax.all_gather(forward, "pcol")
    known = swap(state)
    for level in range(LEVELS - 2, 0, -1):
        known = swap(level_step(level, PR, 1, table, known, forward, upper_inv, panel_u))
    state = level_step(0, PC, 1, table, known, forward, upper_inv, panel_u)
    full_s = lax.all_to_all(state, "pcol", 0, 0)
    shape = rhs.shape
    whole = lambda x: x.transpose(1, 0, 2, 3).reshape(shape)
    args = (rhs, lower, upper, lower_inverse, upper_inverse, pattern, levels, widths)
    done = lax.while_loop(
        lambda c: c[2] > 0,
        lambda c: general(*args) + (jnp.int32(0),),
        (whole(full_f), whole(full_s), table[COUNTS, 3]),
    )
    return done[0], done[1]


def solution(mesh):
    in_specs = (
        P(None, "prow", None, None),
        P(None, "prow", None, "pcol", None, None),
        P(None, "prow", None, "pcol", None, None),
        P(None, "prow", None, None),
        P(None, "prow", None, None),
        P(),
        P(),
        P(),
    )
    out_specs = (P(None, "prow", None, None), P(None, "prow", None, None))
    return jax.shard_map(local, mesh=mesh, in_specs=in_specs, out_specs=out_specs, check_vma=False)
```

```python
import jax
import jax.numpy as jnp
from jax import lax
from jax.experimental import pallas as pl
from jax.experimental.pallas import tpu as pltpu
from jax.sharding import PartitionSpec as P

LEVELS = 6
W = 128
NRHS = 64
NB = 128
RB = 8
CB = 16
PR = 16
PC = 8
HS = NRHS // PC
CAP_L = 10
CAP_U = 28
LIST = 64
GROUP = 4
HBM = pl.BlockSpec(memory_space=pl.ANY)
ROOM = 60 * 1024 * 1024
SMEM = pl.BlockSpec(memory_space=pltpu.SMEM)
VMEM = pl.BlockSpec(memory_space=pltpu.VMEM)
LEVEL, WIDTH, START_L, END_L, START_U, END_U = range(6)
LIST_L, LIST_U, LIST_T, PACK_L, PACK_U, COUNTS = range(8, 14)


def spread(value, axis, source):
    kept = jnp.where(lax.axis_index(axis) == source, value, 0).astype(value.dtype)
    return lax.psum(kept, axis)


def apply_inverse(inverse, right):
    return jnp.einsum("akl,ahl->ahk", inverse, right, precision=lax.Precision.HIGHEST)


def solve_levels(blocks, inverse, right, valid, row_levels, mask, rising):
    prow_count = lax.axis_size("prow")
    pcol_count = lax.axis_size("pcol")
    column = lax.axis_index("pcol")
    ratio = prow_count // pcol_count
    masked = blocks * mask[:, :, None, None]
    row_state = jnp.zeros(right.shape, jnp.float32)
    col_state = jnp.zeros((masked.shape[1],) + right.shape[1:], jnp.float32)
    order = list(range(LEVELS)) if rising else list(range(LEVELS - 1, -1, -1))
    for place, level in enumerate(order):
        partial_sum = jnp.einsum(
            "ackl,chl->ahk", masked, col_state, precision=lax.Precision.HIGHEST
        )
        total = lax.psum(partial_sum, "pcol")
        fresh = apply_inverse(inverse, right - total) * valid
        current = (row_levels == level)[:, None, None]
        row_state = jnp.where(current, fresh, row_state)
        if place + 1 < LEVELS:
            pieces = []
            for offset in range(ratio):
                pieces.append(spread(row_state, "prow", column + offset * pcol_count))
            stacked = jnp.stack(pieces, axis=1)
            col_state = stacked.reshape((-1,) + right.shape[1:])
    return row_state


def general(rhs, lower, upper, lower_inverse, upper_inverse, pattern, levels, widths):
    prow_count = lax.axis_size("prow")
    pcol_count = lax.axis_size("pcol")
    row_index = lax.axis_index("prow")
    col_index = lax.axis_index("pcol")
    row_blocks = rhs.shape[0]
    col_blocks = lower.shape[2]
    width = rhs.shape[3]
    right = rhs.reshape(row_blocks, rhs.shape[2], width)
    lower_local = lower.reshape(row_blocks, col_blocks, width, width)
    upper_local = upper.reshape(row_blocks, col_blocks, width, width)
    lower_inv = lower_inverse.reshape(row_blocks, width, width)
    upper_inv = upper_inverse.reshape(row_blocks, width, width)
    row_levels = lax.dynamic_index_in_dim(
        levels.reshape(row_blocks, prow_count), row_index, 1, keepdims=False
    )
    col_levels = lax.dynamic_index_in_dim(
        levels.reshape(col_blocks, pcol_count), col_index, 1, keepdims=False
    )
    row_widths = lax.dynamic_index_in_dim(
        widths.reshape(row_blocks, prow_count), row_index, 1, keepdims=False
    )
    grid = pattern.reshape(row_blocks, prow_count, col_blocks, pcol_count)
    grid = lax.dynamic_index_in_dim(grid, row_index, 1, keepdims=False)
    grid = lax.dynamic_index_in_dim(grid, col_index, 2, keepdims=False).astype(jnp.float32)
    valid = (jnp.arange(width)[None, :] < row_widths[:, None]).astype(jnp.float32)[:, None, :]
    below = grid * (col_levels[None, :] < row_levels[:, None]).astype(jnp.float32)
    above = grid * (col_levels[None, :] > row_levels[:, None]).astype(jnp.float32)
    forward = solve_levels(lower_local, lower_inv, right, valid, row_levels, below, True)
    solution = solve_levels(upper_local, upper_inv, forward, valid, row_levels, above, False)
    shape = rhs.shape
    return (forward.reshape(shape), solution.reshape(shape))


def dot3(x, w):
    m, n = x.shape[0], w.shape[0]
    xh = x.astype(jnp.bfloat16).astype(jnp.float32)
    xs = jnp.concatenate([xh, x - xh], axis=0).astype(jnp.bfloat16)
    wh = w.astype(jnp.bfloat16)
    wl = (w - wh.astype(jnp.float32)).astype(jnp.bfloat16)
    ws = jnp.concatenate([wh, wl], axis=0)
    y = lax.dot_general(xs, ws, (((1,), (1,)), ((), ())), preferred_element_type=jnp.float32)
    return (y[m:, n:] + y[:m, n:]) + (y[m:, :n] + y[:m, :n])


def iota(shape, dim):
    return lax.broadcasted_iota(jnp.int32, shape, dim)


def cost(mib):
    return pl.CostEstimate(flops=0, bytes_accessed=mib << 20, transcendentals=0)


def flag(cond):
    return jnp.where(cond, 1.0, 0.0)


def table_kernel(pattern, levels, widths, out):
    p = lax.axis_index("prow")
    q = lax.axis_index("pcol")
    lev = levels[...].astype(jnp.float32)
    wid = widths[...].astype(jnp.float32)
    i = iota((NB, NB), 0)
    j = iota((NB, NB), 1)
    lev_col = jnp.sum(jnp.where(i == j, lev, 0.0), axis=1, keepdims=True)
    linked = flag(pattern[...] > 0)
    low = linked * flag(lev < lev_col)
    high = linked * flag(lev > lev_col)
    near = low * flag((lev_col < 2.5) | (lev > 2.5))
    far = low - near
    same = flag((i & (PC - 1)) == (j & (PC - 1)))
    ahead = flag(i < j)
    same_ahead = same * ahead

    def dot(x, y):
        return jnp.dot(x, y, preferred_element_type=jnp.float32)

    by_row = flag((iota((PR, NB), 1) & (PR - 1)) == iota((PR, NB), 0))

    def over(full, cap):
        rows = dot(by_row, full)
        most = jnp.max(jnp.max(dot(rows, same), axis=1, keepdims=True), axis=0, keepdims=True)
        listed = jnp.max(jnp.sum(rows, axis=1, keepdims=True), axis=0, keepdims=True)
        return flag((most > cap) | (listed > LIST))

    full = jnp.maximum(over(near, CAP_L), over(high, CAP_U))

    lane = iota((RB, NB), 1)
    sub = iota((RB, NB), 0)
    mine = flag(lane == sub * PR + p)
    row_lev = jnp.sum(mine * lev, axis=1, keepdims=True)
    row_wid = jnp.sum(mine * wid, axis=1, keepdims=True)
    col = lane & (PC - 1)
    own = flag(col == q)
    node = lane.astype(jnp.float32)
    spot = (sub * CB + (lane >> 3)).astype(jnp.float32)

    def ranks(sel):
        total = jnp.zeros((1, NB), jnp.float32)
        rows = []
        for a in range(RB):
            rows.append(total)
            total = total + sel[a : a + 1]
        prior = jnp.concatenate(rows, axis=0)
        start = jnp.sum(prior, axis=1, keepdims=True)
        end = start + jnp.sum(sel, axis=1, keepdims=True)
        return start, end, start + dot(sel, ahead), dot(prior, same) + dot(sel, same_ahead)

    def listing(sel, place, value, size):
        t = iota((size, NB), 0).astype(jnp.float32)
        held = jnp.zeros((size, NB), jnp.float32)
        for a in range(RB):
            hit = flag(t == place[a : a + 1]) * sel[a : a + 1]
            held = held + hit * value[a : a + 1]
        ones = jnp.ones((RB, NB), jnp.float32)
        row = lax.dot_general(ones, held, (((1,), (1,)), ((), ())), preferred_element_type=jnp.float32)[:1]
        if size < NB:
            row = jnp.concatenate([row, jnp.zeros((1, NB - size), jnp.float32)], axis=1)
        return row

    def count(sel):
        return jnp.sum(jnp.sum(sel, axis=1, keepdims=True), axis=0, keepdims=True)

    def panel(sel, cap):
        start, end, place, rank = ranks(sel)
        slot = (col * cap).astype(jnp.float32) + jnp.minimum(rank, cap - 1.0)
        listed = listing(sel, place, slot, LIST) * NB + listing(sel, place, node, LIST)
        packed = listing(sel * own, rank, spot, 32)
        return jnp.minimum(start, LIST), jnp.minimum(end, LIST), listed, packed, jnp.minimum(count(sel * own), cap)

    near_p = dot(mine, near)
    high_p = dot(mine, high)
    far_p = dot(mine, far)
    start_l, end_l, list_l, pack_l, count_l = panel(near_p, CAP_L)
    start_u, end_u, list_u, pack_u, count_u = panel(high_p, CAP_U)
    _, _, _, rank_t = ranks(far_p)
    list_t = listing(far_p * own, rank_t, spot, NB)
    count_t = count(far_p * own)
    rows = jnp.zeros((RB, NB), jnp.float32)
    for k, value in enumerate([row_lev, row_wid, start_l, end_l, start_u, end_u]):
        rows = rows + flag(lane == k) * value
    counts = jnp.zeros((1, NB), jnp.float32)
    for k, value in enumerate([count_l, count_u, count_t, full]):
        counts = counts + flag(lane[:1] == k) * value
    none = jnp.zeros((1, NB), jnp.float32)
    lists = jnp.concatenate([list_l, list_u, list_t, pack_l, pack_u, counts, none, none], axis=0)
    out[0:8, :] = rows.astype(jnp.int32)
    out[8:16, :] = lists.astype(jnp.int32)


def tables(pattern, levels, widths):
    return pl.pallas_call(
        table_kernel,
        out_shape=jax.ShapeDtypeStruct((16, NB), jnp.int32),
        in_specs=[VMEM, VMEM, VMEM],
        out_specs=VMEM,
        cost_estimate=cost(4),
    )(pattern, levels.reshape(1, NB), widths.reshape(1, NB))


def pack_kernel(where, cap, table, blocks, _, out, held, sems_in, sems_out):
    count = table[COUNTS, where]
    row = PACK_L + where

    def load(t):
        n = table[row, t]
        return pltpu.make_async_copy(blocks.at[n >> 4, n & (CB - 1)], held.at[t], sems_in.at[t])

    def store(t):
        return pltpu.make_async_copy(held.at[t], out.at[t], sems_out.at[t])

    pl.loop(0, count)(lambda t: load(t).start())

    @pl.loop(0, count)
    def _(t):
        load(t).wait()
        store(t).start()

    pl.loop(0, count)(lambda t: store(t).wait())


def pack(where, cap, table, blocks, after):
    return pl.pallas_call(
        lambda *refs: pack_kernel(where, cap, *refs),
        out_shape=jax.ShapeDtypeStruct((cap, W, W), jnp.float32),
        in_specs=[SMEM, HBM, HBM],
        out_specs=HBM,
        scratch_shapes=[
            pltpu.VMEM((cap, W, W), jnp.float32),
            pltpu.SemaphoreType.DMA((cap,)),
            pltpu.SemaphoreType.DMA((cap,)),
        ],
        cost_estimate=cost(4),
    )(table, blocks, after)


def level_kernel(level, copies, kind, turn, both, table, known, right, inverse, panel, *rest):
    if turn:
        inverse_2, out, out_2, blocks, inv, inv_2, sems, isems = rest
    else:
        out, blocks, inv, sems, isems = rest
    p = lax.axis_index("prow")
    row = LIST_U if kind else LIST_L
    first, last = (START_U, END_U) if kind else (START_L, END_L)

    def copy(t):
        return pltpu.make_async_copy(panel.at[table[row, t] >> 7], blocks.at[t], sems.at[t])

    def icopy(a):
        return pltpu.make_async_copy(inverse.at[a], inv.at[a], isems.at[a])

    def icopy_2(a):
        return pltpu.make_async_copy(inverse_2.at[a], inv_2.at[a], isems.at[RB + a])

    for a in range(RB):
        @pl.when(table[a, LEVEL] == level)
        def _():
            if panel is not None:
                pl.loop(table[a, first], table[a, last])(lambda t: copy(t).start())
            icopy(a).start()
            if turn:
                icopy_2(a).start()

    lane = iota((HS, W), 1)
    for a in range(RB):
        old = known[p, a] if known is not None else jnp.zeros((HS, W), jnp.float32)
        for r in range(copies):
            if both:
                out[r, 0, a] = right[a]
                out[r, 1, a] = old
            else:
                out[r, a] = old if not turn else jnp.zeros((HS, W), jnp.float32)
        if turn:
            out_2[a] = old

        @pl.when(table[a, LEVEL] == level)
        def _():
            acc = right[a]
            if panel is not None:
                start, end = table[a, first], table[a, last]

                def step(g, acc):
                    xs, ws = [], []
                    for u in range(GROUP):
                        t = start + g * GROUP + u
                        there = t < end

                        @pl.when(there)
                        def _():
                            copy(t).wait()

                        t = jnp.minimum(t, end - 1)
                        node = table[row, t] & (NB - 1)
                        xs.append(known[node & (PR - 1), node >> 4] * jnp.where(there, 1.0, 0.0))
                        ws.append(blocks[t])
                    for u in range(0, GROUP, 2):
                        x = jnp.concatenate(xs[u : u + 2], axis=1)
                        acc = acc - dot3(x, jnp.concatenate(ws[u : u + 2], axis=1))
                    return acc

                acc = lax.fori_loop(0, (end - start + GROUP - 1) // GROUP, step, acc)
            icopy(a).wait()
            keep = lane < table[a, WIDTH]
            fresh = jnp.where(keep, dot3(acc, inv[a]), 0.0)
            if turn:
                out_2[a] = fresh
                icopy_2(a).wait()
                fresh = jnp.where(keep, dot3(fresh, inv_2[a]), 0.0)
            for r in range(copies):
                if both:
                    out[r, 1, a] = fresh
                else:
                    out[r, a] = fresh


def level_step(level, copies, kind, table, known, right, inverse, panel, turn=None, both=False):
    ins, specs = [table], [SMEM]
    for x, spec in ((known, VMEM), (right, VMEM), (inverse, HBM)):
        if x is not None:
            ins.append(x)
            specs.append(spec)
    if panel is not None:
        ins.append(panel)
        specs.append(HBM)
    if turn is not None:
        ins.append(turn)
        specs.append(HBM)

    def kernel(*refs):
        refs = list(refs)
        given = [refs.pop(0)]
        given.append(refs.pop(0) if known is not None else None)
        given += [refs.pop(0), refs.pop(0)]
        given.append(refs.pop(0) if panel is not None else None)
        level_kernel(level, copies, kind, turn is not None, both, *given, *refs)

    shape = (copies, 2, RB, HS, W) if both else (copies, RB, HS, W)
    out_shape = [jax.ShapeDtypeStruct(shape, jnp.float32)]
    scratch = [pltpu.VMEM((LIST, W, W), jnp.float32), pltpu.VMEM((RB, W, W), jnp.float32)]
    if turn is not None:
        out_shape.append(jax.ShapeDtypeStruct((RB, HS, W), jnp.float32))
        scratch.append(pltpu.VMEM((RB, W, W), jnp.float32))
    scratch += [pltpu.SemaphoreType.DMA((LIST,)), pltpu.SemaphoreType.DMA((2 * RB,))]
    out = pl.pallas_call(
        kernel,
        out_shape=out_shape,
        in_specs=specs,
        out_specs=[VMEM] * len(out_shape),
        scratch_shapes=scratch,
        compiler_params=pltpu.CompilerParams(vmem_limit_bytes=ROOM),
        cost_estimate=cost(8),
    )(*ins)
    return out if turn is not None else out[0]


def across_kernel(table, known, lower, out, blocks, sems):
    count = table[COUNTS, 2]

    def copy(t):
        n = table[LIST_T, t]
        return pltpu.make_async_copy(lower.at[n >> 4, n & (CB - 1)], blocks.at[t], sems.at[t])

    pl.loop(0, count)(lambda t: copy(t).start())
    out[...] = jnp.zeros_like(out)

    def step(t, carry):
        copy(t).wait()
        n = table[LIST_T, t]
        a = n >> 4
        c = n & (CB - 1)
        x = known[:, c & 1, c >> 1].reshape(NRHS, W)
        out[:, a] += dot3(x, blocks[t]).reshape(PC, HS, W)
        return carry

    lax.fori_loop(0, count, step, 0)


def across(table, known, lower):
    return pl.pallas_call(
        across_kernel,
        out_shape=jax.ShapeDtypeStruct((PC, RB, HS, W), jnp.float32),
        in_specs=[SMEM, VMEM, HBM],
        out_specs=VMEM,
        scratch_shapes=[pltpu.VMEM((NB, W, W), jnp.float32), pltpu.SemaphoreType.DMA((NB,))],
        compiler_params=pltpu.CompilerParams(vmem_limit_bytes=ROOM),
        cost_estimate=cost(8),
    )(table, known, lower)


def local(rhs, lower, upper, lower_inverse, upper_inverse, pattern, levels, widths):
    q = lax.axis_index("pcol")
    right = rhs.reshape(RB, NRHS, W)
    lower_blocks = lower.reshape(RB, CB, W, W)
    upper_blocks = upper.reshape(RB, CB, W, W)
    lower_inv = lower_inverse.reshape(RB, W, W)
    upper_inv = upper_inverse.reshape(RB, W, W)
    table = tables(pattern, levels, widths)
    swap = lambda x: lax.all_to_all(x, "prow", 0, 0)

    b = lax.dynamic_slice_in_dim(right, q * HS, HS, 1)
    leaves = level_step(0, PR, 0, table, None, b, lower_inv, None)
    panel_l = lax.all_gather(pack(0, CAP_L, table, lower_blocks, leaves), "pcol", tiled=True)
    known = swap(leaves)
    panel_u = lax.all_gather(pack(1, CAP_U, table, upper_blocks, known), "pcol", tiled=True)
    for level in range(1, LEVELS - 1):
        if level == 3:
            split = known.reshape(2, PC, RB, HS, W).transpose(1, 0, 2, 3, 4)
            columns = lax.all_to_all(split, "pcol", 0, 0)
            sums = lax.all_to_all(across(table, columns, lower_blocks), "pcol", 0, 0)
            b = b - jnp.sum(sums, axis=0)
        known = swap(level_step(level, PR, 0, table, known, b, lower_inv, panel_l))
    state, forward = level_step(LEVELS - 1, PR, 0, table, known, b, lower_inv, panel_l, upper_inv)
    known = swap(state)
    for level in range(LEVELS - 2, 0, -1):
        known = swap(level_step(level, PR, 1, table, known, forward, upper_inv, panel_u))
    state = level_step(0, PC, 1, table, known, forward, upper_inv, panel_u, both=True)
    full = lax.all_to_all(state, "pcol", 0, 0)
    shape = rhs.shape
    whole = lambda x: x.transpose(1, 0, 2, 3).reshape(shape)
    args = (rhs, lower, upper, lower_inverse, upper_inverse, pattern, levels, widths)
    done = lax.while_loop(
        lambda c: c[2] > 0,
        lambda c: general(*args) + (jnp.int32(0),),
        (whole(full[:, 0]), whole(full[:, 1]), table[COUNTS, 3]),
    )
    return done[0], done[1]


def solution(mesh):
    in_specs = (
        P(None, "prow", None, None),
        P(None, "prow", None, "pcol", None, None),
        P(None, "prow", None, "pcol", None, None),
        P(None, "prow", None, None),
        P(None, "prow", None, None),
        P(),
        P(),
        P(),
    )
    out_specs = (P(None, "prow", None, None), P(None, "prow", None, None))
    return jax.shard_map(local, mesh=mesh, in_specs=in_specs, out_specs=out_specs, check_vma=False)
```

```python
import jax
import jax.numpy as jnp
from jax import lax
from jax.experimental import pallas as pl
from jax.experimental.pallas import tpu as pltpu
from jax.sharding import PartitionSpec as P

LEVELS = 6
W = 128
NRHS = 64
NB = 128
RB = 8
CB = 16
PR = 16
PC = 8
HS = NRHS // PC
CAP_L = 10
CAP_U = 28
LIST = 64
GROUP = 4
HBM = pl.BlockSpec(memory_space=pl.ANY)
ROOM = 52 * 1024 * 1024
SMEM = pl.BlockSpec(memory_space=pltpu.SMEM)
VMEM = pl.BlockSpec(memory_space=pltpu.VMEM)
WIDTH = 0
LIST_L, LIST_U, LIST_T, PACK_L, PACK_U, COUNTS, ROWS, STARTS = range(8, 16)
HALF = 16


def spread(value, axis, source):
    kept = jnp.where(lax.axis_index(axis) == source, value, 0).astype(value.dtype)
    return lax.psum(kept, axis)


def apply_inverse(inverse, right):
    return jnp.einsum("akl,ahl->ahk", inverse, right, precision=lax.Precision.HIGHEST)


def solve_levels(blocks, inverse, right, valid, row_levels, mask, rising):
    prow_count = lax.axis_size("prow")
    pcol_count = lax.axis_size("pcol")
    column = lax.axis_index("pcol")
    ratio = prow_count // pcol_count
    masked = blocks * mask[:, :, None, None]
    row_state = jnp.zeros(right.shape, jnp.float32)
    col_state = jnp.zeros((masked.shape[1],) + right.shape[1:], jnp.float32)
    order = list(range(LEVELS)) if rising else list(range(LEVELS - 1, -1, -1))
    for place, level in enumerate(order):
        partial_sum = jnp.einsum(
            "ackl,chl->ahk", masked, col_state, precision=lax.Precision.HIGHEST
        )
        total = lax.psum(partial_sum, "pcol")
        fresh = apply_inverse(inverse, right - total) * valid
        current = (row_levels == level)[:, None, None]
        row_state = jnp.where(current, fresh, row_state)
        if place + 1 < LEVELS:
            pieces = []
            for offset in range(ratio):
                pieces.append(spread(row_state, "prow", column + offset * pcol_count))
            stacked = jnp.stack(pieces, axis=1)
            col_state = stacked.reshape((-1,) + right.shape[1:])
    return row_state


def general(rhs, lower, upper, lower_inverse, upper_inverse, pattern, levels, widths):
    prow_count = lax.axis_size("prow")
    pcol_count = lax.axis_size("pcol")
    row_index = lax.axis_index("prow")
    col_index = lax.axis_index("pcol")
    row_blocks = rhs.shape[0]
    col_blocks = lower.shape[2]
    width = rhs.shape[3]
    right = rhs.reshape(row_blocks, rhs.shape[2], width)
    lower_local = lower.reshape(row_blocks, col_blocks, width, width)
    upper_local = upper.reshape(row_blocks, col_blocks, width, width)
    lower_inv = lower_inverse.reshape(row_blocks, width, width)
    upper_inv = upper_inverse.reshape(row_blocks, width, width)
    row_levels = lax.dynamic_index_in_dim(
        levels.reshape(row_blocks, prow_count), row_index, 1, keepdims=False
    )
    col_levels = lax.dynamic_index_in_dim(
        levels.reshape(col_blocks, pcol_count), col_index, 1, keepdims=False
    )
    row_widths = lax.dynamic_index_in_dim(
        widths.reshape(row_blocks, prow_count), row_index, 1, keepdims=False
    )
    grid = pattern.reshape(row_blocks, prow_count, col_blocks, pcol_count)
    grid = lax.dynamic_index_in_dim(grid, row_index, 1, keepdims=False)
    grid = lax.dynamic_index_in_dim(grid, col_index, 2, keepdims=False).astype(jnp.float32)
    valid = (jnp.arange(width)[None, :] < row_widths[:, None]).astype(jnp.float32)[:, None, :]
    below = grid * (col_levels[None, :] < row_levels[:, None]).astype(jnp.float32)
    above = grid * (col_levels[None, :] > row_levels[:, None]).astype(jnp.float32)
    forward = solve_levels(lower_local, lower_inv, right, valid, row_levels, below, True)
    solution = solve_levels(upper_local, upper_inv, forward, valid, row_levels, above, False)
    shape = rhs.shape
    return (forward.reshape(shape), solution.reshape(shape))


def dot3(x, w):
    m, n = x.shape[0], w.shape[0]
    xh = x.astype(jnp.bfloat16).astype(jnp.float32)
    xs = jnp.concatenate([xh, x - xh], axis=0).astype(jnp.bfloat16)
    wh = w.astype(jnp.bfloat16)
    wl = (w - wh.astype(jnp.float32)).astype(jnp.bfloat16)
    ws = jnp.concatenate([wh, wl], axis=0)
    y = lax.dot_general(xs, ws, (((1,), (1,)), ((), ())), preferred_element_type=jnp.float32)
    return (y[m:, n:] + y[:m, n:]) + (y[m:, :n] + y[:m, :n])


def iota(shape, dim):
    return lax.broadcasted_iota(jnp.int32, shape, dim)


def cost(mib):
    return pl.CostEstimate(flops=0, bytes_accessed=mib << 20, transcendentals=0)


def flag(cond):
    return jnp.where(cond, 1.0, 0.0)


def table_kernel(pattern, levels, widths, out):
    p = lax.axis_index("prow")
    q = lax.axis_index("pcol")
    lev = levels[...].astype(jnp.float32)
    wid = widths[...].astype(jnp.float32)
    i = iota((NB, NB), 0)
    j = iota((NB, NB), 1)
    lev_col = jnp.sum(jnp.where(i == j, lev, 0.0), axis=1, keepdims=True)
    linked = flag(pattern[...] > 0)
    low = linked * flag(lev < lev_col)
    high = linked * flag(lev > lev_col)
    near = low * flag((lev_col < 2.5) | (lev > 2.5))
    far = low - near
    same = flag((i & (PC - 1)) == (j & (PC - 1)))
    ahead = flag(i < j)
    same_ahead = same * ahead

    def dot(x, y):
        return jnp.dot(x, y, preferred_element_type=jnp.float32)

    by_row = flag((iota((PR, NB), 1) & (PR - 1)) == iota((PR, NB), 0))

    def over(full, cap):
        rows = dot(by_row, full)
        most = jnp.max(jnp.max(dot(rows, same), axis=1, keepdims=True), axis=0, keepdims=True)
        listed = jnp.max(jnp.sum(rows, axis=1, keepdims=True), axis=0, keepdims=True)
        return flag((most > cap) | (listed > LIST))

    full = jnp.maximum(over(near, CAP_L), over(high, CAP_U))

    lane = iota((RB, NB), 1)
    sub = iota((RB, NB), 0)
    mine = flag(lane == sub * PR + p)
    row_lev = jnp.sum(mine * lev, axis=1, keepdims=True)
    row_wid = jnp.sum(mine * wid, axis=1, keepdims=True)
    col = lane & (PC - 1)
    own = flag(col == q)
    node = lane.astype(jnp.float32)
    spot = (sub * CB + (lane >> 3)).astype(jnp.float32)

    def ranks(sel):
        total = jnp.zeros((1, NB), jnp.float32)
        rows = []
        for a in range(RB):
            rows.append(total)
            total = total + sel[a : a + 1]
        return dot(jnp.concatenate(rows, axis=0), same) + dot(sel, same_ahead)

    def ordered(size):
        start = jnp.zeros((RB, 1), jnp.float32)
        below = jnp.zeros((1, NB), jnp.float32)
        index = iota((RB, 1), 0)
        for a in range(RB):
            first = (row_lev[a : a + 1] < row_lev) | ((row_lev[a : a + 1] == row_lev) & (index > a))
            start = start + flag(first) * size[a : a + 1]
            below = below + flag(row_lev[a : a + 1] < node[:1]) * size[a : a + 1]
        return start, below

    def listing(sel, place, value, size):
        t = iota((size, NB), 0).astype(jnp.float32)
        held = jnp.zeros((size, NB), jnp.float32)
        for a in range(RB):
            hit = flag(t == place[a : a + 1]) * sel[a : a + 1]
            held = held + hit * value[a : a + 1]
        ones = jnp.ones((RB, NB), jnp.float32)
        row = lax.dot_general(ones, held, (((1,), (1,)), ((), ())), preferred_element_type=jnp.float32)[:1]
        if size < NB:
            row = jnp.concatenate([row, jnp.zeros((1, NB - size), jnp.float32)], axis=1)
        return row

    def count(sel):
        return jnp.sum(jnp.sum(sel, axis=1, keepdims=True), axis=0, keepdims=True)

    def panel(sel, cap):
        rank = ranks(sel)
        start, below = ordered(jnp.sum(sel, axis=1, keepdims=True))
        place = start + dot(sel, ahead)
        slot = (col * cap).astype(jnp.float32) + jnp.minimum(rank, cap - 1.0)
        listed = listing(sel, place, slot, LIST) * (NB * RB) + listing(sel, place, node, LIST) * RB
        listed = listed + listing(sel, place, sub.astype(jnp.float32), LIST)
        packed = listing(sel * own, rank, spot, 32)
        return jnp.minimum(below, LIST), listed, packed, jnp.minimum(count(sel * own), cap)

    near_p = dot(mine, near)
    high_p = dot(mine, high)
    far_p = dot(mine, far)
    below_l, list_l, pack_l, count_l = panel(near_p, CAP_L)
    below_u, list_u, pack_u, count_u = panel(high_p, CAP_U)
    list_t = listing(far_p * own, ranks(far_p), spot, NB)
    count_t = count(far_p * own)
    rows = flag(lane == WIDTH) * row_wid
    counts = jnp.zeros((1, NB), jnp.float32)
    for k, value in enumerate([count_l, count_u, count_t, full]):
        counts = counts + flag(lane[:1] == k) * value
    spot_of, below_r = ordered(jnp.ones((RB, 1), jnp.float32))
    order = jnp.zeros((1, NB), jnp.float32)
    for a in range(RB):
        order = order + flag(spot_of[a : a + 1] == node[:1]) * a

    def beside(x, y):
        return jnp.concatenate([x[:, :HALF], y[:, :HALF], jnp.zeros((1, NB - 2 * HALF), jnp.float32)], axis=1)

    order = beside(order, below_r)
    starts = beside(below_l, below_u)
    lists = jnp.concatenate([list_l, list_u, list_t, pack_l, pack_u, counts, order, starts], axis=0)
    out[0:8, :] = rows.astype(jnp.int32)
    out[8:16, :] = lists.astype(jnp.int32)


def tables(pattern, levels, widths):
    return pl.pallas_call(
        table_kernel,
        out_shape=jax.ShapeDtypeStruct((16, NB), jnp.int32),
        in_specs=[VMEM, VMEM, VMEM],
        out_specs=VMEM,
        cost_estimate=cost(4),
    )(pattern, levels.reshape(1, NB), widths.reshape(1, NB))


def pack_kernel(where, cap, table, blocks, _, out, token, held, sems_in, sems_out):
    count = table[COUNTS, where]
    row = PACK_L + where

    def load(t):
        n = table[row, t]
        return pltpu.make_async_copy(blocks.at[n >> 4, n & (CB - 1)], held.at[t], sems_in.at[t])

    def store(t):
        return pltpu.make_async_copy(held.at[t], out.at[t], sems_out.at[t])

    pl.loop(0, count)(lambda t: load(t).start())
    token[...] = jnp.zeros_like(token)

    @pl.loop(0, count)
    def _(t):
        load(t).wait()
        store(t).start()

    pl.loop(0, count)(lambda t: store(t).wait())


def pack(where, cap, table, blocks, after):
    return pl.pallas_call(
        lambda *refs: pack_kernel(where, cap, *refs),
        out_shape=(
            jax.ShapeDtypeStruct((cap, W, W), jnp.float32),
            jax.ShapeDtypeStruct((HS, W), jnp.float32),
        ),
        in_specs=[SMEM, HBM, HBM],
        out_specs=(HBM, VMEM),
        scratch_shapes=[
            pltpu.VMEM((cap, W, W), jnp.float32),
            pltpu.SemaphoreType.DMA((cap,)),
            pltpu.SemaphoreType.DMA((cap,)),
        ],
        cost_estimate=cost(4),
    )(table, blocks, after)


def level_kernel(level, copies, kind, turn, both, sliced, table, known, right, inverse, panel, less, *rest):
    if turn:
        inverse_2, out, out_2, sums, blocks, inv, inv_2, sems, isems = rest
    else:
        out, sums, blocks, inv, sems, isems = rest
    p = lax.axis_index("prow")
    row = LIST_U if kind else LIST_L
    e0, e1 = table[STARTS, kind * HALF + level], table[STARTS, kind * HALF + level + 1]
    r0, r1 = table[ROWS, HALF + level], table[ROWS, HALF + level + 1]

    def copy(t):
        return pltpu.make_async_copy(panel.at[table[row, t] >> 10], blocks.at[t], sems.at[t])

    def icopy(a):
        return pltpu.make_async_copy(inverse.at[a], inv.at[a], isems.at[a])

    def icopy_2(a):
        return pltpu.make_async_copy(inverse_2.at[a], inv_2.at[a], isems.at[RB + a])

    if panel is not None:
        pl.loop(e0, e1)(lambda t: copy(t).start())

    @pl.loop(r0, r1)
    def _(r):
        icopy(table[ROWS, r]).start()
        if turn:
            icopy_2(table[ROWS, r]).start()

    shift = lax.axis_index("pcol") * HS
    for a in range(RB):
        mine = right[a, pl.ds(shift, HS)] if sliced else right[a]
        if less is not None:
            parts = [less[k, a] for k in range(PC)]
            while len(parts) > 1:
                parts = [x + y for x, y in zip(parts[::2], parts[1::2])]
            mine = mine - parts[0]
        sums[a] = mine
        old = known[p, a] if known is not None else jnp.zeros((HS, W), jnp.float32)
        for r in range(copies):
            if both:
                out[r, 0, a] = mine
                out[r, 1, a] = old
            else:
                out[r, a] = old if not turn else jnp.zeros((HS, W), jnp.float32)
        if turn:
            out_2[a] = old

    if panel is not None:
        @pl.loop(0, (e1 - e0 + GROUP - 1) >> 2)
        def _(g):
            terms = []
            for u in range(GROUP):
                t = e0 + g * GROUP + u
                there = t < e1

                @pl.when(there)
                def _():
                    copy(t).wait()

                t = jnp.minimum(t, e1 - 1)
                node = (table[row, t] >> 3) & (NB - 1)
                x = known[node & (PR - 1), node >> 4] * jnp.where(there, 1.0, 0.0)
                terms.append((table[row, t] & (RB - 1), dot3(x, blocks[t])))
            for a, term in terms:
                sums[a] -= term

    lane = iota((HS, W), 1)

    @pl.loop(0, (r1 - r0 + GROUP - 1) >> 2)
    def _(g):
        fresh = []
        for u in range(GROUP):
            r = r0 + g * GROUP + u
            there = r < r1
            a = table[ROWS, jnp.minimum(r, r1 - 1)]

            @pl.when(there)
            def _():
                icopy(a).wait()
                if turn:
                    icopy_2(a).wait()

            fresh.append((there, a, jnp.where(lane < table[a, WIDTH], dot3(sums[a], inv[a]), 0.0)))
        if turn:
            later = [jnp.where(lane < table[a, WIDTH], dot3(x, inv_2[a]), 0.0) for _, a, x in fresh]
            for there, a, x in fresh:
                out_2[a] = x
            fresh = [(there, a, x) for (there, a, _), x in zip(fresh, later)]
        for there, a, x in fresh:
            @pl.when(there)
            def _():
                for r in range(copies):
                    if both:
                        out[r, 1, a] = x
                    else:
                        out[r, a] = x


def level_step(level, copies, kind, table, known, right, inverse, panel, turn=None, both=False, sliced=False, after=None, less=None):
    ins, specs = [table], [SMEM]
    for x, spec in ((known, VMEM), (right, VMEM), (inverse, HBM)):
        if x is not None:
            ins.append(x)
            specs.append(spec)
    if panel is not None:
        ins.append(panel)
        specs.append(HBM)
    if less is not None:
        ins.append(less)
        specs.append(VMEM)
    if turn is not None:
        ins.append(turn)
        specs.append(HBM)
    if after is not None:
        ins.append(after)
        specs.append(HBM)

    def kernel(*refs):
        refs = list(refs)
        if after is not None:
            refs.pop(len(ins) - 1)
        given = [refs.pop(0)]
        given.append(refs.pop(0) if known is not None else None)
        given += [refs.pop(0), refs.pop(0)]
        given.append(refs.pop(0) if panel is not None else None)
        given.append(refs.pop(0) if less is not None else None)
        level_kernel(level, copies, kind, turn is not None, both, sliced, *given, *refs)

    shape = (copies, 2, RB, HS, W) if both else (copies, RB, HS, W)
    out_shape = [jax.ShapeDtypeStruct(shape, jnp.float32)]
    scratch = [pltpu.VMEM((RB, HS, W), jnp.float32), pltpu.VMEM((LIST, W, W), jnp.float32), pltpu.VMEM((RB, W, W), jnp.float32)]
    if turn is not None:
        out_shape.append(jax.ShapeDtypeStruct((RB, HS, W), jnp.float32))
        scratch.append(pltpu.VMEM((RB, W, W), jnp.float32))
    scratch += [pltpu.SemaphoreType.DMA((LIST,)), pltpu.SemaphoreType.DMA((2 * RB,))]
    out = pl.pallas_call(
        kernel,
        out_shape=out_shape,
        in_specs=specs,
        out_specs=[VMEM] * len(out_shape),
        scratch_shapes=scratch,
        compiler_params=pltpu.CompilerParams(vmem_limit_bytes=ROOM),
        cost_estimate=cost(8),
    )(*ins)
    return out if turn is not None else out[0]


def across_kernel(table, known, lower, out, blocks, sems):
    count = table[COUNTS, 2]

    def copy(t):
        n = table[LIST_T, t]
        return pltpu.make_async_copy(lower.at[n >> 4, n & (CB - 1)], blocks.at[t], sems.at[t])

    pl.loop(0, count)(lambda t: copy(t).start())
    out[...] = jnp.zeros_like(out)

    @pl.loop(0, (count + GROUP - 1) >> 2)
    def _(g):
        terms = []
        for u in range(GROUP):
            t = g * GROUP + u
            there = t < count

            @pl.when(there)
            def _():
                copy(t).wait()

            t = jnp.minimum(t, count - 1)
            n = table[LIST_T, t]
            c = n & (CB - 1)
            x = known[:, c & 1, c >> 1].reshape(NRHS, W) * jnp.where(there, 1.0, 0.0)
            terms.append((n >> 4, dot3(x, blocks[t]).reshape(PC, HS, W)))
        for a, term in terms:
            out[:, a] += term


def across(table, known, lower):
    return pl.pallas_call(
        across_kernel,
        out_shape=jax.ShapeDtypeStruct((PC, RB, HS, W), jnp.float32),
        in_specs=[SMEM, VMEM, HBM],
        out_specs=VMEM,
        scratch_shapes=[pltpu.VMEM((NB, W, W), jnp.float32), pltpu.SemaphoreType.DMA((NB,))],
        compiler_params=pltpu.CompilerParams(vmem_limit_bytes=ROOM),
        cost_estimate=cost(8),
    )(table, known, lower)


def local(rhs, lower, upper, lower_inverse, upper_inverse, pattern, levels, widths):
    right = rhs.reshape(RB, NRHS, W)
    lower_blocks = lower.reshape(RB, CB, W, W)
    upper_blocks = upper.reshape(RB, CB, W, W)
    lower_inv = lower_inverse.reshape(RB, W, W)
    upper_inv = upper_inverse.reshape(RB, W, W)
    table = tables(pattern, levels, widths)
    swap = lambda x: lax.all_to_all(x, "prow", 0, 0)

    packed_l, token = pack(0, CAP_L, table, lower_blocks, table)
    panel_l = lax.all_gather(packed_l, "pcol", tiled=True)
    leaves = level_step(0, PR, 0, table, None, right, lower_inv, None, sliced=True, after=token)
    known = swap(leaves)
    packed_u, _ = pack(1, CAP_U, table, upper_blocks, known[0, 0])
    panel_u = lax.all_gather(packed_u, "pcol", tiled=True)
    known = swap(level_step(1, PR, 0, table, known, right, lower_inv, panel_l, sliced=True))
    known = swap(level_step(2, PR, 0, table, known, right, lower_inv, panel_l, sliced=True))
    split = known.reshape(2, PC, RB, HS, W).transpose(1, 0, 2, 3, 4)
    columns = lax.all_to_all(split, "pcol", 0, 0)
    sums = lax.all_to_all(across(table, columns, lower_blocks), "pcol", 0, 0)
    step = lambda level, copies, *turn: level_step(
        level, copies, 0, table, known, right, lower_inv, panel_l, *turn, sliced=True, less=sums
    )
    for level in range(3, LEVELS - 1):
        known = swap(step(level, PR))
    state, forward = step(LEVELS - 1, PR, upper_inv)
    known = swap(state)
    for level in range(LEVELS - 2, 0, -1):
        known = swap(level_step(level, PR, 1, table, known, forward, upper_inv, panel_u))
    state = level_step(0, PC, 1, table, known, forward, upper_inv, panel_u, both=True)
    full = lax.all_to_all(state, "pcol", 0, 0)
    shape = rhs.shape
    whole = lambda x: x.transpose(1, 0, 2, 3).reshape(shape)
    args = (rhs, lower, upper, lower_inverse, upper_inverse, pattern, levels, widths)
    done = lax.while_loop(
        lambda c: c[2] > 0,
        lambda c: general(*args) + (jnp.int32(0),),
        (whole(full[:, 0]), whole(full[:, 1]), table[COUNTS, 3]),
    )
    return done[0], done[1]


def solution(mesh):
    in_specs = (
        P(None, "prow", None, None),
        P(None, "prow", None, "pcol", None, None),
        P(None, "prow", None, "pcol", None, None),
        P(None, "prow", None, None),
        P(None, "prow", None, None),
        P(),
        P(),
        P(),
    )
    out_specs = (P(None, "prow", None, None), P(None, "prow", None, None))
    return jax.shard_map(local, mesh=mesh, in_specs=in_specs, out_specs=out_specs, check_vma=False)
```

```python
import jax
import jax.numpy as jnp
from jax import lax
from jax.experimental import pallas as pl
from jax.experimental.pallas import tpu as pltpu
from jax.sharding import PartitionSpec as P

LEVELS = 6
W = 128
NRHS = 64
NB = 128
RB = 8
CB = 16
PR = 16
PC = 8
HS = NRHS // PC
CAP_L = 10
CAP_U = 28
LIST = 64
GROUP = 4
HBM = pl.BlockSpec(memory_space=pl.ANY)
ROOM = 52 * 1024 * 1024
SMEM = pl.BlockSpec(memory_space=pltpu.SMEM)
VMEM = pl.BlockSpec(memory_space=pltpu.VMEM)
WIDTH = 0
LIST_L, LIST_U, LIST_T, PACK_L, PACK_U, COUNTS, ROWS, STARTS = range(8, 16)
HALF = 16


def spread(value, axis, source):
    kept = jnp.where(lax.axis_index(axis) == source, value, 0).astype(value.dtype)
    return lax.psum(kept, axis)


def apply_inverse(inverse, right):
    return jnp.einsum("akl,ahl->ahk", inverse, right, precision=lax.Precision.HIGHEST)


def solve_levels(blocks, inverse, right, valid, row_levels, mask, rising):
    prow_count = lax.axis_size("prow")
    pcol_count = lax.axis_size("pcol")
    column = lax.axis_index("pcol")
    ratio = prow_count // pcol_count
    masked = blocks * mask[:, :, None, None]
    row_state = jnp.zeros(right.shape, jnp.float32)
    col_state = jnp.zeros((masked.shape[1],) + right.shape[1:], jnp.float32)
    order = list(range(LEVELS)) if rising else list(range(LEVELS - 1, -1, -1))
    for place, level in enumerate(order):
        partial_sum = jnp.einsum(
            "ackl,chl->ahk", masked, col_state, precision=lax.Precision.HIGHEST
        )
        total = lax.psum(partial_sum, "pcol")
        fresh = apply_inverse(inverse, right - total) * valid
        current = (row_levels == level)[:, None, None]
        row_state = jnp.where(current, fresh, row_state)
        if place + 1 < LEVELS:
            pieces = []
            for offset in range(ratio):
                pieces.append(spread(row_state, "prow", column + offset * pcol_count))
            stacked = jnp.stack(pieces, axis=1)
            col_state = stacked.reshape((-1,) + right.shape[1:])
    return row_state


def general(rhs, lower, upper, lower_inverse, upper_inverse, pattern, levels, widths):
    prow_count = lax.axis_size("prow")
    pcol_count = lax.axis_size("pcol")
    row_index = lax.axis_index("prow")
    col_index = lax.axis_index("pcol")
    row_blocks = rhs.shape[0]
    col_blocks = lower.shape[2]
    width = rhs.shape[3]
    right = rhs.reshape(row_blocks, rhs.shape[2], width)
    lower_local = lower.reshape(row_blocks, col_blocks, width, width)
    upper_local = upper.reshape(row_blocks, col_blocks, width, width)
    lower_inv = lower_inverse.reshape(row_blocks, width, width)
    upper_inv = upper_inverse.reshape(row_blocks, width, width)
    row_levels = lax.dynamic_index_in_dim(
        levels.reshape(row_blocks, prow_count), row_index, 1, keepdims=False
    )
    col_levels = lax.dynamic_index_in_dim(
        levels.reshape(col_blocks, pcol_count), col_index, 1, keepdims=False
    )
    row_widths = lax.dynamic_index_in_dim(
        widths.reshape(row_blocks, prow_count), row_index, 1, keepdims=False
    )
    grid = pattern.reshape(row_blocks, prow_count, col_blocks, pcol_count)
    grid = lax.dynamic_index_in_dim(grid, row_index, 1, keepdims=False)
    grid = lax.dynamic_index_in_dim(grid, col_index, 2, keepdims=False).astype(jnp.float32)
    valid = (jnp.arange(width)[None, :] < row_widths[:, None]).astype(jnp.float32)[:, None, :]
    below = grid * (col_levels[None, :] < row_levels[:, None]).astype(jnp.float32)
    above = grid * (col_levels[None, :] > row_levels[:, None]).astype(jnp.float32)
    forward = solve_levels(lower_local, lower_inv, right, valid, row_levels, below, True)
    solution = solve_levels(upper_local, upper_inv, forward, valid, row_levels, above, False)
    shape = rhs.shape
    return (forward.reshape(shape), solution.reshape(shape))


def dot3(x, w):
    m, n = x.shape[0], w.shape[0]
    xh = x.astype(jnp.bfloat16).astype(jnp.float32)
    xs = jnp.concatenate([xh, x - xh], axis=0).astype(jnp.bfloat16)
    wh = w.astype(jnp.bfloat16)
    wl = (w - wh.astype(jnp.float32)).astype(jnp.bfloat16)
    ws = jnp.concatenate([wh, wl], axis=0)
    y = lax.dot_general(xs, ws, (((1,), (1,)), ((), ())), preferred_element_type=jnp.float32)
    return (y[m:, n:] + y[:m, n:]) + (y[m:, :n] + y[:m, :n])


def iota(shape, dim):
    return lax.broadcasted_iota(jnp.int32, shape, dim)


def cost(mib):
    return pl.CostEstimate(flops=0, bytes_accessed=mib << 20, transcendentals=0)


def flag(cond):
    return jnp.where(cond, 1.0, 0.0)


def table_kernel(pattern, levels, widths, out):
    p = lax.axis_index("prow")
    q = lax.axis_index("pcol")
    lev = levels[...].astype(jnp.float32)
    wid = widths[...].astype(jnp.float32)
    i = iota((NB, NB), 0)
    j = iota((NB, NB), 1)
    lev_col = jnp.sum(jnp.where(i == j, lev, 0.0), axis=1, keepdims=True)
    linked = flag(pattern[...] > 0)
    low = linked * flag(lev < lev_col)
    high = linked * flag(lev > lev_col)
    near = low * flag((lev_col < 2.5) | (lev > 2.5))
    far = low - near
    same = flag((i & (PC - 1)) == (j & (PC - 1)))
    ahead = flag(i < j)
    same_ahead = same * ahead

    def dot(x, y):
        return jnp.dot(x, y, preferred_element_type=jnp.float32)

    by_row = flag((iota((PR, NB), 1) & (PR - 1)) == iota((PR, NB), 0))

    def over(full, cap):
        rows = dot(by_row, full)
        most = jnp.max(jnp.max(dot(rows, same), axis=1, keepdims=True), axis=0, keepdims=True)
        listed = jnp.max(jnp.sum(rows, axis=1, keepdims=True), axis=0, keepdims=True)
        return flag((most > cap) | (listed > LIST))

    full = jnp.maximum(over(near, CAP_L), over(high, CAP_U))

    lane = iota((RB, NB), 1)
    sub = iota((RB, NB), 0)
    mine = flag(lane == sub * PR + p)
    row_lev = jnp.sum(mine * lev, axis=1, keepdims=True)
    row_wid = jnp.sum(mine * wid, axis=1, keepdims=True)
    col = lane & (PC - 1)
    own = flag(col == q)
    node = lane.astype(jnp.float32)
    spot = (sub * CB + (lane >> 3)).astype(jnp.float32)

    def ranks(sel):
        total = jnp.zeros((1, NB), jnp.float32)
        rows = []
        for a in range(RB):
            rows.append(total)
            total = total + sel[a : a + 1]
        return dot(jnp.concatenate(rows, axis=0), same) + dot(sel, same_ahead)

    def ordered():
        start = jnp.zeros((RB, 1), jnp.float32)
        below = jnp.zeros((1, NB), jnp.float32)
        index = iota((RB, 1), 0)
        for a in range(RB):
            first = (row_lev[a : a + 1] < row_lev) | ((row_lev[a : a + 1] == row_lev) & (index > a))
            start = start + flag(first)
            below = below + flag(row_lev[a : a + 1] < node[:1])
        return start, below

    def listing(sel, place, value, size):
        t = iota((size, NB), 0).astype(jnp.float32)
        held = jnp.zeros((size, NB), jnp.float32)
        for a in range(RB):
            hit = flag(t == place[a : a + 1]) * sel[a : a + 1]
            held = held + hit * value[a : a + 1]
        ones = jnp.ones((RB, NB), jnp.float32)
        row = lax.dot_general(ones, held, (((1,), (1,)), ((), ())), preferred_element_type=jnp.float32)[:1]
        if size < NB:
            row = jnp.concatenate([row, jnp.zeros((1, NB - size), jnp.float32)], axis=1)
        return row

    def count(sel):
        return jnp.sum(jnp.sum(sel, axis=1, keepdims=True), axis=0, keepdims=True)

    def by_step(sel, step):
        parts = jnp.concatenate([sel * flag(step == k) for k in range(LEVELS)], axis=0)
        size = RB * LEVELS
        earlier = flag(iota((size, size), 0) > iota((size, size), 1))
        base = jnp.sum(dot(earlier, parts), axis=1, keepdims=True)
        spread = parts * (dot(parts, ahead) + base)
        place = jnp.zeros((RB, NB), jnp.float32)
        below = jnp.zeros((1, NB), jnp.float32)
        for k in range(LEVELS):
            place = place + spread[RB * k : RB * (k + 1)]
            below = below + flag(node[:1] == k) * base[RB * k : RB * k + 1]
        return place, below + flag(node[:1] == LEVELS) * count(sel)

    def panel(sel, cap, step):
        rank = ranks(sel)
        place, below = by_step(sel, step)
        slot = (col * cap).astype(jnp.float32) + jnp.minimum(rank, cap - 1.0)
        listed = listing(sel, place, slot, LIST) * (NB * RB) + listing(sel, place, node, LIST) * RB
        listed = listed + listing(sel, place, sub.astype(jnp.float32), LIST)
        packed = listing(sel * own, rank, spot, 32)
        return jnp.minimum(below, LIST), listed, packed, jnp.minimum(count(sel * own), cap)

    near_p = dot(mine, near)
    high_p = dot(mine, high)
    far_p = dot(mine, far)
    top = jnp.where(row_lev > 2.5, row_lev, jnp.where(row_lev > 0.5, 4.0, 3.0))
    fourth = jnp.minimum(jnp.maximum(row_lev, 2.0), 3.0)
    third = jnp.minimum(jnp.maximum(row_lev, 1.0), 2.0)
    down = jnp.where(lev > 4.5, top, jnp.where(lev > 3.5, fourth, jnp.where(lev > 2.5, third, row_lev)))
    below_l, list_l, pack_l, count_l = panel(near_p, CAP_L, row_lev + 0.0 * node)
    below_u, list_u, pack_u, count_u = panel(high_p, CAP_U, down)
    list_t = listing(far_p * own, ranks(far_p), spot, NB)
    count_t = count(far_p * own)
    rows = flag(lane == WIDTH) * row_wid
    counts = jnp.zeros((1, NB), jnp.float32)
    for k, value in enumerate([count_l, count_u, count_t, full]):
        counts = counts + flag(lane[:1] == k) * value
    spot_of, below_r = ordered()
    order = jnp.zeros((1, NB), jnp.float32)
    for a in range(RB):
        order = order + flag(spot_of[a : a + 1] == node[:1]) * a

    def beside(x, y):
        return jnp.concatenate([x[:, :HALF], y[:, :HALF], jnp.zeros((1, NB - 2 * HALF), jnp.float32)], axis=1)

    order = beside(order, below_r)
    starts = beside(below_l, below_u)
    lists = jnp.concatenate([list_l, list_u, list_t, pack_l, pack_u, counts, order, starts], axis=0)
    out[0:8, :] = rows.astype(jnp.int32)
    out[8:16, :] = lists.astype(jnp.int32)


def tables(pattern, levels, widths):
    return pl.pallas_call(
        table_kernel,
        out_shape=jax.ShapeDtypeStruct((16, NB), jnp.int32),
        in_specs=[VMEM, VMEM, VMEM],
        out_specs=VMEM,
        cost_estimate=cost(4),
    )(pattern, levels.reshape(1, NB), widths.reshape(1, NB))


def pack_kernel(where, cap, table, blocks, _, out, token, held, sems_in, sems_out):
    count = table[COUNTS, where]
    row = PACK_L + where

    def load(t):
        n = table[row, t]
        return pltpu.make_async_copy(blocks.at[n >> 4, n & (CB - 1)], held.at[t], sems_in.at[t])

    def store(t):
        return pltpu.make_async_copy(held.at[t], out.at[t], sems_out.at[t])

    pl.loop(0, count)(lambda t: load(t).start())
    token[...] = jnp.zeros_like(token)

    @pl.loop(0, count)
    def _(t):
        load(t).wait()
        store(t).start()

    pl.loop(0, count)(lambda t: store(t).wait())


def pack(where, cap, table, blocks, after):
    return pl.pallas_call(
        lambda *refs: pack_kernel(where, cap, *refs),
        out_shape=(
            jax.ShapeDtypeStruct((cap, W, W), jnp.float32),
            jax.ShapeDtypeStruct((HS, W), jnp.float32),
        ),
        in_specs=[SMEM, HBM, HBM],
        out_specs=(HBM, VMEM),
        scratch_shapes=[
            pltpu.VMEM((cap, W, W), jnp.float32),
            pltpu.SemaphoreType.DMA((cap,)),
            pltpu.SemaphoreType.DMA((cap,)),
        ],
        cost_estimate=cost(4),
    )(table, blocks, after)


def level_kernel(level, copies, kind, turn, both, sliced, group, table, known, right, inverse, panel, less, *rest):
    if turn:
        inverse_2, out, out_2, sums, blocks, inv, inv_2, sems, isems = rest
    else:
        out, sums, blocks, inv, sems, isems = rest
    p = lax.axis_index("prow")
    row = LIST_U if kind else LIST_L
    e0, e1 = table[STARTS, kind * HALF + level], table[STARTS, kind * HALF + level + 1]
    r0, r1 = table[ROWS, HALF + level], table[ROWS, HALF + level + 1]

    def copy(t):
        return pltpu.make_async_copy(panel.at[table[row, t] >> 10], blocks.at[t], sems.at[t])

    def icopy(a):
        return pltpu.make_async_copy(inverse.at[a], inv.at[a], isems.at[a])

    def icopy_2(a):
        return pltpu.make_async_copy(inverse_2.at[a], inv_2.at[a], isems.at[RB + a])

    if panel is not None:
        pl.loop(e0, e1)(lambda t: copy(t).start())

    @pl.loop(r0, r1)
    def _(r):
        icopy(table[ROWS, r]).start()
        if turn:
            icopy_2(table[ROWS, r]).start()

    shift = lax.axis_index("pcol") * HS
    for a in range(RB):
        mine = right[a, pl.ds(shift, HS)] if sliced else right[a]
        if less is not None and not both:
            parts = [less[k, a] for k in range(PC)]
            while len(parts) > 1:
                parts = [x + y for x, y in zip(parts[::2], parts[1::2])]
            mine = mine - parts[0]
        sums[a] = mine
        old = known[p, a] if known is not None else jnp.zeros((HS, W), jnp.float32)
        for r in range(copies):
            if both:
                out[r, 0, a] = less[a]
                out[r, 1, a] = old
            else:
                out[r, a] = old if not turn else jnp.zeros((HS, W), jnp.float32)
        if turn:
            out_2[a] = old

    if panel is not None:
        @pl.loop(0, (e1 - e0 + group - 1) // group)
        def _(g):
            terms = []
            for u in range(group):
                t = e0 + g * group + u
                there = t < e1

                @pl.when(there)
                def _():
                    copy(t).wait()

                t = jnp.minimum(t, e1 - 1)
                node = (table[row, t] >> 3) & (NB - 1)
                x = known[node & (PR - 1), node >> 4] * jnp.where(there, 1.0, 0.0)
                terms.append((table[row, t] & (RB - 1), dot3(x, blocks[t])))
            for a, term in terms:
                sums[a] -= term

    lane = iota((HS, W), 1)

    @pl.loop(0, (r1 - r0 + GROUP - 1) >> 2)
    def _(g):
        fresh = []
        for u in range(GROUP):
            r = r0 + g * GROUP + u
            there = r < r1
            a = table[ROWS, jnp.minimum(r, r1 - 1)]

            @pl.when(there)
            def _():
                icopy(a).wait()
                if turn:
                    icopy_2(a).wait()

            fresh.append((there, a, jnp.where(lane < table[a, WIDTH], dot3(sums[a], inv[a]), 0.0)))
        if turn:
            later = [jnp.where(lane < table[a, WIDTH], dot3(x, inv_2[a]), 0.0) for _, a, x in fresh]
            for there, a, x in fresh:
                out_2[a] = x
            fresh = [(there, a, x) for (there, a, _), x in zip(fresh, later)]
        for there, a, x in fresh:
            @pl.when(there)
            def _():
                for r in range(copies):
                    if both:
                        out[r, 1, a] = x
                    else:
                        out[r, a] = x


def level_step(level, copies, kind, table, known, right, inverse, panel, turn=None, both=False, sliced=False, after=None, less=None, group=GROUP):
    ins, specs = [table], [SMEM]
    for x, spec in ((known, VMEM), (right, VMEM), (inverse, HBM)):
        if x is not None:
            ins.append(x)
            specs.append(spec)
    if panel is not None:
        ins.append(panel)
        specs.append(HBM)
    if less is not None:
        ins.append(less)
        specs.append(VMEM)
    if turn is not None:
        ins.append(turn)
        specs.append(HBM)
    if after is not None:
        ins.append(after)
        specs.append(HBM)

    def kernel(*refs):
        refs = list(refs)
        if after is not None:
            refs.pop(len(ins) - 1)
        given = [refs.pop(0)]
        given.append(refs.pop(0) if known is not None else None)
        given += [refs.pop(0), refs.pop(0)]
        given.append(refs.pop(0) if panel is not None else None)
        given.append(refs.pop(0) if less is not None else None)
        level_kernel(level, copies, kind, turn is not None, both, sliced, group, *given, *refs)

    shape = (copies, 2, RB, HS, W) if both else (copies, RB, HS, W)
    out_shape = [jax.ShapeDtypeStruct(shape, jnp.float32)]
    carry = kind == 1 and not both
    sums = [] if carry else [pltpu.VMEM((RB, HS, W), jnp.float32)]
    if carry:
        out_shape.append(jax.ShapeDtypeStruct((RB, HS, W), jnp.float32))
    scratch = sums + [pltpu.VMEM((LIST, W, W), jnp.float32), pltpu.VMEM((RB, W, W), jnp.float32)]
    if turn is not None:
        out_shape.append(jax.ShapeDtypeStruct((RB, HS, W), jnp.float32))
        scratch.append(pltpu.VMEM((RB, W, W), jnp.float32))
    scratch += [pltpu.SemaphoreType.DMA((LIST,)), pltpu.SemaphoreType.DMA((2 * RB,))]
    out = pl.pallas_call(
        kernel,
        out_shape=out_shape,
        in_specs=specs,
        out_specs=[VMEM] * len(out_shape),
        scratch_shapes=scratch,
        compiler_params=pltpu.CompilerParams(vmem_limit_bytes=ROOM),
        cost_estimate=cost(8),
    )(*ins)
    return out if len(out) > 1 else out[0]


def across_kernel(table, known, lower, out, blocks, sems):
    count = table[COUNTS, 2]

    def copy(t):
        n = table[LIST_T, t]
        return pltpu.make_async_copy(lower.at[n >> 4, n & (CB - 1)], blocks.at[t], sems.at[t])

    pl.loop(0, count)(lambda t: copy(t).start())
    out[...] = jnp.zeros_like(out)

    @pl.loop(0, (count + GROUP - 1) >> 2)
    def _(g):
        terms = []
        for u in range(GROUP):
            t = g * GROUP + u
            there = t < count

            @pl.when(there)
            def _():
                copy(t).wait()

            t = jnp.minimum(t, count - 1)
            n = table[LIST_T, t]
            c = n & (CB - 1)
            x = known[:, c & 1, c >> 1].reshape(NRHS, W) * jnp.where(there, 1.0, 0.0)
            terms.append((n >> 4, dot3(x, blocks[t]).reshape(PC, HS, W)))
        for a, term in terms:
            out[:, a] += term


def across(table, known, lower):
    return pl.pallas_call(
        across_kernel,
        out_shape=jax.ShapeDtypeStruct((PC, RB, HS, W), jnp.float32),
        in_specs=[SMEM, VMEM, HBM],
        out_specs=VMEM,
        scratch_shapes=[pltpu.VMEM((NB, W, W), jnp.float32), pltpu.SemaphoreType.DMA((NB,))],
        compiler_params=pltpu.CompilerParams(vmem_limit_bytes=ROOM),
        cost_estimate=cost(8),
    )(table, known, lower)


def local(rhs, lower, upper, lower_inverse, upper_inverse, pattern, levels, widths):
    right = rhs.reshape(RB, NRHS, W)
    lower_blocks = lower.reshape(RB, CB, W, W)
    upper_blocks = upper.reshape(RB, CB, W, W)
    lower_inv = lower_inverse.reshape(RB, W, W)
    upper_inv = upper_inverse.reshape(RB, W, W)
    table = tables(pattern, levels, widths)
    swap = lambda x: lax.all_to_all(x, "prow", 0, 0)

    packed_l, token = pack(0, CAP_L, table, lower_blocks, table)
    panel_l = lax.all_gather(packed_l, "pcol", tiled=True)
    leaves = level_step(0, PR, 0, table, None, right, lower_inv, None, sliced=True, after=token)
    known = swap(leaves)
    packed_u, _ = pack(1, CAP_U, table, upper_blocks, known[0, 0])
    panel_u = lax.all_gather(packed_u, "pcol", tiled=True)
    known = swap(level_step(1, PR, 0, table, known, right, lower_inv, panel_l, sliced=True, group=8))
    known = swap(level_step(2, PR, 0, table, known, right, lower_inv, panel_l, sliced=True, group=8))
    split = known.reshape(2, PC, RB, HS, W).transpose(1, 0, 2, 3, 4)
    columns = lax.all_to_all(split, "pcol", 0, 0)
    sums = lax.all_to_all(across(table, columns, lower_blocks), "pcol", 0, 0)
    step = lambda level, copies, *turn: level_step(
        level, copies, 0, table, known, right, lower_inv, panel_l, *turn, sliced=True, less=sums
    )
    for level in range(3, LEVELS - 1):
        known = swap(step(level, PR))
    state, forward = step(LEVELS - 1, PR, upper_inv)
    known = swap(state)
    left = forward
    for level in range(LEVELS - 2, 0, -1):
        state, left = level_step(level, PR, 1, table, known, left, upper_inv, panel_u, group=8)
        known = swap(state)
    state = level_step(0, PC, 1, table, known, left, upper_inv, panel_u, both=True, less=forward, group=8)
    full = lax.all_to_all(state, "pcol", 0, 0)
    shape = rhs.shape
    whole = lambda x: x.transpose(1, 0, 2, 3).reshape(shape)
    args = (rhs, lower, upper, lower_inverse, upper_inverse, pattern, levels, widths)
    done = lax.while_loop(
        lambda c: c[2] > 0,
        lambda c: general(*args) + (jnp.int32(0),),
        (whole(full[:, 0]), whole(full[:, 1]), table[COUNTS, 3]),
    )
    return done[0], done[1]


def solution(mesh):
    in_specs = (
        P(None, "prow", None, None),
        P(None, "prow", None, "pcol", None, None),
        P(None, "prow", None, "pcol", None, None),
        P(None, "prow", None, None),
        P(None, "prow", None, None),
        P(),
        P(),
        P(),
    )
    out_specs = (P(None, "prow", None, None), P(None, "prow", None, None))
    return jax.shard_map(local, mesh=mesh, in_specs=in_specs, out_specs=out_specs, check_vma=False)
```

```python
import jax
import jax.numpy as jnp
from jax import lax
from jax.experimental import pallas as pl
from jax.experimental.pallas import tpu as pltpu
from jax.sharding import PartitionSpec as P

LEVELS = 6
W = 128
NRHS = 64
NB = 128
RB = 8
CB = 16
PR = 16
PC = 8
HS = NRHS // PC
CAP_L = 10
CAP_U = 28
LIST = 64
GROUP = 4
HBM = pl.BlockSpec(memory_space=pl.ANY)
ROOM = 44 * 1024 * 1024
SMEM = pl.BlockSpec(memory_space=pltpu.SMEM)
VMEM = pl.BlockSpec(memory_space=pltpu.VMEM)
WIDTH = 0
LIST_L, LIST_U, LIST_T, PACK_L, PACK_U, COUNTS, ROWS, STARTS = range(8, 16)
HALF = 16


def spread(value, axis, source):
    kept = jnp.where(lax.axis_index(axis) == source, value, 0).astype(value.dtype)
    return lax.psum(kept, axis)


def apply_inverse(inverse, right):
    return jnp.einsum("akl,ahl->ahk", inverse, right, precision=lax.Precision.HIGHEST)


def solve_levels(blocks, inverse, right, valid, row_levels, mask, rising):
    prow_count = lax.axis_size("prow")
    pcol_count = lax.axis_size("pcol")
    column = lax.axis_index("pcol")
    ratio = prow_count // pcol_count
    masked = blocks * mask[:, :, None, None]
    row_state = jnp.zeros(right.shape, jnp.float32)
    col_state = jnp.zeros((masked.shape[1],) + right.shape[1:], jnp.float32)
    order = list(range(LEVELS)) if rising else list(range(LEVELS - 1, -1, -1))
    for place, level in enumerate(order):
        partial_sum = jnp.einsum(
            "ackl,chl->ahk", masked, col_state, precision=lax.Precision.HIGHEST
        )
        total = lax.psum(partial_sum, "pcol")
        fresh = apply_inverse(inverse, right - total) * valid
        current = (row_levels == level)[:, None, None]
        row_state = jnp.where(current, fresh, row_state)
        if place + 1 < LEVELS:
            pieces = []
            for offset in range(ratio):
                pieces.append(spread(row_state, "prow", column + offset * pcol_count))
            stacked = jnp.stack(pieces, axis=1)
            col_state = stacked.reshape((-1,) + right.shape[1:])
    return row_state


def general(rhs, lower, upper, lower_inverse, upper_inverse, pattern, levels, widths):
    prow_count = lax.axis_size("prow")
    pcol_count = lax.axis_size("pcol")
    row_index = lax.axis_index("prow")
    col_index = lax.axis_index("pcol")
    row_blocks = rhs.shape[0]
    col_blocks = lower.shape[2]
    width = rhs.shape[3]
    right = rhs.reshape(row_blocks, rhs.shape[2], width)
    lower_local = lower.reshape(row_blocks, col_blocks, width, width)
    upper_local = upper.reshape(row_blocks, col_blocks, width, width)
    lower_inv = lower_inverse.reshape(row_blocks, width, width)
    upper_inv = upper_inverse.reshape(row_blocks, width, width)
    row_levels = lax.dynamic_index_in_dim(
        levels.reshape(row_blocks, prow_count), row_index, 1, keepdims=False
    )
    col_levels = lax.dynamic_index_in_dim(
        levels.reshape(col_blocks, pcol_count), col_index, 1, keepdims=False
    )
    row_widths = lax.dynamic_index_in_dim(
        widths.reshape(row_blocks, prow_count), row_index, 1, keepdims=False
    )
    grid = pattern.reshape(row_blocks, prow_count, col_blocks, pcol_count)
    grid = lax.dynamic_index_in_dim(grid, row_index, 1, keepdims=False)
    grid = lax.dynamic_index_in_dim(grid, col_index, 2, keepdims=False).astype(jnp.float32)
    valid = (jnp.arange(width)[None, :] < row_widths[:, None]).astype(jnp.float32)[:, None, :]
    below = grid * (col_levels[None, :] < row_levels[:, None]).astype(jnp.float32)
    above = grid * (col_levels[None, :] > row_levels[:, None]).astype(jnp.float32)
    forward = solve_levels(lower_local, lower_inv, right, valid, row_levels, below, True)
    solution = solve_levels(upper_local, upper_inv, forward, valid, row_levels, above, False)
    shape = rhs.shape
    return (forward.reshape(shape), solution.reshape(shape))


def dot3(x, w):
    m, n = x.shape[0], w.shape[0]
    xh = x.astype(jnp.bfloat16).astype(jnp.float32)
    xs = jnp.concatenate([xh, x - xh], axis=0).astype(jnp.bfloat16)
    wh = w.astype(jnp.bfloat16)
    wl = (w - wh.astype(jnp.float32)).astype(jnp.bfloat16)
    ws = jnp.concatenate([wh, wl], axis=0)
    y = lax.dot_general(xs, ws, (((1,), (1,)), ((), ())), preferred_element_type=jnp.float32)
    return (y[m:, n:] + y[:m, n:]) + (y[m:, :n] + y[:m, :n])


def iota(shape, dim):
    return lax.broadcasted_iota(jnp.int32, shape, dim)


def cost(mib):
    return pl.CostEstimate(flops=0, bytes_accessed=mib << 20, transcendentals=0)


def flag(cond):
    return jnp.where(cond, 1.0, 0.0)


def table_kernel(pattern, levels, widths, out):
    p = lax.axis_index("prow")
    q = lax.axis_index("pcol")
    lev = levels[...].astype(jnp.float32)
    wid = widths[...].astype(jnp.float32)
    i = iota((NB, NB), 0)
    j = iota((NB, NB), 1)
    lev_col = jnp.sum(jnp.where(i == j, lev, 0.0), axis=1, keepdims=True)
    linked = flag(pattern[...] > 0)
    low = linked * flag(lev < lev_col)
    high = linked * flag(lev > lev_col)
    near = low * flag((lev_col < 2.5) | (lev > 2.5))
    far = low - near
    same = flag((i & (PC - 1)) == (j & (PC - 1)))
    ahead = flag(i < j)
    same_ahead = same * ahead

    def dot(x, y):
        return jnp.dot(x, y, preferred_element_type=jnp.float32)

    by_row = flag((iota((PR, NB), 1) & (PR - 1)) == iota((PR, NB), 0))

    def over(full, cap):
        rows = dot(by_row, full)
        most = jnp.max(jnp.max(dot(rows, same), axis=1, keepdims=True), axis=0, keepdims=True)
        listed = jnp.max(jnp.sum(rows, axis=1, keepdims=True), axis=0, keepdims=True)
        return flag((most > cap) | (listed > LIST))

    def over_far():
        rows = dot(dot(by_row, far), same)
        return flag(jnp.max(jnp.max(rows, axis=1, keepdims=True), axis=0, keepdims=True) > LIST)

    full = jnp.maximum(jnp.maximum(over(near, CAP_L), over(high, CAP_U)), over_far())

    lane = iota((RB, NB), 1)
    sub = iota((RB, NB), 0)
    mine = flag(lane == sub * PR + p)
    row_lev = jnp.sum(mine * lev, axis=1, keepdims=True)
    row_wid = jnp.sum(mine * wid, axis=1, keepdims=True)
    col = lane & (PC - 1)
    own = flag(col == q)
    node = lane.astype(jnp.float32)
    spot = (sub * CB + (lane >> 3)).astype(jnp.float32)

    def ranks(sel):
        total = jnp.zeros((1, NB), jnp.float32)
        rows = []
        for a in range(RB):
            rows.append(total)
            total = total + sel[a : a + 1]
        return dot(jnp.concatenate(rows, axis=0), same) + dot(sel, same_ahead)

    def ordered():
        start = jnp.zeros((RB, 1), jnp.float32)
        below = jnp.zeros((1, NB), jnp.float32)
        index = iota((RB, 1), 0)
        for a in range(RB):
            first = (row_lev[a : a + 1] < row_lev) | ((row_lev[a : a + 1] == row_lev) & (index > a))
            start = start + flag(first)
            below = below + flag(row_lev[a : a + 1] < node[:1])
        return start, below

    def listing(sel, place, value, size):
        t = iota((size, NB), 0).astype(jnp.float32)
        held = jnp.zeros((size, NB), jnp.float32)
        for a in range(RB):
            hit = flag(t == place[a : a + 1]) * sel[a : a + 1]
            held = held + hit * value[a : a + 1]
        ones = jnp.ones((RB, NB), jnp.float32)
        row = lax.dot_general(ones, held, (((1,), (1,)), ((), ())), preferred_element_type=jnp.float32)[:1]
        if size < NB:
            row = jnp.concatenate([row, jnp.zeros((1, NB - size), jnp.float32)], axis=1)
        return row

    def count(sel):
        return jnp.sum(jnp.sum(sel, axis=1, keepdims=True), axis=0, keepdims=True)

    def by_step(sel, step):
        parts = jnp.concatenate([sel * flag(step == k) for k in range(LEVELS)], axis=0)
        size = RB * LEVELS
        earlier = flag(iota((size, size), 0) > iota((size, size), 1))
        base = jnp.sum(dot(earlier, parts), axis=1, keepdims=True)
        spread = parts * (dot(parts, ahead) + base)
        place = jnp.zeros((RB, NB), jnp.float32)
        below = jnp.zeros((1, NB), jnp.float32)
        for k in range(LEVELS):
            place = place + spread[RB * k : RB * (k + 1)]
            below = below + flag(node[:1] == k) * base[RB * k : RB * k + 1]
        return place, below + flag(node[:1] == LEVELS) * count(sel)

    def panel(sel, cap, step):
        rank = ranks(sel)
        place, below = by_step(sel, step)
        slot = (col * cap).astype(jnp.float32) + jnp.minimum(rank, cap - 1.0)
        listed = listing(sel, place, slot, LIST) * (NB * RB) + listing(sel, place, node, LIST) * RB
        listed = listed + listing(sel, place, sub.astype(jnp.float32), LIST)
        packed = listing(sel * own, rank, spot, 32)
        return jnp.minimum(below, LIST), listed, packed, jnp.minimum(count(sel * own), cap)

    near_p = dot(mine, near)
    high_p = dot(mine, high)
    far_p = dot(mine, far)
    top = jnp.where(row_lev > 2.5, row_lev, jnp.where(row_lev > 0.5, 4.0, 3.0))
    fourth = jnp.minimum(jnp.maximum(row_lev, 2.0), 3.0)
    third = jnp.minimum(jnp.maximum(row_lev, 1.0), 2.0)
    down = jnp.where(lev > 4.5, top, jnp.where(lev > 3.5, fourth, jnp.where(lev > 2.5, third, row_lev)))
    below_l, list_l, pack_l, count_l = panel(near_p, CAP_L, row_lev + 0.0 * node)
    below_u, list_u, pack_u, count_u = panel(high_p, CAP_U, down)
    list_t = listing(far_p * own, ranks(far_p), spot, NB)
    count_t = jnp.minimum(count(far_p * own), LIST)
    rows = flag(lane == WIDTH) * row_wid
    counts = jnp.zeros((1, NB), jnp.float32)
    for k, value in enumerate([count_l, count_u, count_t, full]):
        counts = counts + flag(lane[:1] == k) * value
    spot_of, below_r = ordered()
    order = jnp.zeros((1, NB), jnp.float32)
    for a in range(RB):
        order = order + flag(spot_of[a : a + 1] == node[:1]) * a

    def beside(x, y):
        return jnp.concatenate([x[:, :HALF], y[:, :HALF], jnp.zeros((1, NB - 2 * HALF), jnp.float32)], axis=1)

    order = beside(order, below_r)
    starts = beside(below_l, below_u)
    lists = jnp.concatenate([list_l, list_u, list_t, pack_l, pack_u, counts, order, starts], axis=0)
    out[0:8, :] = rows.astype(jnp.int32)
    out[8:16, :] = lists.astype(jnp.int32)


def tables(pattern, levels, widths):
    return pl.pallas_call(
        table_kernel,
        out_shape=jax.ShapeDtypeStruct((16, NB), jnp.int32),
        in_specs=[VMEM, VMEM, VMEM],
        out_specs=VMEM,
        cost_estimate=cost(4),
    )(pattern, levels.reshape(1, NB), widths.reshape(1, NB))


def pack_kernel(where, cap, with_far, table, blocks, _, *rest):
    rest = list(rest)
    lower = rest.pop(0) if with_far else None
    out, extra, held, sems_in, sems_out = rest[:5]
    count = table[COUNTS, where]
    row = PACK_L + where

    def load(t):
        n = table[row, t]
        return pltpu.make_async_copy(blocks.at[n >> 4, n & (CB - 1)], held.at[t], sems_in.at[t])

    def store(t):
        return pltpu.make_async_copy(held.at[t], out.at[t], sems_out.at[t])

    def load_far(t):
        n = table[LIST_T, t]
        return pltpu.make_async_copy(lower.at[n >> 4, n & (CB - 1)], extra.at[t], rest[5].at[t])

    pl.loop(0, count)(lambda t: load(t).start())
    if with_far:
        pl.loop(0, table[COUNTS, 2])(lambda t: load_far(t).start())
    else:
        extra[...] = jnp.zeros_like(extra)

    @pl.loop(0, count)
    def _(t):
        load(t).wait()
        store(t).start()

    pl.loop(0, count)(lambda t: store(t).wait())
    if with_far:
        pl.loop(0, table[COUNTS, 2])(lambda t: load_far(t).wait())


def pack(where, cap, table, blocks, after, lower=None):
    with_far = lower is not None
    extra = (LIST, W, W) if with_far else (HS, W)
    scratch = [
        pltpu.VMEM((cap, W, W), jnp.float32),
        pltpu.SemaphoreType.DMA((cap,)),
        pltpu.SemaphoreType.DMA((cap,)),
    ]
    if with_far:
        scratch.append(pltpu.SemaphoreType.DMA((LIST,)))
    return pl.pallas_call(
        lambda *refs: pack_kernel(where, cap, with_far, *refs),
        out_shape=(
            jax.ShapeDtypeStruct((cap, W, W), jnp.float32),
            jax.ShapeDtypeStruct(extra, jnp.float32),
        ),
        in_specs=[SMEM, HBM, HBM] + ([HBM] if with_far else []),
        out_specs=(HBM, VMEM),
        scratch_shapes=scratch,
        compiler_params=pltpu.CompilerParams(vmem_limit_bytes=ROOM),
        cost_estimate=cost(4),
    )(table, blocks, after, *([lower] if with_far else []))


def level_kernel(level, copies, kind, turn, both, sliced, group, fetch, table, known, right, inverse, panel, less, *rest):
    rest = list(rest)
    inverse_2 = rest.pop(0) if turn else None
    out = rest.pop(0)
    out_2 = rest.pop(0) if turn else None
    blocks = rest.pop(0) if fetch else panel
    sums = rest.pop(0)
    sems = rest.pop(0) if fetch else None
    p = lax.axis_index("prow")
    row = LIST_U if kind else LIST_L
    e0, e1 = table[STARTS, kind * HALF + level], table[STARTS, kind * HALF + level + 1]
    r0, r1 = table[ROWS, HALF + level], table[ROWS, HALF + level + 1]
    whole = table[STARTS, kind * HALF + LEVELS]

    def copy(t):
        return pltpu.make_async_copy(panel.at[table[row, t] >> 10], blocks.at[t], sems.at[t])

    if fetch:
        pl.loop(e0, e1)(lambda t: copy(t).start())
        pl.loop(0, e0)(lambda t: copy(t).start())
        pl.loop(e1, whole)(lambda t: copy(t).start())

    shift = lax.axis_index("pcol") * HS
    for a in range(RB):
        mine = right[a, pl.ds(shift, HS)] if sliced else right[a]
        if less is not None and not both:
            parts = [less[k, a] for k in range(PC)]
            while len(parts) > 1:
                parts = [x + y for x, y in zip(parts[::2], parts[1::2])]
            mine = mine - parts[0]
        sums[a] = mine
        old = known[p, a] if known is not None else jnp.zeros((HS, W), jnp.float32)
        for r in range(copies):
            if both:
                out[r, 0, a] = less[a]
                out[r, 1, a] = old
            else:
                out[r, a] = old if not turn else jnp.zeros((HS, W), jnp.float32)
        if turn:
            out_2[a] = old

    if panel is not None:
        @pl.loop(0, (e1 - e0 + group - 1) // group)
        def _(g):
            terms = []
            for u in range(group):
                t = e0 + g * group + u
                there = t < e1

                if fetch:
                    @pl.when(there)
                    def _():
                        copy(t).wait()

                t = jnp.minimum(t, e1 - 1)
                node = (table[row, t] >> 3) & (NB - 1)
                x = known[node & (PR - 1), node >> 4] * jnp.where(there, 1.0, 0.0)
                terms.append((table[row, t] & (RB - 1), dot3(x, blocks[t])))
            for a, term in terms:
                sums[a] -= term

    lane = iota((HS, W), 1)

    @pl.loop(0, (r1 - r0 + GROUP - 1) >> 2)
    def _(g):
        fresh = []
        for u in range(GROUP):
            r = r0 + g * GROUP + u
            there = r < r1
            a = table[ROWS, jnp.minimum(r, r1 - 1)]

            fresh.append((there, a, jnp.where(lane < table[a, WIDTH], dot3(sums[a], inverse[a]), 0.0)))
        if turn:
            later = [jnp.where(lane < table[a, WIDTH], dot3(x, inverse_2[a]), 0.0) for _, a, x in fresh]
            for there, a, x in fresh:
                out_2[a] = x
            fresh = [(there, a, x) for (there, a, _), x in zip(fresh, later)]
        for there, a, x in fresh:
            @pl.when(there)
            def _():
                for r in range(copies):
                    if both:
                        out[r, 1, a] = x
                    else:
                        out[r, a] = x

    if fetch:
        pl.loop(0, e0)(lambda t: copy(t).wait())
        pl.loop(e1, whole)(lambda t: copy(t).wait())


def level_step(
    level, copies, kind, table, known, right, inverse, panel, *,
    turn=None, both=False, sliced=False, after=None, less=None, group=GROUP, fetch=False,
):
    ins, specs = [table], [SMEM]
    given = ((known, VMEM), (right, VMEM), (inverse, VMEM), (panel, HBM if fetch else VMEM), (less, VMEM))
    for x, spec in given + ((turn, VMEM), (after, HBM)):
        if x is not None:
            ins.append(x)
            specs.append(spec)

    def kernel(*refs):
        refs = list(refs)
        if after is not None:
            refs.pop(len(ins) - 1)
        args = [refs.pop(0)] + [refs.pop(0) if x is not None else None for x, _ in given]
        level_kernel(level, copies, kind, turn is not None, both, sliced, group, fetch, *args, *refs)

    small = (RB, HS, W)
    shapes = [(copies, 2) + small if both else (copies,) + small]
    if turn is not None:
        shapes.append(small)
    if fetch:
        shapes.append((LIST, W, W))
    scratch = []
    if kind == 1 and not both:
        shapes.append(small)
    else:
        scratch.append(pltpu.VMEM(small, jnp.float32))
    if fetch:
        scratch.append(pltpu.SemaphoreType.DMA((LIST,)))
    out = pl.pallas_call(
        kernel,
        out_shape=[jax.ShapeDtypeStruct(x, jnp.float32) for x in shapes],
        in_specs=specs,
        out_specs=[VMEM] * len(shapes),
        scratch_shapes=scratch,
        compiler_params=pltpu.CompilerParams(vmem_limit_bytes=ROOM),
        cost_estimate=cost(8),
    )(*ins)
    return out if len(out) > 1 else out[0]


def across_kernel(table, known, blocks, out):
    count = table[COUNTS, 2]
    out[...] = jnp.zeros_like(out)

    @pl.loop(0, (count + GROUP - 1) >> 2)
    def _(g):
        terms = []
        for u in range(GROUP):
            t = g * GROUP + u
            there = t < count
            t = jnp.minimum(t, count - 1)
            n = table[LIST_T, t]
            c = n & (CB - 1)
            x = known[:, c & 1, c >> 1].reshape(NRHS, W) * jnp.where(there, 1.0, 0.0)
            terms.append((n >> 4, dot3(x, blocks[t]).reshape(PC, HS, W)))
        for a, term in terms:
            out[:, a] += term


def across(table, known, blocks):
    return pl.pallas_call(
        across_kernel,
        out_shape=jax.ShapeDtypeStruct((PC, RB, HS, W), jnp.float32),
        in_specs=[SMEM, VMEM, VMEM],
        out_specs=VMEM,
        compiler_params=pltpu.CompilerParams(vmem_limit_bytes=ROOM),
        cost_estimate=cost(8),
    )(table, known, blocks)


def local(rhs, lower, upper, lower_inverse, upper_inverse, pattern, levels, widths):
    right = rhs.reshape(RB, NRHS, W)
    lower_blocks = lower.reshape(RB, CB, W, W)
    upper_blocks = upper.reshape(RB, CB, W, W)
    lower_inv = lower_inverse.reshape(RB, W, W)
    upper_inv = upper_inverse.reshape(RB, W, W)
    table = tables(pattern, levels, widths)
    swap = lambda x: lax.all_to_all(x, "prow", 0, 0)

    packed_l, token = pack(0, CAP_L, table, lower_blocks, table)
    panel_l = lax.all_gather(packed_l, "pcol", tiled=True)
    leaves = level_step(0, PR, 0, table, None, right, lower_inv, None, sliced=True, after=token)
    known = swap(leaves)
    packed_u, far_blocks = pack(1, CAP_U, table, upper_blocks, known[0, 0], lower_blocks)
    panel_u = lax.all_gather(packed_u, "pcol", tiled=True)
    state, held = level_step(1, PR, 0, table, known, right, lower_inv, panel_l, sliced=True, group=8, fetch=True)
    known = swap(state)
    known = swap(level_step(2, PR, 0, table, known, right, lower_inv, held, sliced=True, group=8))
    split = known.reshape(2, PC, RB, HS, W).transpose(1, 0, 2, 3, 4)
    columns = lax.all_to_all(split, "pcol", 0, 0)
    sums = lax.all_to_all(across(table, columns, far_blocks), "pcol", 0, 0)
    step = lambda level, turn=None: level_step(
        level, PR, 0, table, known, right, lower_inv, held, turn=turn, sliced=True, less=sums
    )
    for level in range(3, LEVELS - 1):
        known = swap(step(level))
    state, forward = step(LEVELS - 1, upper_inv)
    known = swap(state)
    state, held, left = level_step(4, PR, 1, table, known, forward, upper_inv, panel_u, group=8, fetch=True)
    for level in range(3, 0, -1):
        known = swap(state)
        state, left = level_step(level, PR, 1, table, known, left, upper_inv, held, group=8)
    known = swap(state)
    state = level_step(0, PC, 1, table, known, left, upper_inv, held, both=True, less=forward, group=8)
    full = lax.all_to_all(state, "pcol", 0, 0)
    shape = rhs.shape
    whole = lambda x: x.transpose(1, 0, 2, 3).reshape(shape)
    args = (rhs, lower, upper, lower_inverse, upper_inverse, pattern, levels, widths)
    done = lax.while_loop(
        lambda c: c[2] > 0,
        lambda c: general(*args) + (jnp.int32(0),),
        (whole(full[:, 0]), whole(full[:, 1]), table[COUNTS, 3]),
    )
    return done[0], done[1]


def solution(mesh):
    in_specs = (
        P(None, "prow", None, None),
        P(None, "prow", None, "pcol", None, None),
        P(None, "prow", None, "pcol", None, None),
        P(None, "prow", None, None),
        P(None, "prow", None, None),
        P(),
        P(),
        P(),
    )
    out_specs = (P(None, "prow", None, None), P(None, "prow", None, None))
    return jax.shard_map(local, mesh=mesh, in_specs=in_specs, out_specs=out_specs, check_vma=False)
```

```python
import jax
import jax.numpy as jnp
from jax import lax
from jax.experimental import pallas as pl
from jax.experimental.pallas import tpu as pltpu
from jax.sharding import PartitionSpec as P

LEVELS = 6
W = 128
NRHS = 64
NB = 128
RB = 8
CB = 16
PR = 16
PC = 8
HS = NRHS // PC
CAP_L = 10
CAP_U = 28
LIST = 64
GROUP = 4
ORDER = [[PC * (k & 1) + (k >> 1) for k in range(PR)]]
HBM = pl.BlockSpec(memory_space=pl.ANY)
ROOM = 44 * 1024 * 1024
SMEM = pl.BlockSpec(memory_space=pltpu.SMEM)
VMEM = pl.BlockSpec(memory_space=pltpu.VMEM)
WIDTH = 0
LIST_L, LIST_U, LIST_T, PACK_L, PACK_U, COUNTS, ROWS, STARTS = range(8, 16)
HALF = 16


def spread(value, axis, source):
    kept = jnp.where(lax.axis_index(axis) == source, value, 0).astype(value.dtype)
    return lax.psum(kept, axis)


def apply_inverse(inverse, right):
    return jnp.einsum("akl,ahl->ahk", inverse, right, precision=lax.Precision.HIGHEST)


def solve_levels(blocks, inverse, right, valid, row_levels, mask, rising):
    prow_count = lax.axis_size("prow")
    pcol_count = lax.axis_size("pcol")
    column = lax.axis_index("pcol")
    ratio = prow_count // pcol_count
    masked = blocks * mask[:, :, None, None]
    row_state = jnp.zeros(right.shape, jnp.float32)
    col_state = jnp.zeros((masked.shape[1],) + right.shape[1:], jnp.float32)
    order = list(range(LEVELS)) if rising else list(range(LEVELS - 1, -1, -1))
    for place, level in enumerate(order):
        partial_sum = jnp.einsum(
            "ackl,chl->ahk", masked, col_state, precision=lax.Precision.HIGHEST
        )
        total = lax.psum(partial_sum, "pcol")
        fresh = apply_inverse(inverse, right - total) * valid
        current = (row_levels == level)[:, None, None]
        row_state = jnp.where(current, fresh, row_state)
        if place + 1 < LEVELS:
            pieces = []
            for offset in range(ratio):
                pieces.append(spread(row_state, "prow", column + offset * pcol_count))
            stacked = jnp.stack(pieces, axis=1)
            col_state = stacked.reshape((-1,) + right.shape[1:])
    return row_state


def general(rhs, lower, upper, lower_inverse, upper_inverse, pattern, levels, widths):
    prow_count = lax.axis_size("prow")
    pcol_count = lax.axis_size("pcol")
    row_index = lax.axis_index("prow")
    col_index = lax.axis_index("pcol")
    row_blocks = rhs.shape[0]
    col_blocks = lower.shape[2]
    width = rhs.shape[3]
    right = rhs.reshape(row_blocks, rhs.shape[2], width)
    lower_local = lower.reshape(row_blocks, col_blocks, width, width)
    upper_local = upper.reshape(row_blocks, col_blocks, width, width)
    lower_inv = lower_inverse.reshape(row_blocks, width, width)
    upper_inv = upper_inverse.reshape(row_blocks, width, width)
    row_levels = lax.dynamic_index_in_dim(
        levels.reshape(row_blocks, prow_count), row_index, 1, keepdims=False
    )
    col_levels = lax.dynamic_index_in_dim(
        levels.reshape(col_blocks, pcol_count), col_index, 1, keepdims=False
    )
    row_widths = lax.dynamic_index_in_dim(
        widths.reshape(row_blocks, prow_count), row_index, 1, keepdims=False
    )
    grid = pattern.reshape(row_blocks, prow_count, col_blocks, pcol_count)
    grid = lax.dynamic_index_in_dim(grid, row_index, 1, keepdims=False)
    grid = lax.dynamic_index_in_dim(grid, col_index, 2, keepdims=False).astype(jnp.float32)
    valid = (jnp.arange(width)[None, :] < row_widths[:, None]).astype(jnp.float32)[:, None, :]
    below = grid * (col_levels[None, :] < row_levels[:, None]).astype(jnp.float32)
    above = grid * (col_levels[None, :] > row_levels[:, None]).astype(jnp.float32)
    forward = solve_levels(lower_local, lower_inv, right, valid, row_levels, below, True)
    solution = solve_levels(upper_local, upper_inv, forward, valid, row_levels, above, False)
    shape = rhs.shape
    return (forward.reshape(shape), solution.reshape(shape))


def dot3(x, w):
    m, n = x.shape[0], w.shape[0]
    xh = x.astype(jnp.bfloat16).astype(jnp.float32)
    xs = jnp.concatenate([xh, x - xh], axis=0).astype(jnp.bfloat16)
    wh = w.astype(jnp.bfloat16)
    wl = (w - wh.astype(jnp.float32)).astype(jnp.bfloat16)
    ws = jnp.concatenate([wh, wl], axis=0)
    y = lax.dot_general(xs, ws, (((1,), (1,)), ((), ())), preferred_element_type=jnp.float32)
    return (y[m:, n:] + y[:m, n:]) + (y[m:, :n] + y[:m, :n])


def iota(shape, dim):
    return lax.broadcasted_iota(jnp.int32, shape, dim)


def cost(mib):
    return pl.CostEstimate(flops=0, bytes_accessed=mib << 20, transcendentals=0)


def flag(cond):
    return jnp.where(cond, 1.0, 0.0)


def dot(x, y):
    return jnp.dot(x, y, preferred_element_type=jnp.float32)


def ranks(sel):
    i, j = iota((NB, NB), 0), iota((NB, NB), 1)
    same = flag((i & (PC - 1)) == (j & (PC - 1)))
    total = jnp.zeros((1, NB), jnp.float32)
    rows = []
    for a in range(RB):
        rows.append(total)
        total = total + sel[a : a + 1]
    return dot(jnp.concatenate(rows, axis=0), same) + dot(sel, same * flag(i < j))


def listing(sel, place, value, size):
    t = iota((size, NB), 0).astype(jnp.float32)
    held = jnp.zeros((size, NB), jnp.float32)
    for a in range(RB):
        hit = flag(t == place[a : a + 1]) * sel[a : a + 1]
        held = held + hit * value[a : a + 1]
    ones = jnp.ones((RB, NB), jnp.float32)
    row = lax.dot_general(ones, held, (((1,), (1,)), ((), ())), preferred_element_type=jnp.float32)[:1]
    if size < NB:
        row = jnp.concatenate([row, jnp.zeros((1, NB - size), jnp.float32)], axis=1)
    return row


def count(sel):
    return jnp.sum(jnp.sum(sel, axis=1, keepdims=True), axis=0, keepdims=True)


def table_kernel(pattern, levels, widths, _, out):
    p = lax.axis_index("prow")
    q = lax.axis_index("pcol")
    lev = levels[...].astype(jnp.float32)
    wid = widths[...].astype(jnp.float32)
    i = iota((NB, NB), 0)
    j = iota((NB, NB), 1)
    lev_col = jnp.sum(jnp.where(i == j, lev, 0.0), axis=1, keepdims=True)
    linked = flag(pattern[...] > 0)
    low = linked * flag(lev < lev_col)
    high = linked * flag(lev > lev_col)
    near = low * flag((lev_col < 2.5) | (lev > 2.5))
    far = low - near
    same = flag((i & (PC - 1)) == (j & (PC - 1)))
    ahead = flag(i < j)

    by_row = flag((iota((PR, NB), 1) & (PR - 1)) == iota((PR, NB), 0))

    def over(full, cap):
        rows = dot(by_row, full)
        most = jnp.max(jnp.max(dot(rows, same), axis=1, keepdims=True), axis=0, keepdims=True)
        listed = jnp.max(jnp.sum(rows, axis=1, keepdims=True), axis=0, keepdims=True)
        return flag((most > cap) | (listed > LIST))

    def over_far():
        rows = dot(dot(by_row, far), same)
        return flag(jnp.max(jnp.max(rows, axis=1, keepdims=True), axis=0, keepdims=True) > LIST)

    full = jnp.maximum(jnp.maximum(over(near, CAP_L), over(high, CAP_U)), over_far())

    lane = iota((RB, NB), 1)
    sub = iota((RB, NB), 0)
    mine = flag(lane == sub * PR + p)
    row_lev = jnp.sum(mine * lev, axis=1, keepdims=True)
    row_wid = jnp.sum(mine * wid, axis=1, keepdims=True)
    col = lane & (PC - 1)
    own = flag(col == q)
    node = lane.astype(jnp.float32)
    spot = (sub * CB + (lane >> 3)).astype(jnp.float32)

    def ordered():
        start = jnp.zeros((RB, 1), jnp.float32)
        below = jnp.zeros((1, NB), jnp.float32)
        index = iota((RB, 1), 0)
        for a in range(RB):
            first = (row_lev[a : a + 1] < row_lev) | ((row_lev[a : a + 1] == row_lev) & (index > a))
            start = start + flag(first)
            below = below + flag(row_lev[a : a + 1] < node[:1])
        return start, below

    def by_step(sel, step):
        parts = jnp.concatenate([sel * flag(step == k) for k in range(LEVELS)], axis=0)
        size = RB * LEVELS
        earlier = flag(iota((size, size), 0) > iota((size, size), 1))
        base = jnp.sum(dot(earlier, parts), axis=1, keepdims=True)
        spread = parts * (dot(parts, ahead) + base)
        place = jnp.zeros((RB, NB), jnp.float32)
        below = jnp.zeros((1, NB), jnp.float32)
        for k in range(LEVELS):
            place = place + spread[RB * k : RB * (k + 1)]
            below = below + flag(node[:1] == k) * base[RB * k : RB * k + 1]
        return place, below + flag(node[:1] == LEVELS) * count(sel)

    def panel(sel, cap, step):
        rank = ranks(sel)
        place, below = by_step(sel, step)
        slot = (col * cap).astype(jnp.float32) + jnp.minimum(rank, cap - 1.0)
        listed = listing(sel, place, slot, LIST) * (NB * RB) + listing(sel, place, node, LIST) * RB
        listed = listed + listing(sel, place, sub.astype(jnp.float32), LIST)
        packed = listing(sel * own, rank, spot, 32)
        return jnp.minimum(below, LIST), listed, packed, jnp.minimum(count(sel * own), cap)

    near_p = dot(mine, near)
    high_p = dot(mine, high)
    far_p = dot(mine, far)
    top = jnp.where(row_lev > 2.5, row_lev, jnp.where(row_lev > 0.5, 4.0, 3.0))
    fourth = jnp.minimum(jnp.maximum(row_lev, 2.0), 3.0)
    third = jnp.minimum(jnp.maximum(row_lev, 1.0), 2.0)
    down = jnp.where(lev > 4.5, top, jnp.where(lev > 3.5, fourth, jnp.where(lev > 2.5, third, row_lev)))
    below_l, list_l, pack_l, count_l = panel(near_p, CAP_L, row_lev + 0.0 * node)
    below_u, list_u, pack_u, count_u = panel(high_p, CAP_U, down)
    list_t = listing(far_p * own, ranks(far_p), spot, NB)
    count_t = jnp.minimum(count(far_p * own), LIST)
    rows = flag(lane == WIDTH) * row_wid
    counts = jnp.zeros((1, NB), jnp.float32)
    for k, value in enumerate([count_l, count_u, count_t, full]):
        counts = counts + flag(lane[:1] == k) * value
    spot_of, below_r = ordered()
    order = jnp.zeros((1, NB), jnp.float32)
    for a in range(RB):
        order = order + flag(spot_of[a : a + 1] == node[:1]) * a

    def beside(x, y):
        return jnp.concatenate([x[:, :HALF], y[:, :HALF], jnp.zeros((1, NB - 2 * HALF), jnp.float32)], axis=1)

    order = beside(order, below_r)
    starts = beside(below_l, below_u)
    lists = jnp.concatenate([list_l, list_u, list_t, pack_l, pack_u, counts, order, starts], axis=0)
    out[0:8, :] = rows.astype(jnp.int32)
    out[8:16, :] = lists.astype(jnp.int32)


def tables(pattern, levels, widths, after):
    return pl.pallas_call(
        table_kernel,
        out_shape=jax.ShapeDtypeStruct((16, NB), jnp.int32),
        in_specs=[VMEM, VMEM, VMEM, VMEM],
        out_specs=VMEM,
        cost_estimate=cost(4),
    )(pattern, levels.reshape(1, NB), widths.reshape(1, NB), after)


def first_kernel(pattern, levels, blocks, out, token, lists, places, held, sem, sems_in, sems_out):
    p = lax.axis_index("prow")
    q = lax.axis_index("pcol")
    lev = levels[...].astype(jnp.float32)
    i, j = iota((NB, NB), 0), iota((NB, NB), 1)
    lev_col = jnp.sum(jnp.where(i == j, lev, 0.0), axis=1, keepdims=True)
    near = flag(pattern[...] > 0) * flag(lev < lev_col) * flag((lev_col < 2.5) | (lev > 2.5))
    lane, sub = iota((RB, NB), 1), iota((RB, NB), 0)
    sel = dot(flag(lane == sub * PR + p), near) * flag((lane & (PC - 1)) == q)
    spot = (sub * CB + (lane >> 3)).astype(jnp.float32)
    found = listing(sel, ranks(sel), spot, 32)
    number = jnp.minimum(count(sel), CAP_L)
    rows = jnp.where(sub == 0, found, number + 0.0 * spot)
    lists[...] = rows.astype(jnp.int32)
    move = pltpu.make_async_copy(lists, places, sem)
    move.start()
    token[...] = jnp.zeros_like(token)
    move.wait()
    total = places[1, 0]

    def load(t):
        n = places[0, t]
        return pltpu.make_async_copy(blocks.at[n >> 4, n & (CB - 1)], held.at[t], sems_in.at[t])

    def store(t):
        return pltpu.make_async_copy(held.at[t], out.at[t], sems_out.at[t])

    pl.loop(0, total)(lambda t: load(t).start())

    @pl.loop(0, total)
    def _(t):
        load(t).wait()
        store(t).start()

    pl.loop(0, total)(lambda t: store(t).wait())


def first(pattern, levels, blocks):
    return pl.pallas_call(
        first_kernel,
        out_shape=(
            jax.ShapeDtypeStruct((CAP_L, W, W), jnp.float32),
            jax.ShapeDtypeStruct((1, NB), jnp.int32),
        ),
        in_specs=[VMEM, VMEM, HBM],
        out_specs=(HBM, VMEM),
        scratch_shapes=[
            pltpu.VMEM((RB, NB), jnp.int32),
            pltpu.SMEM((RB, NB), jnp.int32),
            pltpu.VMEM((CAP_L, W, W), jnp.float32),
            pltpu.SemaphoreType.DMA,
            pltpu.SemaphoreType.DMA((CAP_L,)),
            pltpu.SemaphoreType.DMA((CAP_L,)),
        ],
        compiler_params=pltpu.CompilerParams(vmem_limit_bytes=ROOM),
        cost_estimate=cost(4),
    )(pattern, levels.reshape(1, NB), blocks)


def pack_kernel(where, cap, with_far, table, blocks, _, *rest):
    rest = list(rest)
    lower = rest.pop(0) if with_far else None
    out, extra, held, sems_in, sems_out = rest[:5]
    count = table[COUNTS, where]
    row = PACK_L + where

    def load(t):
        n = table[row, t]
        return pltpu.make_async_copy(blocks.at[n >> 4, n & (CB - 1)], held.at[t], sems_in.at[t])

    def store(t):
        return pltpu.make_async_copy(held.at[t], out.at[t], sems_out.at[t])

    def load_far(t):
        n = table[LIST_T, t]
        return pltpu.make_async_copy(lower.at[n >> 4, n & (CB - 1)], extra.at[t], rest[5].at[t])

    pl.loop(0, count)(lambda t: load(t).start())
    if with_far:
        pl.loop(0, table[COUNTS, 2])(lambda t: load_far(t).start())
    else:
        extra[...] = jnp.zeros_like(extra)

    @pl.loop(0, count)
    def _(t):
        load(t).wait()
        store(t).start()

    pl.loop(0, count)(lambda t: store(t).wait())
    if with_far:
        pl.loop(0, table[COUNTS, 2])(lambda t: load_far(t).wait())


def pack(where, cap, table, blocks, after, lower=None):
    with_far = lower is not None
    extra = (LIST, W, W) if with_far else (HS, W)
    scratch = [
        pltpu.VMEM((cap, W, W), jnp.float32),
        pltpu.SemaphoreType.DMA((cap,)),
        pltpu.SemaphoreType.DMA((cap,)),
    ]
    if with_far:
        scratch.append(pltpu.SemaphoreType.DMA((LIST,)))
    return pl.pallas_call(
        lambda *refs: pack_kernel(where, cap, with_far, *refs),
        out_shape=(
            jax.ShapeDtypeStruct((cap, W, W), jnp.float32),
            jax.ShapeDtypeStruct(extra, jnp.float32),
        ),
        in_specs=[SMEM, HBM, HBM] + ([HBM] if with_far else []),
        out_specs=(HBM, VMEM),
        scratch_shapes=scratch,
        compiler_params=pltpu.CompilerParams(vmem_limit_bytes=ROOM),
        cost_estimate=cost(4),
    )(table, blocks, after, *([lower] if with_far else []))


def level_kernel(level, copies, kind, turn, both, sliced, group, fetch, table, known, right, inverse, panel, less, *rest):
    rest = list(rest)
    inverse_2 = rest.pop(0) if turn else None
    out = rest.pop(0)
    out_2 = rest.pop(0) if turn else None
    blocks = rest.pop(0) if fetch else panel
    sums = rest.pop(0)
    sems = rest.pop(0) if fetch else None
    p = lax.axis_index("prow")
    row = LIST_U if kind else LIST_L
    e0, e1 = table[STARTS, kind * HALF + level], table[STARTS, kind * HALF + level + 1]
    r0, r1 = table[ROWS, HALF + level], table[ROWS, HALF + level + 1]
    whole = table[STARTS, kind * HALF + LEVELS]

    def copy(t):
        return pltpu.make_async_copy(panel.at[table[row, t] >> 10], blocks.at[t], sems.at[t])

    if fetch:
        pl.loop(e0, e1)(lambda t: copy(t).start())
        pl.loop(0, e0)(lambda t: copy(t).start())
        pl.loop(e1, whole)(lambda t: copy(t).start())

    shift = lax.axis_index("pcol") * HS
    for a in range(RB):
        mine = right[a, pl.ds(shift, HS)] if sliced else right[a]
        if less is not None and not both:
            parts = [less[k, a] for k in range(PC)]
            while len(parts) > 1:
                parts = [x + y for x, y in zip(parts[::2], parts[1::2])]
            mine = mine - parts[0]
        sums[a] = mine
        old = known[((p & (PC - 1)) << 1) + (p >> 3), a] if known is not None else jnp.zeros((HS, W), jnp.float32)
        for r in range(copies):
            if both:
                out[r, 0, a] = less[a]
                out[r, 1, a] = old
            else:
                out[r, a] = old if not turn else jnp.zeros((HS, W), jnp.float32)
        if turn:
            out_2[a] = old

    if panel is not None:
        @pl.loop(0, (e1 - e0 + group - 1) // group)
        def _(g):
            terms = []
            for u in range(group):
                t = e0 + g * group + u
                there = t < e1

                if fetch:
                    @pl.when(there)
                    def _():
                        copy(t).wait()

                t = jnp.minimum(t, e1 - 1)
                node = (table[row, t] >> 3) & (NB - 1)
                x = known[((node & (PC - 1)) << 1) + ((node >> 3) & 1), node >> 4] * jnp.where(there, 1.0, 0.0)
                terms.append((table[row, t] & (RB - 1), dot3(x, blocks[t])))
            for a, term in terms:
                sums[a] -= term

    lane = iota((HS, W), 1)

    @pl.loop(0, (r1 - r0 + GROUP - 1) >> 2)
    def _(g):
        fresh = []
        for u in range(GROUP):
            r = r0 + g * GROUP + u
            there = r < r1
            a = table[ROWS, jnp.minimum(r, r1 - 1)]

            fresh.append((there, a, jnp.where(lane < table[a, WIDTH], dot3(sums[a], inverse[a]), 0.0)))
        if turn:
            later = [jnp.where(lane < table[a, WIDTH], dot3(x, inverse_2[a]), 0.0) for _, a, x in fresh]
            for there, a, x in fresh:
                out_2[a] = x
            fresh = [(there, a, x) for (there, a, _), x in zip(fresh, later)]
        for there, a, x in fresh:
            @pl.when(there)
            def _():
                for r in range(copies):
                    if both:
                        out[r, 1, a] = x
                    else:
                        out[r, a] = x

    if fetch:
        pl.loop(0, e0)(lambda t: copy(t).wait())
        pl.loop(e1, whole)(lambda t: copy(t).wait())


def level_step(
    level, copies, kind, table, known, right, inverse, panel, *,
    turn=None, both=False, sliced=False, after=None, less=None, group=GROUP, fetch=False,
):
    ins, specs = [table], [SMEM]
    given = ((known, VMEM), (right, VMEM), (inverse, VMEM), (panel, HBM if fetch else VMEM), (less, VMEM))
    for x, spec in given + ((turn, VMEM), (after, HBM)):
        if x is not None:
            ins.append(x)
            specs.append(spec)

    def kernel(*refs):
        refs = list(refs)
        if after is not None:
            refs.pop(len(ins) - 1)
        args = [refs.pop(0)] + [refs.pop(0) if x is not None else None for x, _ in given]
        level_kernel(level, copies, kind, turn is not None, both, sliced, group, fetch, *args, *refs)

    small = (RB, HS, W)
    shapes = [(copies, 2) + small if both else (copies,) + small]
    if turn is not None:
        shapes.append(small)
    if fetch:
        shapes.append((LIST, W, W))
    scratch = []
    if kind == 1 and not both:
        shapes.append(small)
    else:
        scratch.append(pltpu.VMEM(small, jnp.float32))
    if fetch:
        scratch.append(pltpu.SemaphoreType.DMA((LIST,)))
    out = pl.pallas_call(
        kernel,
        out_shape=[jax.ShapeDtypeStruct(x, jnp.float32) for x in shapes],
        in_specs=specs,
        out_specs=[VMEM] * len(shapes),
        scratch_shapes=scratch,
        compiler_params=pltpu.CompilerParams(vmem_limit_bytes=ROOM),
        cost_estimate=cost(8),
    )(*ins)
    return out if len(out) > 1 else out[0]


def across_kernel(table, known, blocks, out):
    count = table[COUNTS, 2]
    out[...] = jnp.zeros_like(out)

    @pl.loop(0, (count + GROUP - 1) >> 2)
    def _(g):
        terms = []
        for u in range(GROUP):
            t = g * GROUP + u
            there = t < count
            t = jnp.minimum(t, count - 1)
            n = table[LIST_T, t]
            c = n & (CB - 1)
            x = known[:, c & 1, c >> 1].reshape(NRHS, W) * jnp.where(there, 1.0, 0.0)
            terms.append((n >> 4, dot3(x, blocks[t]).reshape(PC, HS, W)))
        for a, term in terms:
            out[:, a] += term


def across(table, known, blocks):
    return pl.pallas_call(
        across_kernel,
        out_shape=jax.ShapeDtypeStruct((PC, RB, HS, W), jnp.float32),
        in_specs=[SMEM, VMEM, VMEM],
        out_specs=VMEM,
        compiler_params=pltpu.CompilerParams(vmem_limit_bytes=ROOM),
        cost_estimate=cost(8),
    )(table, known, blocks)


def local(rhs, lower, upper, lower_inverse, upper_inverse, pattern, levels, widths):
    right = rhs.reshape(RB, NRHS, W)
    lower_blocks = lower.reshape(RB, CB, W, W)
    upper_blocks = upper.reshape(RB, CB, W, W)
    lower_inv = lower_inverse.reshape(RB, W, W)
    upper_inv = upper_inverse.reshape(RB, W, W)
    packed_l, token = first(pattern, levels, lower_blocks)
    table = tables(pattern, levels, widths, token)
    swap = lambda x: lax.all_to_all(x, "prow", 0, 0, axis_index_groups=ORDER)

    panel_l = lax.all_gather(packed_l, "pcol", tiled=True)
    leaves = level_step(0, PR, 0, table, None, right, lower_inv, None, sliced=True)
    known = swap(leaves)
    packed_u, far_blocks = pack(1, CAP_U, table, upper_blocks, known[0, 0], lower_blocks)
    panel_u = lax.all_gather(packed_u, "pcol", tiled=True)
    state, held = level_step(1, PR, 0, table, known, right, lower_inv, panel_l, sliced=True, group=8, fetch=True)
    known = swap(state)
    known = swap(level_step(2, PR, 0, table, known, right, lower_inv, held, sliced=True, group=8))
    columns = lax.all_to_all(known.reshape(PC, 2, RB, HS, W), "pcol", 0, 0)
    sums = lax.all_to_all(across(table, columns, far_blocks), "pcol", 0, 0)
    step = lambda level, turn=None: level_step(
        level, PR, 0, table, known, right, lower_inv, held, turn=turn, sliced=True, less=sums
    )
    for level in range(3, LEVELS - 1):
        known = swap(step(level))
    state, forward = step(LEVELS - 1, upper_inv)
    known = swap(state)
    state, held, left = level_step(4, PR, 1, table, known, forward, upper_inv, panel_u, group=8, fetch=True)
    for level in range(3, 0, -1):
        known = swap(state)
        state, left = level_step(level, PR, 1, table, known, left, upper_inv, held, group=8)
    known = swap(state)
    state = level_step(0, PC, 1, table, known, left, upper_inv, held, both=True, less=forward, group=8)
    full = lax.all_to_all(state, "pcol", 0, 0)
    shape = rhs.shape
    whole = lambda x: x.transpose(1, 0, 2, 3).reshape(shape)
    args = (rhs, lower, upper, lower_inverse, upper_inverse, pattern, levels, widths)
    done = lax.while_loop(
        lambda c: c[2] > 0,
        lambda c: general(*args) + (jnp.int32(0),),
        (whole(full[:, 0]), whole(full[:, 1]), table[COUNTS, 3]),
    )
    return done[0], done[1]


def solution(mesh):
    in_specs = (
        P(None, "prow", None, None),
        P(None, "prow", None, "pcol", None, None),
        P(None, "prow", None, "pcol", None, None),
        P(None, "prow", None, None),
        P(None, "prow", None, None),
        P(),
        P(),
        P(),
    )
    out_specs = (P(None, "prow", None, None), P(None, "prow", None, None))
    return jax.shard_map(local, mesh=mesh, in_specs=in_specs, out_specs=out_specs, check_vma=False)
```

```python
import jax
import jax.numpy as jnp
from jax import lax
from jax.experimental import pallas as pl
from jax.experimental.pallas import tpu as pltpu
from jax.sharding import PartitionSpec as P

LEVELS = 6
W = 128
NRHS = 64
NB = 128
RB = 8
CB = 16
PR = 16
PC = 8
HS = NRHS // PC
CAP_L = 10
CAP_U = 28
LIST = 64
GROUP = 4
HBM = pl.BlockSpec(memory_space=pl.ANY)
ROOM = 44 * 1024 * 1024
SMEM = pl.BlockSpec(memory_space=pltpu.SMEM)
VMEM = pl.BlockSpec(memory_space=pltpu.VMEM)
WIDTH = 0
LIST_L, LIST_U, LIST_T, PACK_L, PACK_U, COUNTS, ROWS, STARTS = range(8, 16)
HALF = 16


def spread(value, axis, source):
    kept = jnp.where(lax.axis_index(axis) == source, value, 0).astype(value.dtype)
    return lax.psum(kept, axis)


def apply_inverse(inverse, right):
    return jnp.einsum("akl,ahl->ahk", inverse, right, precision=lax.Precision.HIGHEST)


def solve_levels(blocks, inverse, right, valid, row_levels, mask, rising):
    prow_count = lax.axis_size("prow")
    pcol_count = lax.axis_size("pcol")
    column = lax.axis_index("pcol")
    ratio = prow_count // pcol_count
    masked = blocks * mask[:, :, None, None]
    row_state = jnp.zeros(right.shape, jnp.float32)
    col_state = jnp.zeros((masked.shape[1],) + right.shape[1:], jnp.float32)
    order = list(range(LEVELS)) if rising else list(range(LEVELS - 1, -1, -1))
    for place, level in enumerate(order):
        partial_sum = jnp.einsum(
            "ackl,chl->ahk", masked, col_state, precision=lax.Precision.HIGHEST
        )
        total = lax.psum(partial_sum, "pcol")
        fresh = apply_inverse(inverse, right - total) * valid
        current = (row_levels == level)[:, None, None]
        row_state = jnp.where(current, fresh, row_state)
        if place + 1 < LEVELS:
            pieces = []
            for offset in range(ratio):
                pieces.append(spread(row_state, "prow", column + offset * pcol_count))
            stacked = jnp.stack(pieces, axis=1)
            col_state = stacked.reshape((-1,) + right.shape[1:])
    return row_state


def general(rhs, lower, upper, lower_inverse, upper_inverse, pattern, levels, widths):
    prow_count = lax.axis_size("prow")
    pcol_count = lax.axis_size("pcol")
    row_index = lax.axis_index("prow")
    col_index = lax.axis_index("pcol")
    row_blocks = rhs.shape[0]
    col_blocks = lower.shape[2]
    width = rhs.shape[3]
    right = rhs.reshape(row_blocks, rhs.shape[2], width)
    lower_local = lower.reshape(row_blocks, col_blocks, width, width)
    upper_local = upper.reshape(row_blocks, col_blocks, width, width)
    lower_inv = lower_inverse.reshape(row_blocks, width, width)
    upper_inv = upper_inverse.reshape(row_blocks, width, width)
    row_levels = lax.dynamic_index_in_dim(
        levels.reshape(row_blocks, prow_count), row_index, 1, keepdims=False
    )
    col_levels = lax.dynamic_index_in_dim(
        levels.reshape(col_blocks, pcol_count), col_index, 1, keepdims=False
    )
    row_widths = lax.dynamic_index_in_dim(
        widths.reshape(row_blocks, prow_count), row_index, 1, keepdims=False
    )
    grid = pattern.reshape(row_blocks, prow_count, col_blocks, pcol_count)
    grid = lax.dynamic_index_in_dim(grid, row_index, 1, keepdims=False)
    grid = lax.dynamic_index_in_dim(grid, col_index, 2, keepdims=False).astype(jnp.float32)
    valid = (jnp.arange(width)[None, :] < row_widths[:, None]).astype(jnp.float32)[:, None, :]
    below = grid * (col_levels[None, :] < row_levels[:, None]).astype(jnp.float32)
    above = grid * (col_levels[None, :] > row_levels[:, None]).astype(jnp.float32)
    forward = solve_levels(lower_local, lower_inv, right, valid, row_levels, below, True)
    solution = solve_levels(upper_local, upper_inv, forward, valid, row_levels, above, False)
    shape = rhs.shape
    return (forward.reshape(shape), solution.reshape(shape))


def dot3(x, w):
    m, n = x.shape[0], w.shape[0]
    xh = x.astype(jnp.bfloat16).astype(jnp.float32)
    xs = jnp.concatenate([xh, x - xh], axis=0).astype(jnp.bfloat16)
    wh = w.astype(jnp.bfloat16)
    wl = (w - wh.astype(jnp.float32)).astype(jnp.bfloat16)
    ws = jnp.concatenate([wh, wl], axis=0)
    y = lax.dot_general(xs, ws, (((1,), (1,)), ((), ())), preferred_element_type=jnp.float32)
    return (y[m:, n:] + y[:m, n:]) + (y[m:, :n] + y[:m, :n])


def iota(shape, dim):
    return lax.broadcasted_iota(jnp.int32, shape, dim)


def cost(mib):
    return pl.CostEstimate(flops=0, bytes_accessed=mib << 20, transcendentals=0)


def flag(cond):
    return jnp.where(cond, 1.0, 0.0)


def dot(x, y):
    return jnp.dot(x, y, preferred_element_type=jnp.float32)


def ranks(sel):
    i, j = iota((NB, NB), 0), iota((NB, NB), 1)
    same = flag((i & (PC - 1)) == (j & (PC - 1)))
    total = jnp.zeros((1, NB), jnp.float32)
    rows = []
    for a in range(RB):
        rows.append(total)
        total = total + sel[a : a + 1]
    return dot(jnp.concatenate(rows, axis=0), same) + dot(sel, same * flag(i < j))


def listing(sel, place, value, size):
    t = iota((size, NB), 0).astype(jnp.float32)
    held = jnp.zeros((size, NB), jnp.float32)
    for a in range(RB):
        hit = flag(t == place[a : a + 1]) * sel[a : a + 1]
        held = held + hit * value[a : a + 1]
    ones = jnp.ones((RB, NB), jnp.float32)
    row = lax.dot_general(ones, held, (((1,), (1,)), ((), ())), preferred_element_type=jnp.float32)[:1]
    if size < NB:
        row = jnp.concatenate([row, jnp.zeros((1, NB - size), jnp.float32)], axis=1)
    return row


def count(sel):
    return jnp.sum(jnp.sum(sel, axis=1, keepdims=True), axis=0, keepdims=True)


def table_kernel(pattern, levels, widths, _, out):
    p = lax.axis_index("prow")
    q = lax.axis_index("pcol")
    lev = levels[...].astype(jnp.float32)
    wid = widths[...].astype(jnp.float32)
    i = iota((NB, NB), 0)
    j = iota((NB, NB), 1)
    lev_col = jnp.sum(jnp.where(i == j, lev, 0.0), axis=1, keepdims=True)
    linked = flag(pattern[...] > 0)
    low = linked * flag(lev < lev_col)
    high = linked * flag(lev > lev_col)
    near = low * flag((lev_col < 2.5) | (lev > 2.5))
    far = low - near
    same = flag((i & (PC - 1)) == (j & (PC - 1)))
    ahead = flag(i < j)

    by_row = flag((iota((PR, NB), 1) & (PR - 1)) == iota((PR, NB), 0))

    def over(full, cap):
        rows = dot(by_row, full)
        most = jnp.max(jnp.max(dot(rows, same), axis=1, keepdims=True), axis=0, keepdims=True)
        listed = jnp.max(jnp.sum(rows, axis=1, keepdims=True), axis=0, keepdims=True)
        return flag((most > cap) | (listed > LIST))

    def over_far():
        rows = dot(dot(by_row, far), same)
        return flag(jnp.max(jnp.max(rows, axis=1, keepdims=True), axis=0, keepdims=True) > LIST)

    full = jnp.maximum(jnp.maximum(over(near, CAP_L), over(high, CAP_U)), over_far())

    lane = iota((RB, NB), 1)
    sub = iota((RB, NB), 0)
    mine = flag(lane == sub * PR + p)
    row_lev = jnp.sum(mine * lev, axis=1, keepdims=True)
    row_wid = jnp.sum(mine * wid, axis=1, keepdims=True)
    col = lane & (PC - 1)
    own = flag(col == q)
    node = lane.astype(jnp.float32)
    spot = (sub * CB + (lane >> 3)).astype(jnp.float32)

    def ordered():
        start = jnp.zeros((RB, 1), jnp.float32)
        below = jnp.zeros((1, NB), jnp.float32)
        index = iota((RB, 1), 0)
        for a in range(RB):
            first = (row_lev[a : a + 1] < row_lev) | ((row_lev[a : a + 1] == row_lev) & (index > a))
            start = start + flag(first)
            below = below + flag(row_lev[a : a + 1] < node[:1])
        return start, below

    def by_step(sel, step):
        parts = jnp.concatenate([sel * flag(step == k) for k in range(LEVELS)], axis=0)
        size = RB * LEVELS
        earlier = flag(iota((size, size), 0) > iota((size, size), 1))
        base = jnp.sum(dot(earlier, parts), axis=1, keepdims=True)
        spread = parts * (dot(parts, ahead) + base)
        place = jnp.zeros((RB, NB), jnp.float32)
        below = jnp.zeros((1, NB), jnp.float32)
        for k in range(LEVELS):
            place = place + spread[RB * k : RB * (k + 1)]
            below = below + flag(node[:1] == k) * base[RB * k : RB * k + 1]
        return place, below + flag(node[:1] == LEVELS) * count(sel)

    def panel(sel, cap, step):
        rank = ranks(sel)
        place, below = by_step(sel, step)
        slot = (col * cap).astype(jnp.float32) + jnp.minimum(rank, cap - 1.0)
        listed = listing(sel, place, slot, LIST) * (NB * RB) + listing(sel, place, node, LIST) * RB
        listed = listed + listing(sel, place, sub.astype(jnp.float32), LIST)
        packed = listing(sel * own, rank, spot, 32)
        return jnp.minimum(below, LIST), listed, packed, jnp.minimum(count(sel * own), cap)

    near_p = dot(mine, near)
    high_p = dot(mine, high)
    far_p = dot(mine, far)
    top = jnp.where(row_lev > 2.5, row_lev, jnp.where(row_lev > 0.5, 4.0, 3.0))
    fourth = jnp.minimum(jnp.maximum(row_lev, 2.0), 3.0)
    third = jnp.minimum(jnp.maximum(row_lev, 1.0), 2.0)
    down = jnp.where(lev > 4.5, top, jnp.where(lev > 3.5, fourth, jnp.where(lev > 2.5, third, row_lev)))
    below_l, list_l, pack_l, count_l = panel(near_p, CAP_L, row_lev + 0.0 * node)
    below_u, list_u, pack_u, count_u = panel(high_p, CAP_U, down)
    list_t = listing(far_p * own, ranks(far_p), spot, NB)
    count_t = jnp.minimum(count(far_p * own), LIST)
    rows = flag(lane == WIDTH) * row_wid
    counts = jnp.zeros((1, NB), jnp.float32)
    for k, value in enumerate([count_l, count_u, count_t, full]):
        counts = counts + flag(lane[:1] == k) * value
    spot_of, below_r = ordered()
    order = jnp.zeros((1, NB), jnp.float32)
    for a in range(RB):
        order = order + flag(spot_of[a : a + 1] == node[:1]) * a

    def beside(x, y):
        return jnp.concatenate([x[:, :HALF], y[:, :HALF], jnp.zeros((1, NB - 2 * HALF), jnp.float32)], axis=1)

    order = beside(order, below_r)
    starts = beside(below_l, below_u)
    lists = jnp.concatenate([list_l, list_u, list_t, pack_l, pack_u, counts, order, starts], axis=0)
    out[0:8, :] = rows.astype(jnp.int32)
    out[8:16, :] = lists.astype(jnp.int32)


def tables(pattern, levels, widths, after):
    return pl.pallas_call(
        table_kernel,
        out_shape=jax.ShapeDtypeStruct((16, NB), jnp.int32),
        in_specs=[VMEM, VMEM, VMEM, VMEM],
        out_specs=VMEM,
        cost_estimate=cost(4),
    )(pattern, levels.reshape(1, NB), widths.reshape(1, NB), after)


def first_kernel(pattern, levels, blocks, out, token, lists, places, held, sem, sems_in, sems_out):
    p = lax.axis_index("prow")
    q = lax.axis_index("pcol")
    lev = levels[...].astype(jnp.float32)
    i, j = iota((NB, NB), 0), iota((NB, NB), 1)
    lev_col = jnp.sum(jnp.where(i == j, lev, 0.0), axis=1, keepdims=True)
    near = flag(pattern[...] > 0) * flag(lev < lev_col) * flag((lev_col < 2.5) | (lev > 2.5))
    lane, sub = iota((RB, NB), 1), iota((RB, NB), 0)
    sel = dot(flag(lane == sub * PR + p), near) * flag((lane & (PC - 1)) == q)
    spot = (sub * CB + (lane >> 3)).astype(jnp.float32)
    found = listing(sel, ranks(sel), spot, 32)
    number = jnp.minimum(count(sel), CAP_L)
    rows = jnp.where(sub == 0, found, number + 0.0 * spot)
    lists[...] = rows.astype(jnp.int32)
    move = pltpu.make_async_copy(lists, places, sem)
    move.start()
    token[...] = jnp.zeros_like(token)
    move.wait()
    total = places[1, 0]

    def load(t):
        n = places[0, t]
        return pltpu.make_async_copy(blocks.at[n >> 4, n & (CB - 1)], held.at[t], sems_in.at[t])

    def store(t):
        return pltpu.make_async_copy(held.at[t], out.at[t], sems_out.at[t])

    pl.loop(0, total)(lambda t: load(t).start())

    @pl.loop(0, total)
    def _(t):
        load(t).wait()
        store(t).start()

    pl.loop(0, total)(lambda t: store(t).wait())


def first(pattern, levels, blocks):
    return pl.pallas_call(
        first_kernel,
        out_shape=(
            jax.ShapeDtypeStruct((CAP_L, W, W), jnp.float32),
            jax.ShapeDtypeStruct((1, NB), jnp.int32),
        ),
        in_specs=[VMEM, VMEM, HBM],
        out_specs=(HBM, VMEM),
        scratch_shapes=[
            pltpu.VMEM((RB, NB), jnp.int32),
            pltpu.SMEM((RB, NB), jnp.int32),
            pltpu.VMEM((CAP_L, W, W), jnp.float32),
            pltpu.SemaphoreType.DMA,
            pltpu.SemaphoreType.DMA((CAP_L,)),
            pltpu.SemaphoreType.DMA((CAP_L,)),
        ],
        compiler_params=pltpu.CompilerParams(vmem_limit_bytes=ROOM),
        cost_estimate=cost(4),
    )(pattern, levels.reshape(1, NB), blocks)


def pack_kernel(where, cap, with_far, table, blocks, _, *rest):
    rest = list(rest)
    lower = rest.pop(0) if with_far else None
    out, extra, held, sems_in, sems_out = rest[:5]
    count = table[COUNTS, where]
    row = PACK_L + where

    def load(t):
        n = table[row, t]
        return pltpu.make_async_copy(blocks.at[n >> 4, n & (CB - 1)], held.at[t], sems_in.at[t])

    def store(t):
        return pltpu.make_async_copy(held.at[t], out.at[t], sems_out.at[t])

    def load_far(t):
        n = table[LIST_T, t]
        return pltpu.make_async_copy(lower.at[n >> 4, n & (CB - 1)], extra.at[t], rest[5].at[t])

    pl.loop(0, count)(lambda t: load(t).start())
    if with_far:
        pl.loop(0, table[COUNTS, 2])(lambda t: load_far(t).start())
    else:
        extra[...] = jnp.zeros_like(extra)

    @pl.loop(0, count)
    def _(t):
        load(t).wait()
        store(t).start()

    pl.loop(0, count)(lambda t: store(t).wait())
    if with_far:
        pl.loop(0, table[COUNTS, 2])(lambda t: load_far(t).wait())


def pack(where, cap, table, blocks, after, lower=None):
    with_far = lower is not None
    extra = (LIST, W, W) if with_far else (HS, W)
    scratch = [
        pltpu.VMEM((cap, W, W), jnp.float32),
        pltpu.SemaphoreType.DMA((cap,)),
        pltpu.SemaphoreType.DMA((cap,)),
    ]
    if with_far:
        scratch.append(pltpu.SemaphoreType.DMA((LIST,)))
    return pl.pallas_call(
        lambda *refs: pack_kernel(where, cap, with_far, *refs),
        out_shape=(
            jax.ShapeDtypeStruct((cap, W, W), jnp.float32),
            jax.ShapeDtypeStruct(extra, jnp.float32),
        ),
        in_specs=[SMEM, HBM, HBM] + ([HBM] if with_far else []),
        out_specs=(HBM, VMEM),
        scratch_shapes=scratch,
        compiler_params=pltpu.CompilerParams(vmem_limit_bytes=ROOM),
        cost_estimate=cost(4),
    )(table, blocks, after, *([lower] if with_far else []))


def level_kernel(level, copies, kind, turn, both, sliced, group, fetch, table, known, right, inverse, panel, less, *rest):
    rest = list(rest)
    inverse_2 = rest.pop(0) if turn else None
    out = rest.pop(0)
    out_2 = rest.pop(0) if turn else None
    blocks = rest.pop(0) if fetch else panel
    sums = rest.pop(0)
    sems = rest.pop(0) if fetch else None
    p = lax.axis_index("prow")
    row = LIST_U if kind else LIST_L
    e0, e1 = table[STARTS, kind * HALF + level], table[STARTS, kind * HALF + level + 1]
    r0, r1 = table[ROWS, HALF + level], table[ROWS, HALF + level + 1]
    whole = table[STARTS, kind * HALF + LEVELS]

    def copy(t):
        return pltpu.make_async_copy(panel.at[table[row, t] >> 10], blocks.at[t], sems.at[t])

    if fetch:
        pl.loop(e0, e1)(lambda t: copy(t).start())
        pl.loop(0, e0)(lambda t: copy(t).start())
        pl.loop(e1, whole)(lambda t: copy(t).start())

    shift = lax.axis_index("pcol") * HS
    for a in range(RB):
        mine = right[a, pl.ds(shift, HS)] if sliced else right[a]
        if less is not None and not both:
            parts = [less[k, a] for k in range(PC)]
            while len(parts) > 1:
                parts = [x + y for x, y in zip(parts[::2], parts[1::2])]
            mine = mine - parts[0]
        sums[a] = mine
        old = known[p, a] if known is not None else jnp.zeros((HS, W), jnp.float32)
        for r in range(copies):
            if both:
                out[r, 0, a] = less[a]
                out[r, 1, a] = old
            else:
                out[r, a] = old if not turn else jnp.zeros((HS, W), jnp.float32)
        if turn:
            out_2[a] = old

    if panel is not None:
        @pl.loop(0, (e1 - e0 + group - 1) // group)
        def _(g):
            terms = []
            for u in range(group):
                t = e0 + g * group + u
                there = t < e1

                if fetch:
                    @pl.when(there)
                    def _():
                        copy(t).wait()

                t = jnp.minimum(t, e1 - 1)
                node = (table[row, t] >> 3) & (NB - 1)
                x = known[node & (PR - 1), node >> 4] * jnp.where(there, 1.0, 0.0)
                terms.append((table[row, t] & (RB - 1), dot3(x, blocks[t if kind else table[row, t] >> 10])))
            for a, term in terms:
                sums[a] -= term

    lane = iota((HS, W), 1)

    @pl.loop(0, (r1 - r0 + GROUP - 1) >> 2)
    def _(g):
        fresh = []
        for u in range(GROUP):
            r = r0 + g * GROUP + u
            there = r < r1
            a = table[ROWS, jnp.minimum(r, r1 - 1)]

            fresh.append((there, a, jnp.where(lane < table[a, WIDTH], dot3(sums[a], inverse[a]), 0.0)))
        if turn:
            later = [jnp.where(lane < table[a, WIDTH], dot3(x, inverse_2[a]), 0.0) for _, a, x in fresh]
            for there, a, x in fresh:
                out_2[a] = x
            fresh = [(there, a, x) for (there, a, _), x in zip(fresh, later)]
        for there, a, x in fresh:
            @pl.when(there)
            def _():
                for r in range(copies):
                    if both:
                        out[r, 1, a] = x
                    else:
                        out[r, a] = x

    if fetch:
        pl.loop(0, e0)(lambda t: copy(t).wait())
        pl.loop(e1, whole)(lambda t: copy(t).wait())


def level_step(
    level, copies, kind, table, known, right, inverse, panel, *,
    turn=None, both=False, sliced=False, after=None, less=None, group=GROUP, fetch=False,
):
    ins, specs = [table], [SMEM]
    given = ((known, VMEM), (right, VMEM), (inverse, VMEM), (panel, HBM if fetch else VMEM), (less, VMEM))
    for x, spec in given + ((turn, VMEM), (after, HBM)):
        if x is not None:
            ins.append(x)
            specs.append(spec)

    def kernel(*refs):
        refs = list(refs)
        if after is not None:
            refs.pop(len(ins) - 1)
        args = [refs.pop(0)] + [refs.pop(0) if x is not None else None for x, _ in given]
        level_kernel(level, copies, kind, turn is not None, both, sliced, group, fetch, *args, *refs)

    small = (RB, HS, W)
    shapes = [(copies, 2) + small if both else (copies,) + small]
    if turn is not None:
        shapes.append(small)
    if fetch:
        shapes.append((LIST, W, W))
    scratch = []
    if kind == 1 and not both:
        shapes.append(small)
    else:
        scratch.append(pltpu.VMEM(small, jnp.float32))
    if fetch:
        scratch.append(pltpu.SemaphoreType.DMA((LIST,)))
    out = pl.pallas_call(
        kernel,
        out_shape=[jax.ShapeDtypeStruct(x, jnp.float32) for x in shapes],
        in_specs=specs,
        out_specs=[VMEM] * len(shapes),
        scratch_shapes=scratch,
        compiler_params=pltpu.CompilerParams(vmem_limit_bytes=ROOM),
        cost_estimate=cost(8),
    )(*ins)
    return out if len(out) > 1 else out[0]


def across_kernel(table, known, blocks, out):
    count = table[COUNTS, 2]
    out[...] = jnp.zeros_like(out)

    @pl.loop(0, (count + GROUP - 1) >> 2)
    def _(g):
        terms = []
        for u in range(GROUP):
            t = g * GROUP + u
            there = t < count
            t = jnp.minimum(t, count - 1)
            n = table[LIST_T, t]
            c = n & (CB - 1)
            x = known[:, c & 1, c >> 1].reshape(NRHS, W) * jnp.where(there, 1.0, 0.0)
            terms.append((n >> 4, dot3(x, blocks[t]).reshape(PC, HS, W)))
        for a, term in terms:
            out[:, a] += term


def across(table, known, blocks):
    return pl.pallas_call(
        across_kernel,
        out_shape=jax.ShapeDtypeStruct((PC, RB, HS, W), jnp.float32),
        in_specs=[SMEM, VMEM, VMEM],
        out_specs=VMEM,
        compiler_params=pltpu.CompilerParams(vmem_limit_bytes=ROOM),
        cost_estimate=cost(8),
    )(table, known, blocks)


def local(rhs, lower, upper, lower_inverse, upper_inverse, pattern, levels, widths):
    right = rhs.reshape(RB, NRHS, W)
    lower_blocks = lower.reshape(RB, CB, W, W)
    upper_blocks = upper.reshape(RB, CB, W, W)
    lower_inv = lower_inverse.reshape(RB, W, W)
    upper_inv = upper_inverse.reshape(RB, W, W)
    packed_l, token = first(pattern, levels, lower_blocks)
    table = tables(pattern, levels, widths, token)
    swap = lambda x: lax.all_to_all(x, "prow", 0, 0)

    panel_l = lax.all_gather(packed_l, "pcol", tiled=True)
    leaves = level_step(0, PR, 0, table, None, right, lower_inv, None, sliced=True)
    known = swap(leaves)
    packed_u, far_blocks = pack(1, CAP_U, table, upper_blocks, known[0, 0], lower_blocks)
    panel_u = lax.all_gather(packed_u, "pcol", tiled=True)
    for level in (1, 2):
        known = swap(level_step(level, PR, 0, table, known, right, lower_inv, panel_l, sliced=True, group=8))
    split = known.reshape(2, PC, RB, HS, W).transpose(1, 0, 2, 3, 4)
    columns = lax.all_to_all(split, "pcol", 0, 0)
    sums = lax.all_to_all(across(table, columns, far_blocks), "pcol", 0, 0)
    step = lambda level, turn=None: level_step(
        level, PR, 0, table, known, right, lower_inv, panel_l, turn=turn, sliced=True, less=sums
    )
    for level in range(3, LEVELS - 1):
        known = swap(step(level))
    state, forward = step(LEVELS - 1, upper_inv)
    known = swap(state)
    state, held, left = level_step(4, PR, 1, table, known, forward, upper_inv, panel_u, group=8, fetch=True)
    for level in range(3, 0, -1):
        known = swap(state)
        state, left = level_step(level, PR, 1, table, known, left, upper_inv, held, group=8)
    known = swap(state)
    state = level_step(0, PC, 1, table, known, left, upper_inv, held, both=True, less=forward, group=8)
    full = lax.all_to_all(state, "pcol", 0, 0)
    shape = rhs.shape
    whole = lambda x: x.transpose(1, 0, 2, 3).reshape(shape)
    args = (rhs, lower, upper, lower_inverse, upper_inverse, pattern, levels, widths)
    done = lax.while_loop(
        lambda c: c[2] > 0,
        lambda c: general(*args) + (jnp.int32(0),),
        (whole(full[:, 0]), whole(full[:, 1]), table[COUNTS, 3]),
    )
    return done[0], done[1]


def solution(mesh):
    in_specs = (
        P(None, "prow", None, None),
        P(None, "prow", None, "pcol", None, None),
        P(None, "prow", None, "pcol", None, None),
        P(None, "prow", None, None),
        P(None, "prow", None, None),
        P(),
        P(),
        P(),
    )
    out_specs = (P(None, "prow", None, None), P(None, "prow", None, None))
    return jax.shard_map(local, mesh=mesh, in_specs=in_specs, out_specs=out_specs, check_vma=False)
```

```python
import jax
import jax.numpy as jnp
from jax import lax
from jax.experimental import pallas as pl
from jax.experimental.pallas import tpu as pltpu
from jax.sharding import PartitionSpec as P

LEVELS = 6
W = 128
NRHS = 64
NB = 128
RB = 8
CB = 16
PR = 16
PC = 8
HS = NRHS // PC
CAP_L = 10
CAP_U = 28
LIST = 64
GROUP = 4
HBM = pl.BlockSpec(memory_space=pl.ANY)
ROOM = 44 * 1024 * 1024
SMEM = pl.BlockSpec(memory_space=pltpu.SMEM)
VMEM = pl.BlockSpec(memory_space=pltpu.VMEM)
WIDTH = 0
LIST_L, LIST_U, LIST_T, PACK_L, PACK_U, COUNTS, ROWS, STARTS = range(8, 16)
HALF = 16


def spread(value, axis, source):
    kept = jnp.where(lax.axis_index(axis) == source, value, 0).astype(value.dtype)
    return lax.psum(kept, axis)


def apply_inverse(inverse, right):
    return jnp.einsum("akl,ahl->ahk", inverse, right, precision=lax.Precision.HIGHEST)


def solve_levels(blocks, inverse, right, valid, row_levels, mask, rising):
    prow_count = lax.axis_size("prow")
    pcol_count = lax.axis_size("pcol")
    column = lax.axis_index("pcol")
    ratio = prow_count // pcol_count
    masked = blocks * mask[:, :, None, None]
    row_state = jnp.zeros(right.shape, jnp.float32)
    col_state = jnp.zeros((masked.shape[1],) + right.shape[1:], jnp.float32)
    order = list(range(LEVELS)) if rising else list(range(LEVELS - 1, -1, -1))
    for place, level in enumerate(order):
        partial_sum = jnp.einsum(
            "ackl,chl->ahk", masked, col_state, precision=lax.Precision.HIGHEST
        )
        total = lax.psum(partial_sum, "pcol")
        fresh = apply_inverse(inverse, right - total) * valid
        current = (row_levels == level)[:, None, None]
        row_state = jnp.where(current, fresh, row_state)
        if place + 1 < LEVELS:
            pieces = []
            for offset in range(ratio):
                pieces.append(spread(row_state, "prow", column + offset * pcol_count))
            stacked = jnp.stack(pieces, axis=1)
            col_state = stacked.reshape((-1,) + right.shape[1:])
    return row_state


def general(rhs, lower, upper, lower_inverse, upper_inverse, pattern, levels, widths):
    prow_count = lax.axis_size("prow")
    pcol_count = lax.axis_size("pcol")
    row_index = lax.axis_index("prow")
    col_index = lax.axis_index("pcol")
    row_blocks = rhs.shape[0]
    col_blocks = lower.shape[2]
    width = rhs.shape[3]
    right = rhs.reshape(row_blocks, rhs.shape[2], width)
    lower_local = lower.reshape(row_blocks, col_blocks, width, width)
    upper_local = upper.reshape(row_blocks, col_blocks, width, width)
    lower_inv = lower_inverse.reshape(row_blocks, width, width)
    upper_inv = upper_inverse.reshape(row_blocks, width, width)
    row_levels = lax.dynamic_index_in_dim(
        levels.reshape(row_blocks, prow_count), row_index, 1, keepdims=False
    )
    col_levels = lax.dynamic_index_in_dim(
        levels.reshape(col_blocks, pcol_count), col_index, 1, keepdims=False
    )
    row_widths = lax.dynamic_index_in_dim(
        widths.reshape(row_blocks, prow_count), row_index, 1, keepdims=False
    )
    grid = pattern.reshape(row_blocks, prow_count, col_blocks, pcol_count)
    grid = lax.dynamic_index_in_dim(grid, row_index, 1, keepdims=False)
    grid = lax.dynamic_index_in_dim(grid, col_index, 2, keepdims=False).astype(jnp.float32)
    valid = (jnp.arange(width)[None, :] < row_widths[:, None]).astype(jnp.float32)[:, None, :]
    below = grid * (col_levels[None, :] < row_levels[:, None]).astype(jnp.float32)
    above = grid * (col_levels[None, :] > row_levels[:, None]).astype(jnp.float32)
    forward = solve_levels(lower_local, lower_inv, right, valid, row_levels, below, True)
    solution = solve_levels(upper_local, upper_inv, forward, valid, row_levels, above, False)
    shape = rhs.shape
    return (forward.reshape(shape), solution.reshape(shape))


def dot3(x, w):
    m, n = x.shape[0], w.shape[0]
    xh = x.astype(jnp.bfloat16).astype(jnp.float32)
    xs = jnp.concatenate([xh, x - xh], axis=0).astype(jnp.bfloat16)
    wh = w.astype(jnp.bfloat16)
    wl = (w - wh.astype(jnp.float32)).astype(jnp.bfloat16)
    ws = jnp.concatenate([wh, wl], axis=0)
    y = lax.dot_general(xs, ws, (((1,), (1,)), ((), ())), preferred_element_type=jnp.float32)
    return (y[m:, n:] + y[:m, n:]) + (y[m:, :n] + y[:m, :n])


def iota(shape, dim):
    return lax.broadcasted_iota(jnp.int32, shape, dim)


def cost(mib):
    return pl.CostEstimate(flops=0, bytes_accessed=mib << 20, transcendentals=0)


def flag(cond):
    return jnp.where(cond, 1.0, 0.0)


def dot(x, y):
    return jnp.dot(x, y, preferred_element_type=jnp.float32)


def ranks(sel):
    i, j = iota((NB, NB), 0), iota((NB, NB), 1)
    same = flag((i & (PC - 1)) == (j & (PC - 1)))
    total = jnp.zeros((1, NB), jnp.float32)
    rows = []
    for a in range(RB):
        rows.append(total)
        total = total + sel[a : a + 1]
    return dot(jnp.concatenate(rows, axis=0), same) + dot(sel, same * flag(i < j))


def listing(sel, place, value, size):
    t = iota((size, NB), 0).astype(jnp.float32)
    held = jnp.zeros((size, NB), jnp.float32)
    for a in range(RB):
        hit = flag(t == place[a : a + 1]) * sel[a : a + 1]
        held = held + hit * value[a : a + 1]
    ones = jnp.ones((RB, NB), jnp.float32)
    row = lax.dot_general(ones, held, (((1,), (1,)), ((), ())), preferred_element_type=jnp.float32)[:1]
    if size < NB:
        row = jnp.concatenate([row, jnp.zeros((1, NB - size), jnp.float32)], axis=1)
    return row


def count(sel):
    return jnp.sum(jnp.sum(sel, axis=1, keepdims=True), axis=0, keepdims=True)


def table_kernel(pattern, levels, widths, _, out):
    p = lax.axis_index("prow")
    q = lax.axis_index("pcol")
    lev = levels[...].astype(jnp.float32)
    wid = widths[...].astype(jnp.float32)
    i = iota((NB, NB), 0)
    j = iota((NB, NB), 1)
    lev_col = jnp.sum(jnp.where(i == j, lev, 0.0), axis=1, keepdims=True)
    linked = flag(pattern[...] > 0)
    low = linked * flag(lev < lev_col)
    high = linked * flag(lev > lev_col)
    near = low * flag((lev_col < 2.5) | (lev > 2.5))
    far = low - near
    same = flag((i & (PC - 1)) == (j & (PC - 1)))
    ahead = flag(i < j)

    by_row = flag((iota((PR, NB), 1) & (PR - 1)) == iota((PR, NB), 0))

    def over(full, cap):
        rows = dot(by_row, full)
        most = jnp.max(jnp.max(dot(rows, same), axis=1, keepdims=True), axis=0, keepdims=True)
        listed = jnp.max(jnp.sum(rows, axis=1, keepdims=True), axis=0, keepdims=True)
        return flag((most > cap) | (listed > LIST))

    def over_far():
        rows = dot(dot(by_row, far), same)
        return flag(jnp.max(jnp.max(rows, axis=1, keepdims=True), axis=0, keepdims=True) > LIST)

    full = jnp.maximum(jnp.maximum(over(near, CAP_L), over(high, CAP_U)), over_far())

    lane = iota((RB, NB), 1)
    sub = iota((RB, NB), 0)
    mine = flag(lane == sub * PR + p)
    row_lev = jnp.sum(mine * lev, axis=1, keepdims=True)
    row_wid = jnp.sum(mine * wid, axis=1, keepdims=True)
    col = lane & (PC - 1)
    own = flag(col == q)
    node = lane.astype(jnp.float32)
    spot = (sub * CB + (lane >> 3)).astype(jnp.float32)

    def ordered():
        start = jnp.zeros((RB, 1), jnp.float32)
        below = jnp.zeros((1, NB), jnp.float32)
        index = iota((RB, 1), 0)
        for a in range(RB):
            first = (row_lev[a : a + 1] < row_lev) | ((row_lev[a : a + 1] == row_lev) & (index > a))
            start = start + flag(first)
            below = below + flag(row_lev[a : a + 1] < node[:1])
        return start, below

    def by_step(sel, step):
        parts = jnp.concatenate([sel * flag(step == k) for k in range(LEVELS)], axis=0)
        size = RB * LEVELS
        earlier = flag(iota((size, size), 0) > iota((size, size), 1))
        base = jnp.sum(dot(earlier, parts), axis=1, keepdims=True)
        spread = parts * (dot(parts, ahead) + base)
        place = jnp.zeros((RB, NB), jnp.float32)
        below = jnp.zeros((1, NB), jnp.float32)
        for k in range(LEVELS):
            place = place + spread[RB * k : RB * (k + 1)]
            below = below + flag(node[:1] == k) * base[RB * k : RB * k + 1]
        return place, below + flag(node[:1] == LEVELS) * count(sel)

    def panel(sel, cap, step):
        rank = ranks(sel)
        place, below = by_step(sel, step)
        slot = (col * cap).astype(jnp.float32) + jnp.minimum(rank, cap - 1.0)
        listed = listing(sel, place, slot, LIST) * (NB * RB) + listing(sel, place, node, LIST) * RB
        listed = listed + listing(sel, place, sub.astype(jnp.float32), LIST)
        packed = listing(sel * own, rank, spot, 32)
        return jnp.minimum(below, LIST), listed, packed, jnp.minimum(count(sel * own), cap)

    near_p = dot(mine, near)
    high_p = dot(mine, high)
    far_p = dot(mine, far)
    top = jnp.where(row_lev > 2.5, row_lev, jnp.where(row_lev > 0.5, 4.0, 3.0))
    fourth = jnp.minimum(jnp.maximum(row_lev, 2.0), 3.0)
    third = jnp.minimum(jnp.maximum(row_lev, 1.0), 2.0)
    down = jnp.where(lev > 4.5, top, jnp.where(lev > 3.5, fourth, jnp.where(lev > 2.5, third, row_lev)))
    below_l, list_l, pack_l, count_l = panel(near_p, CAP_L, row_lev + 0.0 * node)
    below_u, list_u, pack_u, count_u = panel(high_p, CAP_U, down)
    list_t = listing(far_p * own, ranks(far_p), spot, NB)
    count_t = jnp.minimum(count(far_p * own), LIST)
    rows = flag(lane == WIDTH) * row_wid
    counts = jnp.zeros((1, NB), jnp.float32)
    for k, value in enumerate([count_l, count_u, count_t, full]):
        counts = counts + flag(lane[:1] == k) * value
    spot_of, below_r = ordered()
    order = jnp.zeros((1, NB), jnp.float32)
    for a in range(RB):
        order = order + flag(spot_of[a : a + 1] == node[:1]) * a

    def beside(x, y):
        return jnp.concatenate([x[:, :HALF], y[:, :HALF], jnp.zeros((1, NB - 2 * HALF), jnp.float32)], axis=1)

    order = beside(order, below_r)
    starts = beside(below_l, below_u)
    lists = jnp.concatenate([list_l, list_u, list_t, pack_l, pack_u, counts, order, starts], axis=0)
    out[0:8, :] = rows.astype(jnp.int32)
    out[8:16, :] = lists.astype(jnp.int32)


def tables(pattern, levels, widths, after):
    return pl.pallas_call(
        table_kernel,
        out_shape=jax.ShapeDtypeStruct((16, NB), jnp.int32),
        in_specs=[VMEM, VMEM, VMEM, VMEM],
        out_specs=VMEM,
        cost_estimate=cost(4),
    )(pattern, levels.reshape(1, NB), widths.reshape(1, NB), after)


def first_kernel(pattern, levels, blocks, out, token, lists, places, held, sem, sems_in, sems_out):
    p = lax.axis_index("prow")
    q = lax.axis_index("pcol")
    lev = levels[...].astype(jnp.float32)
    lane, sub = iota((RB, NB), 1), iota((RB, NB), 0)
    mine = flag(lane == sub * PR + p)
    row_lev = jnp.sum(mine * lev, axis=1, keepdims=True)
    wanted = flag(lev < row_lev) * flag((row_lev < 2.5) | (lev > 2.5)) * flag((lane & (PC - 1)) == q)
    sel = dot(mine, flag(pattern[...] > 0)) * wanted
    spot = (sub * CB + (lane >> 3)).astype(jnp.float32)
    found = listing(sel, ranks(sel), spot, 32)
    number = jnp.minimum(count(sel), CAP_L)
    rows = jnp.where(sub == 0, found, number + 0.0 * spot)
    lists[...] = rows.astype(jnp.int32)
    move = pltpu.make_async_copy(lists, places, sem)
    move.start()
    token[...] = jnp.zeros_like(token)
    move.wait()
    total = places[1, 0]

    def load(t):
        n = places[0, t]
        return pltpu.make_async_copy(blocks.at[n >> 4, n & (CB - 1)], held.at[t], sems_in.at[t])

    def store(t):
        return pltpu.make_async_copy(held.at[t], out.at[t], sems_out.at[t])

    pl.loop(0, total)(lambda t: load(t).start())

    @pl.loop(0, total)
    def _(t):
        load(t).wait()
        store(t).start()

    pl.loop(0, total)(lambda t: store(t).wait())


def first(pattern, levels, blocks):
    return pl.pallas_call(
        first_kernel,
        out_shape=(
            jax.ShapeDtypeStruct((CAP_L, W, W), jnp.float32),
            jax.ShapeDtypeStruct((1, NB), jnp.int32),
        ),
        in_specs=[VMEM, VMEM, HBM],
        out_specs=(HBM, VMEM),
        scratch_shapes=[
            pltpu.VMEM((RB, NB), jnp.int32),
            pltpu.SMEM((RB, NB), jnp.int32),
            pltpu.VMEM((CAP_L, W, W), jnp.float32),
            pltpu.SemaphoreType.DMA,
            pltpu.SemaphoreType.DMA((CAP_L,)),
            pltpu.SemaphoreType.DMA((CAP_L,)),
        ],
        compiler_params=pltpu.CompilerParams(vmem_limit_bytes=ROOM),
        cost_estimate=cost(4),
    )(pattern, levels.reshape(1, NB), blocks)


def pack_kernel(where, cap, with_far, table, blocks, _, *rest):
    rest = list(rest)
    lower = rest.pop(0) if with_far else None
    out, extra, held, sems_in, sems_out = rest[:5]
    count = table[COUNTS, where]
    row = PACK_L + where

    def load(t):
        n = table[row, t]
        return pltpu.make_async_copy(blocks.at[n >> 4, n & (CB - 1)], held.at[t], sems_in.at[t])

    def store(t):
        return pltpu.make_async_copy(held.at[t], out.at[t], sems_out.at[t])

    def load_far(t):
        n = table[LIST_T, t]
        return pltpu.make_async_copy(lower.at[n >> 4, n & (CB - 1)], extra.at[t], rest[5].at[t])

    pl.loop(0, count)(lambda t: load(t).start())
    if with_far:
        pl.loop(0, table[COUNTS, 2])(lambda t: load_far(t).start())
    else:
        extra[...] = jnp.zeros_like(extra)

    @pl.loop(0, count)
    def _(t):
        load(t).wait()
        store(t).start()

    pl.loop(0, count)(lambda t: store(t).wait())
    if with_far:
        pl.loop(0, table[COUNTS, 2])(lambda t: load_far(t).wait())


def pack(where, cap, table, blocks, after, lower=None):
    with_far = lower is not None
    extra = (LIST, W, W) if with_far else (HS, W)
    scratch = [
        pltpu.VMEM((cap, W, W), jnp.float32),
        pltpu.SemaphoreType.DMA((cap,)),
        pltpu.SemaphoreType.DMA((cap,)),
    ]
    if with_far:
        scratch.append(pltpu.SemaphoreType.DMA((LIST,)))
    return pl.pallas_call(
        lambda *refs: pack_kernel(where, cap, with_far, *refs),
        out_shape=(
            jax.ShapeDtypeStruct((cap, W, W), jnp.float32),
            jax.ShapeDtypeStruct(extra, jnp.float32),
        ),
        in_specs=[SMEM, HBM, HBM] + ([HBM] if with_far else []),
        out_specs=(HBM, VMEM),
        scratch_shapes=scratch,
        compiler_params=pltpu.CompilerParams(vmem_limit_bytes=ROOM),
        cost_estimate=cost(4),
    )(table, blocks, after, *([lower] if with_far else []))


def level_kernel(level, copies, kind, turn, both, sliced, group, fetch, table, known, right, inverse, panel, less, *rest):
    rest = list(rest)
    inverse_2 = rest.pop(0) if turn else None
    out = rest.pop(0)
    out_2 = rest.pop(0) if turn else None
    blocks = rest.pop(0) if fetch else panel
    sums = rest.pop(0)
    sems = rest.pop(0) if fetch else None
    p = lax.axis_index("prow")
    row = LIST_U if kind else LIST_L
    e0, e1 = table[STARTS, kind * HALF + level], table[STARTS, kind * HALF + level + 1]
    r0, r1 = table[ROWS, HALF + level], table[ROWS, HALF + level + 1]
    whole = table[STARTS, kind * HALF + LEVELS]

    def copy(t):
        return pltpu.make_async_copy(panel.at[table[row, t] >> 10], blocks.at[t], sems.at[t])

    if fetch:
        pl.loop(e0, e1)(lambda t: copy(t).start())
        pl.loop(0, e0)(lambda t: copy(t).start())
        pl.loop(e1, whole)(lambda t: copy(t).start())

    shift = lax.axis_index("pcol") * HS
    for a in range(RB):
        mine = right[a, pl.ds(shift, HS)] if sliced else right[a]
        if less is not None and not both:
            parts = [less[k, a] for k in range(PC)]
            while len(parts) > 1:
                parts = [x + y for x, y in zip(parts[::2], parts[1::2])]
            mine = mine - parts[0]
        sums[a] = mine
        old = known[p, a] if known is not None else jnp.zeros((HS, W), jnp.float32)
        for r in range(copies):
            if both:
                out[r, 0, a] = less[a]
                out[r, 1, a] = old
            else:
                out[r, a] = old if not turn else jnp.zeros((HS, W), jnp.float32)
        if turn:
            out_2[a] = old

    if panel is not None:
        @pl.loop(0, (e1 - e0 + group - 1) // group)
        def _(g):
            terms = []
            for u in range(group):
                t = e0 + g * group + u
                there = t < e1

                if fetch:
                    @pl.when(there)
                    def _():
                        copy(t).wait()

                t = jnp.minimum(t, e1 - 1)
                node = (table[row, t] >> 3) & (NB - 1)
                x = known[node & (PR - 1), node >> 4] * jnp.where(there, 1.0, 0.0)
                terms.append((table[row, t] & (RB - 1), dot3(x, blocks[t if kind else table[row, t] >> 10])))
            for a, term in terms:
                sums[a] -= term

    lane = iota((HS, W), 1)

    @pl.loop(0, (r1 - r0 + GROUP - 1) >> 2)
    def _(g):
        fresh = []
        for u in range(GROUP):
            r = r0 + g * GROUP + u
            there = r < r1
            a = table[ROWS, jnp.minimum(r, r1 - 1)]

            fresh.append((there, a, jnp.where(lane < table[a, WIDTH], dot3(sums[a], inverse[a]), 0.0)))
        if turn:
            later = [jnp.where(lane < table[a, WIDTH], dot3(x, inverse_2[a]), 0.0) for _, a, x in fresh]
            for there, a, x in fresh:
                out_2[a] = x
            fresh = [(there, a, x) for (there, a, _), x in zip(fresh, later)]
        for there, a, x in fresh:
            @pl.when(there)
            def _():
                for r in range(copies):
                    if both:
                        out[r, 1, a] = x
                    else:
                        out[r, a] = x

    if fetch:
        pl.loop(0, e0)(lambda t: copy(t).wait())
        pl.loop(e1, whole)(lambda t: copy(t).wait())


def level_step(
    level, copies, kind, table, known, right, inverse, panel, *,
    turn=None, both=False, sliced=False, after=None, less=None, group=GROUP, fetch=False,
):
    ins, specs = [table], [SMEM]
    given = ((known, VMEM), (right, VMEM), (inverse, VMEM), (panel, HBM if fetch else VMEM), (less, VMEM))
    for x, spec in given + ((turn, VMEM), (after, HBM)):
        if x is not None:
            ins.append(x)
            specs.append(spec)

    def kernel(*refs):
        refs = list(refs)
        if after is not None:
            refs.pop(len(ins) - 1)
        args = [refs.pop(0)] + [refs.pop(0) if x is not None else None for x, _ in given]
        level_kernel(level, copies, kind, turn is not None, both, sliced, group, fetch, *args, *refs)

    small = (RB, HS, W)
    shapes = [(copies, 2) + small if both else (copies,) + small]
    if turn is not None:
        shapes.append(small)
    if fetch:
        shapes.append((LIST, W, W))
    scratch = []
    if kind == 1 and not both:
        shapes.append(small)
    else:
        scratch.append(pltpu.VMEM(small, jnp.float32))
    if fetch:
        scratch.append(pltpu.SemaphoreType.DMA((LIST,)))
    out = pl.pallas_call(
        kernel,
        out_shape=[jax.ShapeDtypeStruct(x, jnp.float32) for x in shapes],
        in_specs=specs,
        out_specs=[VMEM] * len(shapes),
        scratch_shapes=scratch,
        compiler_params=pltpu.CompilerParams(vmem_limit_bytes=ROOM),
        cost_estimate=cost(8),
    )(*ins)
    return out if len(out) > 1 else out[0]


def across_kernel(table, known, blocks, out):
    count = table[COUNTS, 2]
    out[...] = jnp.zeros_like(out)

    @pl.loop(0, (count + GROUP - 1) >> 2)
    def _(g):
        terms = []
        for u in range(GROUP):
            t = g * GROUP + u
            there = t < count
            t = jnp.minimum(t, count - 1)
            n = table[LIST_T, t]
            c = n & (CB - 1)
            x = known[:, c & 1, c >> 1].reshape(NRHS, W) * jnp.where(there, 1.0, 0.0)
            terms.append((n >> 4, dot3(x, blocks[t]).reshape(PC, HS, W)))
        for a, term in terms:
            out[:, a] += term


def across(table, known, blocks):
    return pl.pallas_call(
        across_kernel,
        out_shape=jax.ShapeDtypeStruct((PC, RB, HS, W), jnp.float32),
        in_specs=[SMEM, VMEM, VMEM],
        out_specs=VMEM,
        compiler_params=pltpu.CompilerParams(vmem_limit_bytes=ROOM),
        cost_estimate=cost(8),
    )(table, known, blocks)


def local(rhs, lower, upper, lower_inverse, upper_inverse, pattern, levels, widths):
    right = rhs.reshape(RB, NRHS, W)
    lower_blocks = lower.reshape(RB, CB, W, W)
    upper_blocks = upper.reshape(RB, CB, W, W)
    lower_inv = lower_inverse.reshape(RB, W, W)
    upper_inv = upper_inverse.reshape(RB, W, W)
    packed_l, token = first(pattern, levels, lower_blocks)
    table = tables(pattern, levels, widths, token)
    swap = lambda x: lax.all_to_all(x, "prow", 0, 0)

    panel_l = lax.all_gather(packed_l, "pcol", tiled=True)
    leaves = level_step(0, PR, 0, table, None, right, lower_inv, None, sliced=True)
    known = swap(leaves)
    packed_u, far_blocks = pack(1, CAP_U, table, upper_blocks, known[0, 0], lower_blocks)
    panel_u = lax.all_gather(packed_u, "pcol", tiled=True)
    for level in (1, 2):
        known = swap(level_step(level, PR, 0, table, known, right, lower_inv, panel_l, sliced=True, group=8))
    split = known.reshape(2, PC, RB, HS, W).transpose(1, 0, 2, 3, 4)
    columns = lax.all_to_all(split, "pcol", 0, 0)
    sums = lax.all_to_all(across(table, columns, far_blocks), "pcol", 0, 0)
    step = lambda level, turn=None: level_step(
        level, PR, 0, table, known, right, lower_inv, panel_l, turn=turn, sliced=True, less=sums
    )
    for level in range(3, LEVELS - 1):
        known = swap(step(level))
    state, forward = step(LEVELS - 1, upper_inv)
    known = swap(state)
    state, held, left = level_step(4, PR, 1, table, known, forward, upper_inv, panel_u, group=8, fetch=True)
    for level in range(3, 0, -1):
        known = swap(state)
        state, left = level_step(level, PR, 1, table, known, left, upper_inv, held, group=8)
    known = swap(state)
    state = level_step(0, PC, 1, table, known, left, upper_inv, held, both=True, less=forward, group=8)
    full = lax.all_to_all(state, "pcol", 0, 0)
    shape = rhs.shape
    whole = lambda x: x.transpose(1, 0, 2, 3).reshape(shape)
    args = (rhs, lower, upper, lower_inverse, upper_inverse, pattern, levels, widths)
    done = lax.while_loop(
        lambda c: c[2] > 0,
        lambda c: general(*args) + (jnp.int32(0),),
        (whole(full[:, 0]), whole(full[:, 1]), table[COUNTS, 3]),
    )
    return done[0], done[1]


def solution(mesh):
    in_specs = (
        P(None, "prow", None, None),
        P(None, "prow", None, "pcol", None, None),
        P(None, "prow", None, "pcol", None, None),
        P(None, "prow", None, None),
        P(None, "prow", None, None),
        P(),
        P(),
        P(),
    )
    out_specs = (P(None, "prow", None, None), P(None, "prow", None, None))
    return jax.shard_map(local, mesh=mesh, in_specs=in_specs, out_specs=out_specs, check_vma=False)
```

```python
import jax
import jax.numpy as jnp
from jax import lax
from jax.experimental import pallas as pl
from jax.experimental.pallas import tpu as pltpu
from jax.sharding import PartitionSpec as P

LEVELS = 6
W = 128
NRHS = 64
NB = 128
RB = 8
CB = 16
PR = 16
PC = 8
HS = NRHS // PC
CAP_L = 10
CAP_U = 28
LIST = 64
GROUP = 4
HBM = pl.BlockSpec(memory_space=pl.ANY)
ROOM = 44 * 1024 * 1024
SMEM = pl.BlockSpec(memory_space=pltpu.SMEM)
VMEM = pl.BlockSpec(memory_space=pltpu.VMEM)
WIDTH = 0
LIST_L, LIST_U, LIST_T, PACK_L, PACK_U, COUNTS, ROWS, STARTS = range(8, 16)
HALF = 16


def spread(value, axis, source):
    kept = jnp.where(lax.axis_index(axis) == source, value, 0).astype(value.dtype)
    return lax.psum(kept, axis)


def apply_inverse(inverse, right):
    return jnp.einsum("akl,ahl->ahk", inverse, right, precision=lax.Precision.HIGHEST)


def solve_levels(blocks, inverse, right, valid, row_levels, mask, rising):
    prow_count = lax.axis_size("prow")
    pcol_count = lax.axis_size("pcol")
    column = lax.axis_index("pcol")
    ratio = prow_count // pcol_count
    masked = blocks * mask[:, :, None, None]
    row_state = jnp.zeros(right.shape, jnp.float32)
    col_state = jnp.zeros((masked.shape[1],) + right.shape[1:], jnp.float32)
    order = list(range(LEVELS)) if rising else list(range(LEVELS - 1, -1, -1))
    for place, level in enumerate(order):
        partial_sum = jnp.einsum(
            "ackl,chl->ahk", masked, col_state, precision=lax.Precision.HIGHEST
        )
        total = lax.psum(partial_sum, "pcol")
        fresh = apply_inverse(inverse, right - total) * valid
        current = (row_levels == level)[:, None, None]
        row_state = jnp.where(current, fresh, row_state)
        if place + 1 < LEVELS:
            pieces = []
            for offset in range(ratio):
                pieces.append(spread(row_state, "prow", column + offset * pcol_count))
            stacked = jnp.stack(pieces, axis=1)
            col_state = stacked.reshape((-1,) + right.shape[1:])
    return row_state


def general(rhs, lower, upper, lower_inverse, upper_inverse, pattern, levels, widths):
    prow_count = lax.axis_size("prow")
    pcol_count = lax.axis_size("pcol")
    row_index = lax.axis_index("prow")
    col_index = lax.axis_index("pcol")
    row_blocks = rhs.shape[0]
    col_blocks = lower.shape[2]
    width = rhs.shape[3]
    right = rhs.reshape(row_blocks, rhs.shape[2], width)
    lower_local = lower.reshape(row_blocks, col_blocks, width, width)
    upper_local = upper.reshape(row_blocks, col_blocks, width, width)
    lower_inv = lower_inverse.reshape(row_blocks, width, width)
    upper_inv = upper_inverse.reshape(row_blocks, width, width)
    row_levels = lax.dynamic_index_in_dim(
        levels.reshape(row_blocks, prow_count), row_index, 1, keepdims=False
    )
    col_levels = lax.dynamic_index_in_dim(
        levels.reshape(col_blocks, pcol_count), col_index, 1, keepdims=False
    )
    row_widths = lax.dynamic_index_in_dim(
        widths.reshape(row_blocks, prow_count), row_index, 1, keepdims=False
    )
    grid = pattern.reshape(row_blocks, prow_count, col_blocks, pcol_count)
    grid = lax.dynamic_index_in_dim(grid, row_index, 1, keepdims=False)
    grid = lax.dynamic_index_in_dim(grid, col_index, 2, keepdims=False).astype(jnp.float32)
    valid = (jnp.arange(width)[None, :] < row_widths[:, None]).astype(jnp.float32)[:, None, :]
    below = grid * (col_levels[None, :] < row_levels[:, None]).astype(jnp.float32)
    above = grid * (col_levels[None, :] > row_levels[:, None]).astype(jnp.float32)
    forward = solve_levels(lower_local, lower_inv, right, valid, row_levels, below, True)
    solution = solve_levels(upper_local, upper_inv, forward, valid, row_levels, above, False)
    shape = rhs.shape
    return (forward.reshape(shape), solution.reshape(shape))


def dot3(x, w):
    m, n = x.shape[0], w.shape[0]
    xh = x.astype(jnp.bfloat16).astype(jnp.float32)
    xs = jnp.concatenate([xh, x - xh], axis=0).astype(jnp.bfloat16)
    wh = w.astype(jnp.bfloat16)
    wl = (w - wh.astype(jnp.float32)).astype(jnp.bfloat16)
    ws = jnp.concatenate([wh, wl], axis=0)
    y = lax.dot_general(xs, ws, (((1,), (1,)), ((), ())), preferred_element_type=jnp.float32)
    return (y[m:, n:] + y[:m, n:]) + (y[m:, :n] + y[:m, :n])


def iota(shape, dim):
    return lax.broadcasted_iota(jnp.int32, shape, dim)


def cost(mib):
    return pl.CostEstimate(flops=0, bytes_accessed=mib << 20, transcendentals=0)


def flag(cond):
    return jnp.where(cond, 1.0, 0.0)


def dot(x, y):
    return jnp.dot(x, y, preferred_element_type=jnp.float32)


def ranks(sel):
    i, j = iota((NB, NB), 0), iota((NB, NB), 1)
    same = flag((i & (PC - 1)) == (j & (PC - 1)))
    total = jnp.zeros((1, NB), jnp.float32)
    rows = []
    for a in range(RB):
        rows.append(total)
        total = total + sel[a : a + 1]
    return dot(jnp.concatenate(rows, axis=0), same) + dot(sel, same * flag(i < j))


def listing(sel, place, value, size):
    t = iota((size, NB), 0).astype(jnp.float32)
    held = jnp.zeros((size, NB), jnp.float32)
    for a in range(RB):
        hit = flag(t == place[a : a + 1]) * sel[a : a + 1]
        held = held + hit * value[a : a + 1]
    ones = jnp.ones((RB, NB), jnp.float32)
    row = lax.dot_general(ones, held, (((1,), (1,)), ((), ())), preferred_element_type=jnp.float32)[:1]
    if size < NB:
        row = jnp.concatenate([row, jnp.zeros((1, NB - size), jnp.float32)], axis=1)
    return row


def count(sel):
    return jnp.sum(jnp.sum(sel, axis=1, keepdims=True), axis=0, keepdims=True)


def table_kernel(pattern, levels, widths, _, out):
    p = lax.axis_index("prow")
    q = lax.axis_index("pcol")
    lev = levels[...].astype(jnp.float32)
    wid = widths[...].astype(jnp.float32)
    i = iota((NB, NB), 0)
    j = iota((NB, NB), 1)
    lev_col = jnp.sum(jnp.where(i == j, lev, 0.0), axis=1, keepdims=True)
    linked = flag(pattern[...] > 0)
    low = linked * flag(lev < lev_col)
    high = linked * flag(lev > lev_col)
    near = low * flag((lev_col < 2.5) | (lev > 2.5))
    far = low - near
    same = flag((i & (PC - 1)) == (j & (PC - 1)))
    ahead = flag(i < j)

    by_row = flag((iota((PR, NB), 1) & (PR - 1)) == iota((PR, NB), 0))

    def over(full, cap):
        rows = dot(by_row, full)
        most = jnp.max(jnp.max(dot(rows, same), axis=1, keepdims=True), axis=0, keepdims=True)
        listed = jnp.max(jnp.sum(rows, axis=1, keepdims=True), axis=0, keepdims=True)
        return flag((most > cap) | (listed > LIST))

    def over_far():
        rows = dot(dot(by_row, far), same)
        return flag(jnp.max(jnp.max(rows, axis=1, keepdims=True), axis=0, keepdims=True) > LIST)

    full = jnp.maximum(jnp.maximum(over(near, CAP_L), over(high, CAP_U)), over_far())

    lane = iota((RB, NB), 1)
    sub = iota((RB, NB), 0)
    mine = flag(lane == sub * PR + p)
    row_lev = jnp.sum(mine * lev, axis=1, keepdims=True)
    row_wid = jnp.sum(mine * wid, axis=1, keepdims=True)
    col = lane & (PC - 1)
    own = flag(col == q)
    node = lane.astype(jnp.float32)
    spot = (sub * CB + (lane >> 3)).astype(jnp.float32)

    def ordered():
        start = jnp.zeros((RB, 1), jnp.float32)
        below = jnp.zeros((1, NB), jnp.float32)
        index = iota((RB, 1), 0)
        for a in range(RB):
            first = (row_lev[a : a + 1] < row_lev) | ((row_lev[a : a + 1] == row_lev) & (index > a))
            start = start + flag(first)
            below = below + flag(row_lev[a : a + 1] < node[:1])
        return start, below

    def by_step(sel, step):
        parts = jnp.concatenate([sel * flag(step == k) for k in range(LEVELS)], axis=0)
        size = RB * LEVELS
        earlier = flag(iota((size, size), 0) > iota((size, size), 1))
        base = jnp.sum(dot(earlier, parts), axis=1, keepdims=True)
        spread = parts * (dot(parts, ahead) + base)
        place = jnp.zeros((RB, NB), jnp.float32)
        below = jnp.zeros((1, NB), jnp.float32)
        for k in range(LEVELS):
            place = place + spread[RB * k : RB * (k + 1)]
            below = below + flag(node[:1] == k) * base[RB * k : RB * k + 1]
        return place, below + flag(node[:1] == LEVELS) * count(sel)

    def panel(sel, cap, step):
        rank = ranks(sel)
        place, below = by_step(sel, step)
        slot = (col * cap).astype(jnp.float32) + jnp.minimum(rank, cap - 1.0)
        listed = listing(sel, place, slot, LIST) * (NB * RB) + listing(sel, place, node, LIST) * RB
        listed = listed + listing(sel, place, sub.astype(jnp.float32), LIST)
        packed = listing(sel * own, rank, spot, 32)
        return jnp.minimum(below, LIST), listed, packed, jnp.minimum(count(sel * own), cap)

    near_p = dot(mine, near)
    high_p = dot(mine, high)
    far_p = dot(mine, far)
    top = jnp.where(row_lev > 2.5, row_lev, jnp.where(row_lev > 0.5, 4.0, 3.0))
    fourth = jnp.minimum(jnp.maximum(row_lev, 2.0), 3.0)
    third = jnp.minimum(jnp.maximum(row_lev, 1.0), 2.0)
    down = jnp.where(lev > 4.5, top, jnp.where(lev > 3.5, fourth, jnp.where(lev > 2.5, third, row_lev)))
    below_l, list_l, pack_l, count_l = panel(near_p, CAP_L, row_lev + 0.0 * node)
    below_u, list_u, pack_u, count_u = panel(high_p, CAP_U, down)
    list_t = listing(far_p * own, ranks(far_p), spot, NB)
    count_t = jnp.minimum(count(far_p * own), LIST)
    rows = flag(lane == WIDTH) * row_wid
    counts = jnp.zeros((1, NB), jnp.float32)
    for k, value in enumerate([count_l, count_u, count_t, full]):
        counts = counts + flag(lane[:1] == k) * value
    spot_of, below_r = ordered()
    order = jnp.zeros((1, NB), jnp.float32)
    for a in range(RB):
        order = order + flag(spot_of[a : a + 1] == node[:1]) * a

    def beside(x, y):
        return jnp.concatenate([x[:, :HALF], y[:, :HALF], jnp.zeros((1, NB - 2 * HALF), jnp.float32)], axis=1)

    order = beside(order, below_r)
    starts = beside(below_l, below_u)
    lists = jnp.concatenate([list_l, list_u, list_t, pack_l, pack_u, counts, order, starts], axis=0)
    out[0:8, :] = rows.astype(jnp.int32)
    out[8:16, :] = lists.astype(jnp.int32)


def tables(pattern, levels, widths, after):
    return pl.pallas_call(
        table_kernel,
        out_shape=jax.ShapeDtypeStruct((16, NB), jnp.int32),
        in_specs=[VMEM, VMEM, VMEM, VMEM],
        out_specs=VMEM,
        cost_estimate=cost(4),
    )(pattern, levels.reshape(1, NB), widths.reshape(1, NB), after)


def first_kernel(pattern, levels, blocks, out, token, lists, places, held, sem, sems_in, sems_out):
    p = lax.axis_index("prow")
    q = lax.axis_index("pcol")
    lev = levels[...].astype(jnp.float32)
    lane, sub = iota((RB, NB), 1), iota((RB, NB), 0)
    mine = flag(lane == sub * PR + p)
    row_lev = jnp.sum(mine * lev, axis=1, keepdims=True)
    wanted = flag(lev < row_lev) * flag((row_lev < 2.5) | (lev > 2.5)) * flag((lane & (PC - 1)) == q)
    sel = dot(mine, flag(pattern[...] > 0)) * wanted
    spot = (sub * CB + (lane >> 3)).astype(jnp.float32)
    found = listing(sel, ranks(sel), spot, 32)
    number = jnp.minimum(count(sel), CAP_L)
    rows = jnp.where(sub == 0, found, number + 0.0 * spot)
    lists[...] = rows.astype(jnp.int32)
    move = pltpu.make_async_copy(lists, places, sem)
    move.start()
    token[...] = jnp.zeros_like(token)
    move.wait()
    total = places[1, 0]

    def load(t):
        n = places[0, t]
        return pltpu.make_async_copy(blocks.at[n >> 4, n & (CB - 1)], held.at[t], sems_in.at[t])

    def store(t):
        return pltpu.make_async_copy(held.at[t], out.at[t], sems_out.at[t])

    pl.loop(0, total)(lambda t: load(t).start())

    @pl.loop(0, total)
    def _(t):
        load(t).wait()
        store(t).start()

    pl.loop(0, total)(lambda t: store(t).wait())


def first(pattern, levels, blocks):
    return pl.pallas_call(
        first_kernel,
        out_shape=(
            jax.ShapeDtypeStruct((CAP_L, W, W), jnp.float32),
            jax.ShapeDtypeStruct((1, NB), jnp.int32),
        ),
        in_specs=[VMEM, VMEM, HBM],
        out_specs=(HBM, VMEM),
        scratch_shapes=[
            pltpu.VMEM((RB, NB), jnp.int32),
            pltpu.SMEM((RB, NB), jnp.int32),
            pltpu.VMEM((CAP_L, W, W), jnp.float32),
            pltpu.SemaphoreType.DMA,
            pltpu.SemaphoreType.DMA((CAP_L,)),
            pltpu.SemaphoreType.DMA((CAP_L,)),
        ],
        compiler_params=pltpu.CompilerParams(vmem_limit_bytes=ROOM),
        cost_estimate=cost(4),
    )(pattern, levels.reshape(1, NB), blocks)


def pack_kernel(where, cap, with_far, table, blocks, _, *rest):
    rest = list(rest)
    lower = rest.pop(0) if with_far else None
    out, extra, held, sems_in, sems_out = rest[:5]
    count = table[COUNTS, where]
    row = PACK_L + where

    def load(t):
        n = table[row, t]
        return pltpu.make_async_copy(blocks.at[n >> 4, n & (CB - 1)], held.at[t], sems_in.at[t])

    def store(t):
        return pltpu.make_async_copy(held.at[t], out.at[t], sems_out.at[t])

    def load_far(t):
        n = table[LIST_T, t]
        return pltpu.make_async_copy(lower.at[n >> 4, n & (CB - 1)], extra.at[t], rest[5].at[t])

    pl.loop(0, count)(lambda t: load(t).start())
    if with_far:
        pl.loop(0, table[COUNTS, 2])(lambda t: load_far(t).start())
    else:
        extra[...] = jnp.zeros_like(extra)

    @pl.loop(0, count)
    def _(t):
        load(t).wait()
        store(t).start()

    pl.loop(0, count)(lambda t: store(t).wait())
    if with_far:
        pl.loop(0, table[COUNTS, 2])(lambda t: load_far(t).wait())


def pack(where, cap, table, blocks, after, lower=None):
    with_far = lower is not None
    extra = (LIST, W, W) if with_far else (HS, W)
    scratch = [
        pltpu.VMEM((cap, W, W), jnp.float32),
        pltpu.SemaphoreType.DMA((cap,)),
        pltpu.SemaphoreType.DMA((cap,)),
    ]
    if with_far:
        scratch.append(pltpu.SemaphoreType.DMA((LIST,)))
    return pl.pallas_call(
        lambda *refs: pack_kernel(where, cap, with_far, *refs),
        out_shape=(
            jax.ShapeDtypeStruct((cap, W, W), jnp.float32),
            jax.ShapeDtypeStruct(extra, jnp.float32),
        ),
        in_specs=[SMEM, HBM, HBM] + ([HBM] if with_far else []),
        out_specs=(HBM, VMEM),
        scratch_shapes=scratch,
        compiler_params=pltpu.CompilerParams(vmem_limit_bytes=ROOM),
        cost_estimate=cost(4),
    )(table, blocks, after, *([lower] if with_far else []))


def level_kernel(level, copies, kind, turn, both, sliced, group, fetch, table, known, right, inverse, panel, less, *rest):
    rest = list(rest)
    inverse_2 = rest.pop(0) if turn else None
    out = rest.pop(0)
    out_2 = rest.pop(0) if turn else None
    blocks = rest.pop(0) if fetch else panel
    sums = rest.pop(0)
    sems = rest.pop(0) if fetch else None
    p = lax.axis_index("prow")
    row = LIST_U if kind else LIST_L
    e0, e1 = table[STARTS, kind * HALF + level], table[STARTS, kind * HALF + level + 1]
    r0, r1 = table[ROWS, HALF + level], table[ROWS, HALF + level + 1]
    whole = table[STARTS, kind * HALF + LEVELS]

    def copy(t):
        return pltpu.make_async_copy(panel.at[table[row, t] >> 10], blocks.at[t], sems.at[t])

    if fetch:
        pl.loop(e0, e1)(lambda t: copy(t).start())
        pl.loop(0, e0)(lambda t: copy(t).start())
        pl.loop(e1, whole)(lambda t: copy(t).start())

    shift = lax.axis_index("pcol") * HS
    for a in range(RB):
        mine = right[a, pl.ds(shift, HS)] if sliced else right[a]
        if less is not None and not both:
            parts = [less[k, a] for k in range(PC)]
            while len(parts) > 1:
                parts = [x + y for x, y in zip(parts[::2], parts[1::2])]
            mine = mine - parts[0]
        sums[a] = mine
        old = known[p, a] if known is not None else jnp.zeros((HS, W), jnp.float32)
        for r in range(copies):
            if both:
                out[r, 0, a] = less[a]
                out[r, 1, a] = old
            else:
                out[r, a] = old if not turn else jnp.zeros((HS, W), jnp.float32)
        if turn:
            out_2[a] = old

    if panel is not None:
        @pl.loop(0, (e1 - e0 + group - 1) // group)
        def _(g):
            terms = []
            for u in range(group):
                t = e0 + g * group + u
                there = t < e1

                if fetch:
                    @pl.when(there)
                    def _():
                        copy(t).wait()

                t = jnp.minimum(t, e1 - 1)
                node = (table[row, t] >> 3) & (NB - 1)
                x = known[node & (PR - 1), node >> 4] * jnp.where(there, 1.0, 0.0)
                terms.append((table[row, t] & (RB - 1), dot3(x, blocks[t if kind else table[row, t] >> 10])))
            for a, term in terms:
                sums[a] -= term

    lane = iota((HS, W), 1)

    @pl.loop(0, (r1 - r0 + GROUP - 1) >> 2)
    def _(g):
        fresh = []
        for u in range(GROUP):
            r = r0 + g * GROUP + u
            there = r < r1
            a = table[ROWS, jnp.minimum(r, r1 - 1)]

            fresh.append((there, a, jnp.where(lane < table[a, WIDTH], dot3(sums[a], inverse[a]), 0.0)))
        if turn:
            later = [jnp.where(lane < table[a, WIDTH], dot3(x, inverse_2[a]), 0.0) for _, a, x in fresh]
            for there, a, x in fresh:
                out_2[a] = x
            fresh = [(there, a, x) for (there, a, _), x in zip(fresh, later)]
        for there, a, x in fresh:
            @pl.when(there)
            def _():
                for r in range(copies):
                    if both:
                        out[r, 1, a] = x
                    else:
                        out[r, a] = x

    if fetch:
        pl.loop(0, e0)(lambda t: copy(t).wait())
        pl.loop(e1, whole)(lambda t: copy(t).wait())


def level_step(
    level, copies, kind, table, known, right, inverse, panel, *,
    turn=None, both=False, sliced=False, after=None, less=None, group=GROUP, fetch=False,
):
    ins, specs = [table], [SMEM]
    given = ((known, VMEM), (right, VMEM), (inverse, VMEM), (panel, HBM if fetch else VMEM), (less, VMEM))
    for x, spec in given + ((turn, VMEM), (after, HBM)):
        if x is not None:
            ins.append(x)
            specs.append(spec)

    def kernel(*refs):
        refs = list(refs)
        if after is not None:
            refs.pop(len(ins) - 1)
        args = [refs.pop(0)] + [refs.pop(0) if x is not None else None for x, _ in given]
        level_kernel(level, copies, kind, turn is not None, both, sliced, group, fetch, *args, *refs)

    small = (RB, HS, W)
    shapes = [(copies, 2) + small if both else (copies,) + small]
    if turn is not None:
        shapes.append(small)
    if fetch:
        shapes.append((LIST, W, W))
    scratch = []
    if kind == 1 and not both:
        shapes.append(small)
    else:
        scratch.append(pltpu.VMEM(small, jnp.float32))
    if fetch:
        scratch.append(pltpu.SemaphoreType.DMA((LIST,)))
    out = pl.pallas_call(
        kernel,
        out_shape=[jax.ShapeDtypeStruct(x, jnp.float32) for x in shapes],
        in_specs=specs,
        out_specs=[VMEM] * len(shapes),
        scratch_shapes=scratch,
        compiler_params=pltpu.CompilerParams(vmem_limit_bytes=ROOM),
        cost_estimate=cost(8),
    )(*ins)
    return out if len(out) > 1 else out[0]


def across_kernel(table, known, blocks, out):
    count = table[COUNTS, 2]
    out[...] = jnp.zeros_like(out)

    @pl.loop(0, (count + GROUP - 1) >> 2)
    def _(g):
        terms = []
        for u in range(GROUP):
            t = g * GROUP + u
            there = t < count
            t = jnp.minimum(t, count - 1)
            n = table[LIST_T, t]
            c = n & (CB - 1)
            x = known[:, c & 1, c >> 1].reshape(NRHS, W) * jnp.where(there, 1.0, 0.0)
            terms.append((n >> 4, dot3(x, blocks[t]).reshape(PC, HS, W)))
        for a, term in terms:
            out[:, a] += term


def across(table, known, blocks):
    return pl.pallas_call(
        across_kernel,
        out_shape=jax.ShapeDtypeStruct((PC, RB, HS, W), jnp.float32),
        in_specs=[SMEM, VMEM, VMEM],
        out_specs=VMEM,
        compiler_params=pltpu.CompilerParams(vmem_limit_bytes=ROOM),
        cost_estimate=cost(8),
    )(table, known, blocks)


def local(rhs, lower, upper, lower_inverse, upper_inverse, pattern, levels, widths):
    right = rhs.reshape(RB, NRHS, W)
    lower_blocks = lower.reshape(RB, CB, W, W)
    upper_blocks = upper.reshape(RB, CB, W, W)
    lower_inv = lower_inverse.reshape(RB, W, W)
    upper_inv = upper_inverse.reshape(RB, W, W)
    packed_l, token = first(pattern, levels, lower_blocks)
    table = tables(pattern, levels, widths, token)
    swap = lambda x: lax.all_to_all(x, "prow", 0, 0)

    panel_l = lax.all_gather(packed_l, "pcol", tiled=True)
    leaves = level_step(0, PR, 0, table, None, right, lower_inv, None, sliced=True)
    known = swap(leaves)
    packed_u, far_blocks = pack(1, CAP_U, table, upper_blocks, known[0, 0], lower_blocks)
    panel_u = lax.all_gather(packed_u, "pcol", tiled=True)
    for level in (1, 2):
        known = swap(level_step(level, PR, 0, table, known, right, lower_inv, panel_l, sliced=True, group=8))
    split = known.reshape(2, PC, RB, HS, W).transpose(1, 0, 2, 3, 4)
    columns = lax.all_to_all(split, "pcol", 0, 0)
    sums = lax.all_to_all(across(table, columns, far_blocks), "pcol", 0, 0)
    step = lambda level, turn=None: level_step(
        level, PR, 0, table, known, right, lower_inv, panel_l, turn=turn, sliced=True, less=sums
    )
    for level in range(3, LEVELS - 1):
        known = swap(step(level))
    state, forward = step(LEVELS - 1, upper_inv)
    known = swap(state)
    state, held, left = level_step(4, PR, 1, table, known, forward, upper_inv, panel_u, group=8, fetch=True)
    for level in range(3, 0, -1):
        known = swap(state)
        state, left = level_step(level, PR, 1, table, known, left, upper_inv, held, group=16 if level == 3 else 8)
    known = swap(state)
    state = level_step(0, PC, 1, table, known, left, upper_inv, held, both=True, less=forward, group=8)
    full = lax.all_to_all(state, "pcol", 0, 0)
    shape = rhs.shape
    whole = lambda x: x.transpose(1, 0, 2, 3).reshape(shape)
    args = (rhs, lower, upper, lower_inverse, upper_inverse, pattern, levels, widths)
    done = lax.while_loop(
        lambda c: c[2] > 0,
        lambda c: general(*args) + (jnp.int32(0),),
        (whole(full[:, 0]), whole(full[:, 1]), table[COUNTS, 3]),
    )
    return done[0], done[1]


def solution(mesh):
    in_specs = (
        P(None, "prow", None, None),
        P(None, "prow", None, "pcol", None, None),
        P(None, "prow", None, "pcol", None, None),
        P(None, "prow", None, None),
        P(None, "prow", None, None),
        P(),
        P(),
        P(),
    )
    out_specs = (P(None, "prow", None, None), P(None, "prow", None, None))
    return jax.shard_map(local, mesh=mesh, in_specs=in_specs, out_specs=out_specs, check_vma=False)
```
